512 devices in a mesh: owner: 128 (over z, y, core), rep: 4 (over x).
Axes of the slice: x: 4, y: 8, z: 8, core: 2. Of those that a mesh axis runs over, the one named last changes fastest.
Arguments:
- features: bfloat16 [32768, 768], P('owner'), may hold values from -6 to 6
- hidden_weight: bfloat16 [1024, 768], P('owner'), may hold values from -0.21875 to 0.21875
- class_weight: bfloat16 [153, 1024], replicated, may hold values from -210 to 210
- request_ids: int32 [65536, 4], P(('owner', 'rep')), may hold values from 0 to 255
- request_counts: int32 [65536, 2], P(('owner', 'rep')), may hold values from 1 to 2, as said below
- outer_tiles: int32 [1024, 2], P(('owner', 'rep')), may hold values from 0 to 3
- outer_masks: int32 [1024, 2, 128, 128], P(('owner', 'rep')), may hold values 0 or 1
- inner_tiles: int32 [512, 2], P(('owner', 'rep')), may hold values from 0 to 1
- inner_masks: int32 [512, 2, 128, 128], P(('owner', 'rep')), may hold values 0 or 1
- labels: int32 [65536], P(('owner', 'rep')), may hold values from 0 to 152
Outputs:
- hidden_grad: float32 [1024, 768], P('owner')
- class_grad: float32 [153, 1024], replicated
- node_grad: bfloat16 [32768, 1024], P('owner', 'rep')
The draws below stay inside these ranges and needn't reach their ends.
Inputs may be any that keep to these rules, and one draw needn't show every extreme that they name: `request_counts`: column 0 counts live hop-one slots, column 1 live hop-two slots, each of the 2 slots of its part; the rest are padding. Some owners are requested more than others. `outer_tiles`: column block numbers may repeat within a row block; repeated tiles add. `inner_tiles`: column block numbers may repeat within a row block; repeated tiles add.
All inputs are finite; a program needn't handle non-finite values. No bound on the sum of `outer_masks` or of `inner_masks` on one device may be relied on, other than what follows from the above.
Results may differ from the reference program's by a relative error of at most 0.012.
The reference program's roundings to bfloat16 on the way (of `frontier`, `agg_one`, `hidden`, `agg_two`, `logit_grad` and `pre_grad`) count: a program that leaves them out, or rounds other values in their place, can miss the bound.
Values may be sent and summed in bfloat16 or wider, within the bound.
A program may use at most 64 MiB of HBM per device.

```python
import jax
import jax.numpy as jnp
from jax import lax

D = 768
HID = 1024
CLASSES = 153
ROWS = 256
H1 = 256
SEEDS = 128
TILE = 128
K = 2
NODES = 32768
CAP1 = 2
CAP = 4
N_OWNER = 128
N_REP = 4


def draw_class_weight(key, part):
    key = jax.random.fold_in(key, 7)
    normal_key = jax.random.fold_in(key, 0)
    normal_part = jnp.clip(jax.random.normal(normal_key, (CLASSES, HID), jnp.float32), -5.0, 5.0)
    return normal_part.astype(jnp.bfloat16)


def draw_request_counts(key, part):
    key = jax.random.fold_in(key, 3)
    subkeys = jax.random.split(key, 5)
    senders = N_OWNER * N_REP
    owner_heat = jax.random.randint(subkeys[0], (1, N_OWNER), 1, 5)
    hot_peer = jax.random.randint(subkeys[1], (), 0, N_OWNER)
    peer_index = jnp.arange(N_OWNER)[None, :]
    owner_heat = jnp.where(peer_index == hot_peer, 4, owner_heat)
    first_part = jax.random.randint(subkeys[2], (senders, N_OWNER), 0, CAP1)
    second_part = jax.random.randint(subkeys[3], (senders, N_OWNER), 0, CAP1)
    busy_sender = jax.random.randint(subkeys[4], (), 0, senders)
    filled = (jnp.arange(senders)[:, None] == busy_sender) & (peer_index == hot_peer)
    first_part = jnp.where(filled, CAP1, jnp.minimum(CAP1, 1 + first_part * owner_heat // 4))
    second_part = jnp.where(filled, CAP1, jnp.minimum(CAP1, 1 + second_part * owner_heat // 4))
    return jnp.stack([first_part, second_part], axis=-1).reshape(senders * N_OWNER, 2).astype(jnp.int32)


def draw_labels(key, part):
    key = jax.random.fold_in(key, 11)
    subkeys = jax.random.split(key, 3)
    senders = N_OWNER * N_REP
    home_class = jax.random.randint(subkeys[0], (senders, 1), 0, CLASSES)
    spread_class = jax.random.randint(subkeys[1], (senders, SEEDS), 0, CLASSES)
    coin = jax.random.randint(subkeys[2], (senders, SEEDS), 0, 2)
    chosen = jnp.where(coin == 0, home_class, spread_class)
    return chosen.reshape(senders * SEEDS).astype(jnp.int32)


def touch_ends(entries, stream_key, least, largest):
    place = [jax.random.randint(jax.random.fold_in(stream_key, axis), (), 0, length) for axis, length in enumerate(entries.shape)]
    widest = entries.shape.index(max(entries.shape))
    next_to = place[:widest] + [(place[widest] + 1) % entries.shape[widest]] + place[widest + 1:]
    return entries.at[tuple(place)].set(least).at[tuple(next_to)].set(largest)


def block_levels(own_key, extent, pieces, smallest, largest):
    factor_of = 1.0
    for dim, shards_of in pieces:
        steps = jax.random.uniform(jax.random.fold_in(jax.random.fold_in(own_key, 6), dim), (shards_of,), jnp.float32, smallest / len(pieces), largest / len(pieces))
        factor_of = factor_of * jnp.repeat(jnp.exp(steps), extent[dim] // shards_of).reshape((-1,) + (1,) * (len(extent) - 1 - dim))
    return factor_of


def bell_draw(key, extent, scale, reach, cuts=(), kind=jnp.bfloat16):
    drawn = jax.random.normal(key, extent, jnp.float32) * scale
    if len(cuts) > 0:
        drawn = block_levels(key, extent, cuts, -0.22, 0.18) * drawn
    return jnp.clip(drawn, min=-reach, max=reach).astype(kind)


def setup_inputs(seed: int = 0) -> dict:
    key_list = jax.random.split(jax.random.key(seed), 11)
    return {
        "features": bell_draw(key_list[0], (NODES, D), 1.0, 6.0, ((0, 128),)),
        "hidden_weight": bell_draw(key_list[1], (HID, D), D ** -0.5, 0.21875, ((0, 128),)),
        "class_weight": draw_class_weight(jax.random.fold_in(key_list[10], 71), 0),
        "request_ids": touch_ends(jax.random.randint(key_list[3], (N_OWNER * N_REP * N_OWNER, CAP), 0, ROWS), jax.random.fold_in(key_list[3], 1), 0, ROWS - 1).astype(jnp.int32),
        "request_counts": draw_request_counts(jax.random.fold_in(key_list[10], 71), 0),
        "outer_tiles": touch_ends(jax.random.randint(key_list[5], (N_OWNER * N_REP * (H1 // TILE), K), 0, 2 * H1 // TILE), jax.random.fold_in(key_list[5], 1), 0, (2 * H1 // TILE) - 1).astype(jnp.int32),
        "outer_masks": touch_ends((jax.random.randint(key_list[6], (N_OWNER * N_REP * (H1 // TILE), K, TILE, TILE), 0, 8) < 1).astype(jnp.int32), jax.random.fold_in(key_list[6], 1), 0, 1),
        "inner_tiles": touch_ends(jax.random.randint(key_list[7], (N_OWNER * N_REP * (SEEDS // TILE), K), 0, H1 // TILE), jax.random.fold_in(key_list[7], 1), 0, (H1 // TILE) - 1).astype(jnp.int32),
        "inner_masks": touch_ends((jax.random.randint(key_list[8], (N_OWNER * N_REP * (SEEDS // TILE), K, TILE, TILE), 0, 16) < 1).astype(jnp.int32), jax.random.fold_in(key_list[8], 1), 0, 1),
        "labels": draw_labels(jax.random.fold_in(key_list[10], 71), 0),
    }


def tile_product(tile_weights, tile_cols, row_blocks):
    picked = row_blocks[tile_cols]
    return jnp.einsum("bkij,bkjw->biw", tile_weights, picked, precision=lax.Precision.HIGHEST)


def slot_validity(counts_part, slot_count):
    half_slots = slot_count // 2
    position = jnp.arange(slot_count, dtype=jnp.int32)[None, :]
    first_ok = position < counts_part[:, 0:1]
    second_ok = (position - half_slots) < counts_part[:, 1:2]
    return jnp.where(position < half_slots, first_ok, second_ok).astype(jnp.float32)


def reference(features, hidden_weight, class_weight, request_ids, request_counts, outer_tiles, outer_masks, inner_tiles, inner_masks, labels):
    senders = N_OWNER * N_REP
    half_slots = H1 // N_OWNER
    slot_count = 2 * half_slots
    table = features.reshape(N_OWNER, ROWS, D)
    owner_index = jnp.arange(N_OWNER, dtype=jnp.int32)

    def one_device(carry, inputs):
        hidden_acc, class_acc, node_acc = carry
        wanted, counts_part, outer_cols, outer_bits, inner_cols, inner_bits, seed_labels = inputs
        fetched = table[owner_index[:, None], wanted]
        validity = slot_validity(counts_part, slot_count)
        frontier = fetched.reshape(2 * H1, D).astype(jnp.float32)
        own_rows = fetched[:, :half_slots].reshape(H1, D).astype(jnp.float32)
        valid_blocks = validity.reshape(2 * H1 // TILE, TILE)
        outer_weights = outer_bits.astype(jnp.float32) * valid_blocks[outer_cols][:, :, None, :]
        outer_degree = jnp.sum(outer_weights, axis=(1, 3)).reshape(H1, 1)
        gathered = tile_product(outer_weights, outer_cols, frontier.reshape(2 * H1 // TILE, TILE, D)).reshape(H1, D)
        agg_one = ((own_rows + gathered) / (1.0 + outer_degree)).astype(jnp.bfloat16)
        pre_act = jnp.dot(agg_one, hidden_weight.T, preferred_element_type=jnp.float32)
        hidden = jnp.maximum(pre_act, 0.0).astype(jnp.bfloat16)
        hop_valid = validity[:, :half_slots].reshape(H1 // TILE, TILE)
        inner_weights = inner_bits.astype(jnp.float32) * hop_valid[inner_cols][:, :, None, :]
        inner_degree = jnp.maximum(jnp.sum(inner_weights, axis=(1, 3)).reshape(SEEDS, 1), 1.0)
        summed = tile_product(inner_weights, inner_cols, hidden.astype(jnp.float32).reshape(H1 // TILE, TILE, HID))
        agg_two = (summed.reshape(SEEDS, HID) / inner_degree).astype(jnp.bfloat16)
        logits = jnp.dot(agg_two, class_weight.T, preferred_element_type=jnp.float32)
        shifted = logits - jnp.max(logits, axis=1, keepdims=True)
        exponent = jnp.exp(shifted)
        softmax_out = exponent / jnp.sum(exponent, axis=1, keepdims=True)
        one_hot = (seed_labels[:, None] == jnp.arange(CLASSES, dtype=jnp.int32)[None, :]).astype(jnp.float32)
        logit_grad = ((softmax_out - one_hot) / SEEDS).astype(jnp.bfloat16)
        class_term = jnp.dot(logit_grad.T, agg_two, preferred_element_type=jnp.float32)
        agg_grad = jnp.dot(logit_grad, class_weight, preferred_element_type=jnp.float32) / inner_degree
        spread = jnp.einsum("bkij,biw->bkjw", inner_weights, agg_grad.reshape(SEEDS // TILE, TILE, HID), precision=lax.Precision.HIGHEST)
        hidden_diff = jnp.zeros((H1 // TILE, TILE, HID), jnp.float32).at[inner_cols].add(spread).reshape(H1, HID)
        pre_grad = jnp.where(pre_act > 0.0, hidden_diff, 0.0).astype(jnp.bfloat16)
        hidden_term = jnp.dot(pre_grad.T, agg_one, preferred_element_type=jnp.float32)
        targets = (owner_index[:, None] * ROWS + wanted[:, :half_slots]).reshape(-1)
        node_acc = node_acc.at[targets].add(hidden_diff)
        return (hidden_acc + hidden_term, class_acc + class_term, node_acc), None

    stacked = (
        request_ids.reshape(senders, N_OWNER, slot_count),
        request_counts.reshape(senders, N_OWNER, 2),
        outer_tiles.reshape(senders, H1 // TILE, K),
        outer_masks.reshape(senders, H1 // TILE, K, TILE, TILE),
        inner_tiles.reshape(senders, SEEDS // TILE, K),
        inner_masks.reshape(senders, SEEDS // TILE, K, TILE, TILE),
        labels.reshape(senders, SEEDS),
    )
    start_carry = (
        jnp.zeros((HID, D), jnp.float32),
        jnp.zeros((CLASSES, HID), jnp.float32),
        jnp.zeros((NODES, HID), jnp.float32),
    )
    final_carry, unused = lax.scan(one_device, start_carry, stacked)
    hidden_grad, class_grad, node_total = final_carry
    return (hidden_grad, class_grad, node_total.astype(jnp.bfloat16))
```

```python
import functools

import jax
import jax.numpy as jnp
from jax import lax
from jax.experimental import pallas as pl
from jax.experimental.pallas import tpu as pltpu
from jax.sharding import PartitionSpec as P

MESH = pl.DeviceIdType.MESH
F32 = jnp.float32
BF16 = jnp.bfloat16

GRIDS = {(128, 4): (8, 8, 2, 4), (16, 2): (2, 4, 2, 2)}


def iota(shape, dim):
    return lax.broadcasted_iota(jnp.int32, shape, dim)


def quo(a, n):
    return lax.shift_right_logical(a, jnp.full_like(a, n.bit_length() - 1))


def rem(a, n):
    return lax.bitwise_and(a, jnp.full_like(a, n - 1))


def flag(cond, dtype=BF16):
    return jnp.where(cond, 1.0, 0.0).astype(F32).astype(dtype)


def dot(a, b, ca=1, cb=0):
    return lax.dot_general(a, b, (((ca,), (cb,)), ((), ())), preferred_element_type=F32)


def regroup(outer, middle, inner, transpose=False):
    n = outer * middle * inner
    o, i = iota((n, n), 0), iota((n, n), 1)
    if transpose:
        o, i = i, o
    m, rest = quo(o, outer * inner), rem(o, outer * inner)
    a, b = quo(rest, inner), rem(rest, inner)
    return flag(i == a * (middle * inner) + m * inner + b)


def kernel(
    dims,
    feat_hbm, weight_ref, cls_ref, ids_ref, counts_ref, otile_ref, omask_hbm, itile_ref, imask_hbm, labels_ref,
    hidden_out, class_out, node_out,
    feat, omask, imask,
    i1s, i1r, i2s, i2r,
    ws, wr, w_all,
    fa1s, fa1r, fa2s, fa2r, fb1s, fb1r, fb2s, fb2r,
    agg, pre,
    na1s, na1r, na2s, na2r, nb1s, nb1r, nb2s, nb2r, xs, xr,
    gmine, gs0, gr0, gs1, gr1, gs2, gr2, gs3, gr3, gs4, gr4,
    cmine, cs0, cr0, cs1, cr1, cs2, cr2, cs3, cr3, cfin, ca4, ca5, ca6,
    local_sem,
    i1_ss, i1_rs, i2_ss, i2_rs,
    w1_ss, w1_rs, w2_ss, w2_rs, w3_ss, w3_rs, w4_ss, w4_rs,
    fa1_ss, fa1_rs, fa2_ss, fa2_rs, fb1_ss, fb1_rs, fb2_ss, fb2_rs,
    na1_ss, na1_rs, na2_ss, na2_rs, nb1_ss, nb1_rs, nb2_ss, nb2_rs, x_ss, x_rs,
    g0_ss, g0_rs, g1_ss, g1_rs, g2_ss, g2_rs, g3_ss, g3_rs, g4_ss, g4_rs,
    c0_ss, c0_rs, c1_ss, c1_rs, c2_ss, c2_rs, c3_ss, c3_rs, c4_ss, c4_rs, c5_ss, c5_rs, c6_ss, c6_rs,
):
    Z, Y, C, X, cap, tile, rows, classes = dims
    Q = Y * C
    NO = Z * Q
    half = cap // 2
    hop, front = NO * half, NO * cap
    D, HID = agg.shape[1], pre.shape[1]
    DH, HH = D // 2, HID // 2
    YL = Y // X
    nb, cb, cw = cs2.shape
    CP = nb * cb
    seeds = labels_ref.shape[1]
    row_blocks, col_blocks, K = hop // tile, front // tile, otile_ref.shape[1]
    LW = i2s.shape[2]
    S8 = 8

    me_o = lax.axis_index("owner")
    x = lax.axis_index("rep")
    z = me_o // Q
    q = me_o % Q
    y = q // C
    c = q % C
    sib = C - 1 - c

    def copy(src, dst, ss, rs, zz, qq, xx):
        return pltpu.make_async_remote_copy(
            src_ref=src, dst_ref=dst, send_sem=ss, recv_sem=rs,
            device_id=(zz * Q + qq, xx), device_id_type=MESH,
        )

    def each(n, body):
        def step(i, carry):
            body(i)
            return carry
        lax.fori_loop(1, n, step, 0)

    class Exchange:
        def __init__(self, n, me, at, src, dst, ss, rs):
            self.n, self.me, self.at, self.src, self.dst, self.ss, self.rs = n, me, at, src, dst, ss, rs

        def out(self, d):
            to = (self.me + d) % self.n
            return copy(self.src(to), self.dst(self.me), self.ss.at[d], self.rs.at[self.me], *self.at(to))

        def inn(self, d):
            frm = (self.me + d) % self.n
            return copy(self.src(frm), self.dst(frm), self.ss.at[d], self.rs.at[frm], *self.at(frm))

        def start(self):
            each(self.n, lambda d: self.out(d).start())

        def recv(self):
            each(self.n, lambda d: self.inn(d).wait_recv())

        def sent(self):
            each(self.n, lambda d: self.out(d).wait_send())

    def along_z(src, dst, ss, rs):
        return Exchange(Z, z, lambda t: (t, q, x), src, dst, ss, rs)

    def along_q(src, dst, ss, rs):
        return Exchange(Q, q, lambda t: (z, t, x), src, dst, ss, rs)

    def along_y(src, dst, ss, rs):
        return Exchange(Y, y, lambda t: (z, t * C + c, x), src, dst, ss, rs)

    def along_x(src, dst, ss, rs):
        return Exchange(X, x, lambda t: (z, q, t), src, dst, ss, rs)

    def to_sibling(src, dst, ss, rs):
        return copy(src, dst, ss, rs, z, y * C + sib, x)

    loads = [
        pltpu.make_async_copy(feat_hbm, feat, local_sem.at[0]),
        pltpu.make_async_copy(omask_hbm, omask, local_sem.at[1]),
        pltpu.make_async_copy(imask_hbm, imask, local_sem.at[2]),
    ]
    for load in loads:
        load.start()

    barrier = pltpu.get_barrier_semaphore()

    def greet(zz, qq, xx):
        pl.semaphore_signal(barrier, inc=1, device_id=(zz * Q + qq, xx), device_id_type=MESH)

    each(Z, lambda d: greet((z + d) % Z, q, x))
    each(Q, lambda d: greet(z, (q + d) % Q, x))
    for core in range(C):
        each(X, lambda d: greet(z, y * C + core, (x + d) % X))

    i1s[...] = jnp.zeros_like(i1s)
    i1s[0:cap, :] = ids_ref[...].astype(F32)
    w32 = weight_ref[...].astype(F32)
    ws[...] = jnp.concatenate([w32[:, :DH], w32[:, DH:]], axis=0).astype(BF16)

    pl.semaphore_wait(barrier, (Z - 1) + (Q - 1) + C * (X - 1))

    ex_i1 = along_z(lambda t: i1s, lambda f: i1r.at[f], i1_ss, i1_rs)
    ex_i1.start()
    i1r[z] = i1s[...]

    w_core = y % C

    def w1_copy(t):
        return copy(ws, wr.at[c], w1_ss.at[t], w1_rs.at[c], z, t * C + w_core, x)

    def w1_each(act):
        def step(t, carry):
            @pl.when((y // C == x) & jnp.logical_not((t == y) & (w_core == c)))
            def _():
                act(t)
            return carry
        lax.fori_loop(0, Y, step, 0)

    w1_each(lambda t: w1_copy(t).start())
    y_mine = x * C + c

    ex_i1.recv()
    marks = flag(iota((Q, NO), 1) == z * Q + iota((Q, NO), 0))
    asked = i1r[...].reshape(Z * S8, NO).astype(BF16)
    if LW > Z * S8:
        asked = jnp.concatenate([asked] * (LW // (Z * S8)), axis=0)
    for_q = dot(marks, asked, 1, 1)
    for k in range(Q):
        i2s[k] = jnp.broadcast_to(for_q[k:k + 1, :], (8, LW))
    ex_i2 = along_q(lambda t: i2s.at[t], lambda f: i2r.at[f], i2_ss, i2_rs)
    ex_i2.start()
    i2r[q] = i2s[q]

    for c0 in range(C):
        own = (y == y_mine) & (c == c0)

        @pl.when(own)
        def _():
            wr[c0] = ws[...]

        @pl.when(jnp.logical_not(own))
        def _():
            copy(ws, wr.at[c0], w1_ss.at[0], w1_rs.at[c0], z, y_mine * C + c0, x).wait_recv()
    for hcol in range(2):
        cols = slice(hcol * DH, (hcol + 1) * DH)
        w_all[z, x, c, :, cols] = jnp.concatenate(
            [wr[c0, hcol * 8:(hcol + 1) * 8, :].astype(F32) for c0 in range(C)], axis=0
        ).astype(BF16)
    ex_w2 = along_z(lambda t: w_all.at[z, x, c], lambda f: w_all.at[f, x, c], w2_ss, w2_rs)
    ex_w2.start()

    for load in loads[:1]:
        load.wait()
    lane_q = iota((front, Q * 8), 1)

    ex_i2.recv()
    wanted = i2r[...].reshape(Q * 8, LW).astype(BF16)

    def picked(col_of, q_of):
        spread = dot(flag(iota((front, LW), 1) == col_of), wanted, 1, 1)
        ids = jnp.sum(jnp.where(lane_q == q_of * 8, spread, 0.0), axis=1, keepdims=True)
        return flag(ids == iota((front, rows), 1).astype(F32))

    r = iota((front, 1), 0)
    pick_a = picked(quo(r, cap * Q) * S8 + quo(rem(r, cap * Q), Q), rem(r, Q))
    fa1s[...] = dot(pick_a, feat[:, :DH]).astype(BF16).reshape(fa1s.shape)
    ex_fa1 = along_z(lambda t: fa1s.at[t], lambda f: fa1r.at[f], fa1_ss, fa1_rs)
    ex_fa1.start()
    fa1r[z] = fa1s[z]
    pick_b = picked(rem(r, Z) * S8 + quo(rem(r, cap * Z), Z), quo(r, cap * Z))
    fb1s[...] = dot(pick_b, feat[:, DH:]).astype(BF16).reshape(fb1s.shape)
    ex_fb1 = along_q(lambda t: fb1s.at[t], lambda f: fb1r.at[f], fb1_ss, fb1_rs)
    ex_fb1.start()
    fb1r[q] = fb1s[q]

    ex_w2.recv()
    ex_w3 = along_x(lambda t: w_all.at[:, x, c], lambda f: w_all.at[:, f, c], w3_ss, w3_rs)
    ex_w3.start()

    for load in loads[1:]:
        load.wait()
    counts = counts_ref[...].astype(F32)
    counts8 = jnp.concatenate([counts, jnp.zeros((6, NO), F32)], axis=0).astype(BF16)

    def validity(slots):
        n = NO * slots
        at = iota((NO, n), 1)
        per = dot(counts8, flag(iota((NO, n), 0) == quo(at, slots)))
        j = rem(iota((1, n), 1), slots).astype(F32)
        first = flag(j < per[0:1, :], F32)
        second = flag(j - half < per[1:2, :], F32)
        return jnp.where(j < half, first, second)

    valid = validity(cap)
    outer_rows = []
    for b in range(row_blocks):
        blocks = []
        for cbk in range(col_blocks):
            m = jnp.zeros((tile, tile), jnp.int32)
            for k in range(K):
                m = m + omask[b, k] * (otile_ref[b, k] == cbk).astype(jnp.int32)
            blocks.append(m.astype(F32) * valid[:, cbk * tile:(cbk + 1) * tile])
        outer_rows.append(jnp.concatenate(blocks, axis=1))
    outer = jnp.concatenate(outer_rows, axis=0)
    outer_scale = 1.0 + jnp.sum(outer, axis=1, keepdims=True)
    oi, oc = iota((hop, front), 0), iota((hop, front), 1)
    self_col = quo(oi, half) * cap + rem(oi, half)
    outer_self = (outer + flag(oc == self_col, F32)).astype(BF16)
    outer_a = dot(outer_self, regroup(Z, Q, cap, transpose=True)).astype(BF16)

    hop_valid = validity(half)
    blocks = []
    for cbk in range(row_blocks):
        m = jnp.zeros((tile, tile), jnp.int32)
        for k in range(K):
            m = m + imask[0, k] * (itile_ref[0, k] == cbk).astype(jnp.int32)
        blocks.append(m.astype(F32) * hop_valid[:, cbk * tile:(cbk + 1) * tile])
    inner32 = jnp.concatenate(blocks, axis=1)
    inner_degree = jnp.maximum(jnp.sum(inner32, axis=1, keepdims=True), 1.0)
    inner = inner32.astype(BF16)

    label_row = labels_ref[...]
    label_col = jnp.sum(
        jnp.where(iota((seeds, seeds), 0) == iota((seeds, seeds), 1), label_row, 0), axis=1, keepdims=True
    )
    one_hot = flag(label_col == iota((seeds, classes), 1), F32)

    ex_fa1.recv()
    move_a = regroup(Z * cap, Q, 1)
    fa2s[...] = dot(move_a, fa1r[...].reshape(front, DH)).astype(BF16).reshape(fa2s.shape)
    ex_fa2 = along_q(lambda t: fa2s.at[t], lambda f: fa2r.at[f], fa2_ss, fa2_rs)
    ex_fa2.start()
    fa2r[q] = fa2s[q]
    ex_fb1.recv()
    move_b = regroup(Q * cap, Z, 1)
    fb2s[...] = dot(move_b, fb1r[...].reshape(front, DH)).astype(BF16).reshape(fb2s.shape)
    ex_fb2 = along_z(lambda t: fb2s.at[t], lambda f: fb2r.at[f], fb2_ss, fb2_rs)
    ex_fb2.start()
    fb2r[z] = fb2s[z]

    ex_w3.recv()
    w4 = to_sibling(w_all.at[:, :, c], w_all.at[:, :, c], w4_ss, w4_rs)
    w4_in = to_sibling(w_all.at[:, :, sib], w_all.at[:, :, sib], w4_ss, w4_rs)
    w4.start()

    ex_fa2.recv()
    agg[:, :DH] = (dot(outer_a, fa2r[...].reshape(front, DH)) / outer_scale).astype(BF16)
    ex_fb2.recv()
    agg[:, DH:] = (dot(outer_self, fb2r[...].reshape(front, DH)) / outer_scale).astype(BF16)

    w4_in.wait_recv()
    pre[...] = dot(agg[...], w_all[...].reshape(HID, D), 1, 1)
    hidden = jnp.maximum(pre[...], 0.0).astype(BF16)
    agg_two = (dot(inner, hidden) / inner_degree).astype(BF16)
    logits = dot(agg_two, cls_ref[...], 1, 1)
    exponent = jnp.exp(logits - jnp.max(logits, axis=1, keepdims=True))
    softmax = exponent / jnp.sum(exponent, axis=1, keepdims=True)
    logit_grad = ((softmax - one_hot) / seeds).astype(BF16)
    agg_grad = dot(logit_grad, cls_ref[...]) / inner_degree
    high = agg_grad.astype(BF16)
    low = (agg_grad - high.astype(F32)).astype(BF16)
    hidden_diff = dot(inner, high, 0, 0) + dot(inner, low, 0, 0)

    diff16 = hidden_diff.astype(BF16)
    na1s[...] = diff16[:, :HH].reshape(na1s.shape)
    ex_na1 = along_z(lambda t: na1s.at[t], lambda f: na1r.at[f], na1_ss, na1_rs)
    ex_na1.start()
    na1r[z] = na1s[z]
    swap_a = regroup(Z, Q, half)
    nb1s[...] = dot(swap_a, diff16[:, HH:]).astype(BF16).reshape(nb1s.shape)
    ex_nb1 = along_q(lambda t: nb1s.at[t], lambda f: nb1r.at[f], nb1_ss, nb1_rs)
    ex_nb1.start()
    nb1r[q] = nb1s[q]

    pre_grad = jnp.where(pre[...] > 0.0, hidden_diff, 0.0).astype(BF16)
    theirs = pl.ds(pl.multiple_of(sib * DH, DH), DH)
    ours = pl.ds(pl.multiple_of(c * DH, DH), DH)
    gs0[...] = dot(pre_grad, agg[:, theirs], 0, 0).astype(BF16).reshape(gs0.shape)
    g0 = to_sibling(gs0, gr0, g0_ss, g0_rs)
    g0.start()
    gmine[...] = dot(pre_grad, agg[:, ours], 0, 0).reshape(gmine.shape)

    widen = flag(iota((classes, CP), 0) == iota((classes, CP), 1))
    class_rows = dot(dot(logit_grad, widen).astype(BF16), agg_two, 0, 0)
    left, right = class_rows[:, :HH], class_rows[:, HH:]
    cs0[...] = jnp.where(c == 0, right, left).astype(BF16)
    cmine[...] = jnp.where(c == 0, left, right)
    c0 = to_sibling(cs0, cr0, c0_ss, c0_rs)
    c0.start()

    g0.wait_recv()
    gmine[...] = gmine[...] + gr0[...].astype(F32)
    gs1[...] = gmine[...].astype(BF16)
    ex_g1 = along_x(lambda t: gs1.at[:, t], lambda f: gr1.at[f], g1_ss, g1_rs)
    ex_g1.start()
    gr1[x] = gs1[:, x]

    c0.wait_recv()
    cmine[...] = cmine[...] + cr0[...].astype(F32)
    for t in range(X):
        cs1[t] = cmine[:, t * cw:(t + 1) * cw].astype(BF16)
    ex_c1 = along_x(lambda t: cs1.at[t], lambda f: cr1.at[f], c1_ss, c1_rs)
    ex_c1.start()
    cr1[x] = cs1[x]

    ex_na1.recv()
    na2s[...] = dot(swap_a, na1r[...].reshape(hop, HH)).astype(BF16).reshape(na2s.shape)
    ex_na2 = along_q(lambda t: na2s.at[t], lambda f: na2r.at[f], na2_ss, na2_rs)
    ex_na2.start()
    na2r[q] = na2s[q]
    ex_nb1.recv()
    swap_b = regroup(Q, Z, half)
    nb2s[...] = dot(swap_b, nb1r[...].reshape(hop, HH)).astype(BF16).reshape(nb2s.shape)
    ex_nb2 = along_z(lambda t: nb2s.at[t], lambda f: nb2r.at[f], nb2_ss, nb2_rs)
    ex_nb2.start()
    nb2r[z] = nb2s[z]

    def total(ref, n):
        acc = ref[0].astype(F32)
        for k in range(1, n):
            acc = acc + ref[k].astype(F32)
        return acc

    ex_g1.recv()
    gs2[...] = total(gr1, X).astype(BF16)
    ex_g2 = along_z(lambda t: gs2.at[t], lambda f: gr2.at[f], g2_ss, g2_rs)
    ex_g2.start()
    gr2[z] = gs2[z]

    ex_c1.recv()
    cs2[...] = total(cr1, X).astype(BF16).reshape(cs2.shape)

    def c2_copy(to, frm):
        return copy(cs2.at[to], cr2.at[frm], c2_ss.at[to], c2_rs.at[frm], to, q, x)

    def to_blocks(act):
        def step(t, carry):
            @pl.when(t != z)
            def _():
                act(t)
            return carry
        lax.fori_loop(0, nb, step, 0)

    to_blocks(lambda t: c2_copy(t, z).start())
    summing = z < nb

    ex_c2_in = Exchange(Z, z, lambda t: (t, q, x), lambda t: cs2.at[0], lambda f: cr2.at[f], c2_ss, c2_rs)
    ex_c3 = along_y(lambda t: cs3, lambda f: cr3.at[f], c3_ss, c3_rs)

    @pl.when(summing)
    def _():
        cr2[z] = cs2[z]
        ex_c2_in.recv()
        cs3[...] = total(cr2, Z).astype(BF16)
        ex_c3.start()
        cr3[y] = cs3[...]

    ex_g2.recv()
    gs3[...] = total(gr2, Z).astype(BF16).reshape(gs3.shape)

    def g3_copy(yl, to, frm):
        return copy(gs3.at[yl], gr3.at[frm], g3_ss.at[yl], g3_rs.at[frm], z, to * C + c, x)

    for yl in range(YL):
        @pl.when(x * YL + yl != y)
        def _():
            g3_copy(yl, x * YL + yl, y).start()
    owning = y // YL == x
    ex_g3_in = Exchange(Y, y, lambda t: (z, t * C + c, x), lambda t: gs3.at[0], lambda f: gr3.at[f], g4_ss, g3_rs)

    def scatter(j_of, z_of, q_of, arrived):
        spread = dot(wanted, flag(iota((LW, hop), 0) == z_of * S8 + j_of))
        ids = jnp.sum(jnp.where(iota((Q * 8, hop), 0) == q_of * 8, spread, 0.0), axis=0, keepdims=True)
        return dot(flag(iota((rows, hop), 0).astype(F32) == ids), arrived)

    s = iota((1, hop), 1)
    ex_na2.recv()
    node_a = scatter(rem(s, half), rem(quo(s, half), Z), quo(s, half * Z), na2r[...].reshape(hop, HH)).astype(BF16)
    xw = HID // X
    for t in range(X // 2):
        xs[t] = node_a[:, t * xw:(t + 1) * xw]
    ex_nb2.recv()
    node_b = scatter(rem(s, half), quo(s, half * Q), rem(quo(s, half), Q), nb2r[...].reshape(hop, HH)).astype(BF16)
    for t in range(X // 2):
        xs[X // 2 + t] = node_b[:, t * xw:(t + 1) * xw]
    ex_x = along_x(lambda t: xs.at[t], lambda f: xr.at[f], x_ss, x_rs)
    ex_x.start()
    xr[x] = xs[x]

    def g4_copy(xx, cc):
        return copy(gs4.at[cc], gr4.at[c], g4_ss.at[xx * C + cc], g4_rs.at[c], z, y * C + cc, xx)

    def g4_each(act):
        for xx in range(X):
            for cc in range(C):
                @pl.when(owning & jnp.logical_not((x == xx) & (c == cc)))
                def _():
                    act(xx, cc)

    @pl.when(owning)
    def _():
        gr3[y] = gs3[y % YL]
        ex_g3_in.recv()
        gs4[...] = total(gr3, Y).reshape(gs4.shape)
        gr4[c] = gs4[c]

    g4_each(lambda xx, cc: g4_copy(xx, cc).start())

    ca4_copy = lambda to, frm: copy(cfin, ca4.at[frm], c4_ss.at[to], c4_rs.at[frm], to, q, x)

    @pl.when(summing)
    def _():
        ex_c3.recv()
        cfin[...] = total(cr3, Y).astype(BF16)
        each(Z, lambda d: ca4_copy((z + d) % Z, z).start())
        ca4[z] = cfin[...]

    to_blocks(lambda t: ca4_copy(t, t).wait_recv())
    ex_c5 = along_x(lambda t: ca4, lambda f: ca5.at[f], c5_ss, c5_rs)
    ex_c5.start()
    ca5[x] = ca4[...]
    ex_c5.recv()
    c6 = to_sibling(ca5, ca6, c6_ss, c6_rs)
    c6.start()

    for cc in range(C):
        @pl.when(jnp.logical_not(owning & (c == cc)))
        def _():
            copy(gs4.at[0], gr4.at[cc], g4_ss.at[0], g4_rs.at[cc], z, y * C + cc, y // YL).wait_recv()
        hidden_out[:, cc * DH:(cc + 1) * DH] = gr4[cc]

    ex_x.recv()
    node_out[...] = total(xr, X).astype(BF16)

    c6.wait_recv()
    mine5, theirs6 = ca5[...], ca6[...]
    for t in range(X):
        m, o = mine5[t].reshape(CP, cw), theirs6[t].reshape(CP, cw)
        for cc in range(C):
            class_out[:, cc * HH + t * cw:cc * HH + (t + 1) * cw] = jnp.where(c == cc, m, o)

    for ex in (ex_i1, ex_i2, ex_w2, ex_w3, ex_fa1, ex_fb1, ex_fa2, ex_fb2, ex_na1, ex_nb1, ex_na2, ex_nb2,
               ex_g1, ex_g2, ex_c1, ex_c5, ex_x):
        ex.sent()
    w1_each(lambda t: w1_copy(t).wait_send())
    for one in (w4, g0, c0, c6):
        one.wait_send()
    to_blocks(lambda t: c2_copy(t, z).wait_send())

    @pl.when(summing)
    def _():
        ex_c3.sent()
        each(Z, lambda d: ca4_copy((z + d) % Z, z).wait_send())

    for yl in range(YL):
        @pl.when(x * YL + yl != y)
        def _():
            g3_copy(yl, x * YL + yl, y).wait_send()
    g4_each(lambda xx, cc: g4_copy(xx, cc).wait_send())


def on_device(
    grid, features, hidden_weight, class_weight, request_ids, request_counts,
    outer_tiles, outer_masks, inner_tiles, inner_masks, labels,
):
    Z, Y, C, X = grid
    Q = Y * C
    NO = Z * Q
    cap = request_ids.shape[1]
    half = cap // 2
    rows, D = features.shape
    classes, HID = class_weight.shape
    tile = outer_masks.shape[2]
    hop = NO * half
    DH, HH, YL = D // 2, HID // 2, Y // X
    cb = 32 if classes > 32 else 8
    nb = -(-classes // cb)
    CP, cw = nb * cb, HID // (C * X)
    LW = max(Z * 8, 128)
    dims = (Z, Y, C, X, cap, tile, rows, classes)
    vm, dma = pltpu.VMEM, pltpu.SemaphoreType.DMA
    scratch = [
        vm(features.shape, BF16), vm(outer_masks.shape, jnp.int32), vm(inner_masks.shape, jnp.int32),
        vm((8, NO), F32), vm((Z, 8, NO), F32), vm((Q, 8, LW), F32), vm((Q, 8, LW), F32),
        vm((16, DH), BF16), vm((C, 16, DH), BF16), vm((Z, X, C, 16, D), BF16),
        vm((Z, cap * Q, DH), BF16), vm((Z, cap * Q, DH), BF16), vm((Q, cap * Z, DH), BF16), vm((Q, cap * Z, DH), BF16),
        vm((Q, cap * Z, DH), BF16), vm((Q, cap * Z, DH), BF16), vm((Z, cap * Q, DH), BF16), vm((Z, cap * Q, DH), BF16),
        vm((hop, D), BF16), vm((hop, HID), F32),
        vm((Z, Q * half, HH), BF16), vm((Z, Q * half, HH), BF16), vm((Q, Z * half, HH), BF16), vm((Q, Z * half, HH), BF16),
        vm((Q, Z * half, HH), BF16), vm((Q, Z * half, HH), BF16), vm((Z, Q * half, HH), BF16), vm((Z, Q * half, HH), BF16),
        vm((X, rows, HID // X), BF16), vm((X, rows, HID // X), BF16),
        vm((Z, X, YL * 16, DH), F32), vm((Z, X, YL * 16, DH), BF16), vm((Z, X, YL * 16, DH), BF16),
        vm((Z, X, YL * 16, DH), BF16), vm((X, Z, YL * 16, DH), BF16),
        vm((Z, YL * 16, DH), BF16), vm((Z, YL * 16, DH), BF16),
        vm((YL, 16, DH), BF16), vm((Y, 16, DH), BF16), vm((C, 8, DH), F32), vm((C, 8, DH), F32),
        vm((CP, HH), F32), vm((CP, HH), BF16), vm((CP, HH), BF16),
        vm((X, CP, cw), BF16), vm((X, CP, cw), BF16), vm((nb, cb, cw), BF16), vm((Z, cb, cw), BF16),
        vm((cb, cw), BF16), vm((Y, cb, cw), BF16), vm((cb, cw), BF16), vm((nb, cb, cw), BF16),
        vm((X, nb, cb, cw), BF16), vm((X, nb, cb, cw), BF16),
        dma((3,)),
        dma((Z,)), dma((Z,)), dma((Q,)), dma((Q,)),
        dma((Y,)), dma((C,)), dma((Z,)), dma((Z,)), dma((X,)), dma((X,)), dma, dma,
        dma((Z,)), dma((Z,)), dma((Q,)), dma((Q,)), dma((Q,)), dma((Q,)), dma((Z,)), dma((Z,)),
        dma((Z,)), dma((Z,)), dma((Q,)), dma((Q,)), dma((Q,)), dma((Q,)), dma((Z,)), dma((Z,)), dma((X,)), dma((X,)),
        dma, dma, dma((X,)), dma((X,)), dma((Z,)), dma((Z,)), dma((YL,)), dma((Y,)), dma((X * C,)), dma((C,)),
        dma, dma, dma((X,)), dma((X,)), dma((Z,)), dma((Z,)), dma((Y,)), dma((Y,)), dma((Z,)), dma((Z,)),
        dma((X,)), dma((X,)), dma, dma,
    ]
    hbm = pl.BlockSpec(memory_space=pl.ANY)
    vmem = pl.BlockSpec(memory_space=pltpu.VMEM)
    smem = pl.BlockSpec(memory_space=pltpu.SMEM)
    hidden_grad, class_grad, node_grad = pl.pallas_call(
        functools.partial(kernel, dims),
        out_shape=(
            jax.ShapeDtypeStruct(hidden_weight.shape, F32),
            jax.ShapeDtypeStruct((CP, HID), BF16),
            jax.ShapeDtypeStruct((rows, HID // X), BF16),
        ),
        in_specs=[hbm, vmem, vmem, vmem, vmem, smem, hbm, smem, hbm, vmem],
        out_specs=(vmem, vmem, vmem),
        scratch_shapes=scratch,
        compiler_params=pltpu.CompilerParams(
            collective_id=0, has_side_effects=True, vmem_limit_bytes=56 * 1024 * 1024
        ),
        cost_estimate=pl.CostEstimate(flops=2_000_000_000, bytes_accessed=3_000_000, transcendentals=20_000),
    )(
        features, hidden_weight, class_weight, request_ids.T, request_counts.T,
        outer_tiles, outer_masks, inner_tiles, inner_masks, labels.reshape(1, -1),
    )
    return hidden_grad, class_grad[:classes].astype(F32), node_grad


def solution(mesh):
    grid = GRIDS[(mesh.shape["owner"], mesh.shape["rep"])]
    placed = (
        P("owner", None),
        P("owner", None),
        P(),
        P(("owner", "rep"), None),
        P(("owner", "rep"), None),
        P(("owner", "rep"), None),
        P(("owner", "rep"), None, None, None),
        P(("owner", "rep"), None),
        P(("owner", "rep"), None, None, None),
        P(("owner", "rep")),
    )
    return jax.shard_map(
        functools.partial(on_device, grid),
        mesh=mesh,
        in_specs=placed,
        out_specs=(P("owner", None), P(), P("owner", "rep")),
        check_vma=False,
    )
```

```python
import functools

import jax
import jax.numpy as jnp
from jax import lax
from jax.experimental import pallas as pl
from jax.experimental.pallas import tpu as pltpu
from jax.sharding import PartitionSpec as P

MESH = pl.DeviceIdType.MESH
F32 = jnp.float32
BF16 = jnp.bfloat16

GRIDS = {(128, 4): (8, 8, 2, 4), (16, 2): (2, 4, 2, 2)}


def iota(shape, dim):
    return lax.broadcasted_iota(jnp.int32, shape, dim)


def quo(a, n):
    return lax.shift_right_logical(a, jnp.full_like(a, n.bit_length() - 1))


def rem(a, n):
    return lax.bitwise_and(a, jnp.full_like(a, n - 1))


def flag(cond, dtype=BF16):
    return jnp.where(cond, 1.0, 0.0).astype(F32).astype(dtype)


def dot(a, b, ca=1, cb=0):
    return lax.dot_general(a, b, (((ca,), (cb,)), ((), ())), preferred_element_type=F32)


def regroup(outer, middle, inner, transpose=False):
    n = outer * middle * inner
    o, i = iota((n, n), 0), iota((n, n), 1)
    if transpose:
        o, i = i, o
    m, rest = quo(o, outer * inner), rem(o, outer * inner)
    a, b = quo(rest, inner), rem(rest, inner)
    return flag(i == a * (middle * inner) + m * inner + b)


def kernel(
    dims,
    feat_hbm, weight_ref, cls_hbm, ids_ref, counts_ref, otile_ref, omask_hbm, itile_ref, imask_hbm, labels_ref,
    hidden_out, class_out, node_out,
    feat, omask, imask, cls,
    i1s, i1r, i2s, i2r, wx, place_a, place_b,
    ws, wr, w_all,
    fa1s, fa1r, fa2s, fa2r, fb1s, fb1r, fb2s, fb2r, move_a, move_b, swap_a, swap_b,
    agg, agr, pre, pg, pgr,
    na1s, na1r, na2s, na2r, nb1s, nb1r, nb2s, nb2r,
    gs1, gr1, gs2, gr2, gs3, gr3, gs4, gr4,
    cmine, cs0, cr0, cs1, cr1, cs2, cr2, cs3, cr3, cfin, ca4, ca5,
    local_sem,
    i1_ss, i1_rs, i2_ss, i2_rs, wx_ss, wx_rs,
    w1_ss, w1_rs, w2_ss, w2_rs, w3_ss, w3_rs, w4_ss, w4_rs,
    fa1_ss, fa1_rs, fa2_ss, fa2_rs, fb1_ss, fb1_rs, fb2_ss, fb2_rs,
    na1_ss, na1_rs, na2_ss, na2_rs, nb1_ss, nb1_rs, nb2_ss, nb2_rs,
    ga_ss, ga_rs, g0_ss, g0_rs, g1_ss, g1_rs, g2_ss, g2_rs, g3_ss, g3_rs, g4_ss, g4_rs,
    c0_ss, c0_rs, c1_ss, c1_rs, c2_ss, c2_rs, c3_ss, c3_rs, c4_ss, c4_rs, c5_ss, c5_rs,
):
    Z, Y, C, X, cap, tile, rows, classes = dims
    Q = Y * C
    NO = Z * Q
    half = cap // 2
    hop, front = NO * half, NO * cap
    D, HID = feat.shape[1], pre.shape[1]
    DH, HH = D // 2, HID // 2
    YL = Y // X
    nb, cb, cw = cs2.shape
    CP = nb * cb
    seeds = labels_ref.shape[1]
    row_blocks, col_blocks, K = hop // tile, front // tile, otile_ref.shape[1]
    LW = i2s.shape[2]
    S8 = 8

    me_o = lax.axis_index("owner")
    x = lax.axis_index("rep")
    z = me_o // Q
    q = me_o % Q
    y = q // C
    c = q % C
    sib = C - 1 - c

    def copy(src, dst, ss, rs, zz, qq, xx):
        return pltpu.make_async_remote_copy(
            src_ref=src, dst_ref=dst, send_sem=ss, recv_sem=rs,
            device_id=(zz * Q + qq, xx), device_id_type=MESH,
        )

    def each(n, body):
        def step(i, carry):
            body(i)
            return carry
        lax.fori_loop(1, n, step, 0)

    class Exchange:
        def __init__(self, n, me, at, src, dst, bulk, ss, rs):
            self.n, self.me, self.at, self.src, self.dst, self.bulk, self.ss, self.rs = n, me, at, src, dst, bulk, ss, rs

        def start(self):
            def send(d):
                to = lax.bitwise_and(self.me + d, self.n - 1)
                copy(self.src(to), self.dst(self.me), self.ss, self.rs, *self.at(to)).start()
            each(self.n, send)

        def all(self):
            return copy(self.bulk, self.bulk, self.ss, self.rs, *self.at(lax.bitwise_and(self.me + 1, self.n - 1)))

        def recv(self):
            self.all().wait_recv()

        def sent(self):
            self.all().wait_send()

    def along_z(*rest):
        return Exchange(Z, z, lambda t: (t, q, x), *rest)

    def along_q(*rest):
        return Exchange(Q, q, lambda t: (z, t, x), *rest)

    def along_y(*rest):
        return Exchange(Y, y, lambda t: (z, t * C + c, x), *rest)

    def along_x(*rest):
        return Exchange(X, x, lambda t: (z, q, t), *rest)

    def along_xz(*rest):
        return Exchange(X * Z, x * Z + z, lambda t: (lax.bitwise_and(t, Z - 1), q, t // Z), *rest)

    def along_xc(*rest):
        return Exchange(X * C, x * C + c, lambda t: (z, y * C + lax.bitwise_and(t, C - 1), t // C), *rest)

    def blocks(ref, n):
        return ref.at[pl.ds(0, n - 1)]

    def to_sibling(src, dst, ss, rs):
        return copy(src, dst, ss, rs, z, y * C + sib, x)

    loads = [
        pltpu.make_async_copy(feat_hbm, feat, local_sem.at[0]),
        pltpu.make_async_copy(omask_hbm, omask, local_sem.at[1]),
        pltpu.make_async_copy(imask_hbm, imask, local_sem.at[2]),
        pltpu.make_async_copy(cls_hbm, cls, local_sem.at[3]),
    ]
    for load in loads:
        load.start()

    barrier = pltpu.get_barrier_semaphore()

    def greet(zz, qq, xx):
        pl.semaphore_signal(barrier, inc=1, device_id=(zz * Q + qq, xx), device_id_type=MESH)

    def greet_xz(d):
        t = lax.bitwise_and(x * Z + z + d, X * Z - 1)
        greet(lax.bitwise_and(t, Z - 1), q, t // Z)

    each(Q, lambda d: greet(z, lax.bitwise_and(q + d, Q - 1), x))
    each(X * Z, greet_xz)
    each(X, lambda d: greet(z, y * C + sib, lax.bitwise_and(x + d, X - 1)))

    i1s[...] = jnp.zeros_like(i1s)
    i1s[0:cap, :] = ids_ref[...].astype(F32)
    w32 = weight_ref[...].astype(F32)
    ws[...] = jnp.concatenate([w32[:, :DH], w32[:, DH:]], axis=0).astype(BF16)

    pl.semaphore_wait(barrier, (Q - 1) + (X * Z - 1) + (X - 1))

    ex_i1 = along_z(lambda t: i1s, lambda f: i1r.at[f], blocks(i1r, Z), i1_ss, i1_rs)
    ex_i1.start()
    i1r[z] = i1s[...]

    w_core = y % C

    def w1_copy(t):
        return copy(ws, wr.at[c], w1_ss.at[t], w1_rs.at[c], z, t * C + w_core, x)

    def w1_each(act):
        def step(t, carry):
            @pl.when((y // C == x) & jnp.logical_not((t == y) & (w_core == c)))
            def _():
                act(t)
            return carry
        lax.fori_loop(0, Y, step, 0)

    w1_each(lambda t: w1_copy(t).start())
    y_mine = x * C + c

    ex_i1.recv()
    marks = flag(iota((Q, NO), 1) == z * Q + iota((Q, NO), 0))
    asked = i1r[...].reshape(Z * S8, NO).astype(BF16)
    if LW > Z * S8:
        asked = jnp.concatenate([asked] * (LW // (Z * S8)), axis=0)
    for_q = dot(marks, asked, 1, 1)
    for k in range(Q):
        i2s[k] = jnp.broadcast_to(for_q[k:k + 1, :], (8, LW))
    ex_i2 = along_q(lambda t: i2s.at[t], lambda f: i2r.at[f], blocks(i2r, Q), i2_ss, i2_rs)
    ex_i2.start()
    i2r[q] = i2s[q]

    for c0 in range(C):
        own = (y == y_mine) & (c == c0)

        @pl.when(own)
        def _():
            wr[c0] = ws[...]

        @pl.when(jnp.logical_not(own))
        def _():
            copy(ws, wr.at[c0], w1_ss.at[0], w1_rs.at[c0], z, y_mine * C + c0, x).wait_recv()
    for hcol in range(2):
        cols = slice(hcol * DH, (hcol + 1) * DH)
        w_all[z, x, c, :, cols] = jnp.concatenate(
            [wr[c0, hcol * 8:(hcol + 1) * 8, :].astype(F32) for c0 in range(C)], axis=0
        ).astype(BF16)
    ex_w2 = along_z(
        lambda t: w_all.at[z, x, c], lambda f: w_all.at[f, x, c], w_all.at[pl.ds(0, Z - 1), x, c], w2_ss, w2_rs
    )
    ex_w2.start()

    for load in loads[:1]:
        load.wait()
    lane_q = iota((front, Q * 8), 1)

    ex_i2.recv()
    wanted = i2r[...].reshape(Q * 8, LW).astype(BF16)

    wx[x] = wanted
    ex_wx = along_x(lambda t: wx.at[x], lambda f: wx.at[f], blocks(wx, X), wx_ss, wx_rs)

    def picked(col_of, q_of):
        spread = dot(flag(iota((front, LW), 1) == col_of), wanted, 1, 1)
        ids = jnp.sum(jnp.where(lane_q == q_of * 8, spread, 0.0), axis=1, keepdims=True)
        return flag(ids == iota((front, rows), 1).astype(F32))

    r = iota((front, 1), 0)
    pick_a = picked(quo(r, cap * Q) * S8 + quo(rem(r, cap * Q), Q), rem(r, Q))
    fa1s[...] = dot(pick_a, feat[:, :DH]).astype(BF16).reshape(fa1s.shape)
    ex_fa1 = along_z(lambda t: fa1s.at[t], lambda f: fa1r.at[f], blocks(fa1r, Z), fa1_ss, fa1_rs)
    ex_fa1.start()
    fa1r[z] = fa1s[z]
    pick_b = picked(rem(r, Z) * S8 + quo(rem(r, cap * Z), Z), quo(r, cap * Z))
    fb1s[...] = dot(pick_b, feat[:, DH:]).astype(BF16).reshape(fb1s.shape)
    ex_fb1 = along_q(lambda t: fb1s.at[t], lambda f: fb1r.at[f], blocks(fb1r, Q), fb1_ss, fb1_rs)
    ex_fb1.start()
    fb1r[q] = fb1s[q]
    ex_wx.start()
    move_a[...] = regroup(Z * cap, Q, 1)
    move_b[...] = regroup(Q * cap, Z, 1)

    ex_w2.recv()
    ex_w3 = along_x(
        lambda t: w_all.at[:, x, c], lambda f: w_all.at[:, f, c], w_all.at[:, pl.ds(0, X - 1), c], w3_ss, w3_rs
    )
    ex_w3.start()

    for load in loads[1:]:
        load.wait()
    counts = counts_ref[...].astype(F32)
    counts8 = jnp.concatenate([counts, jnp.zeros((6, NO), F32)], axis=0).astype(BF16)

    def validity(slots):
        n = NO * slots
        at = iota((NO, n), 1)
        per = dot(counts8, flag(iota((NO, n), 0) == quo(at, slots)))
        j = rem(iota((1, n), 1), slots).astype(F32)
        first = flag(j < per[0:1, :], F32)
        second = flag(j - half < per[1:2, :], F32)
        return jnp.where(j < half, first, second)

    valid = validity(cap)
    outer_rows = []
    for b in range(row_blocks):
        tiles = []
        for cbk in range(col_blocks):
            m = jnp.zeros((tile, tile), jnp.int32)
            for k in range(K):
                m = m + omask[b, k] * (otile_ref[b, k] == cbk).astype(jnp.int32)
            tiles.append(m.astype(F32) * valid[:, cbk * tile:(cbk + 1) * tile])
        outer_rows.append(jnp.concatenate(tiles, axis=1))
    outer = jnp.concatenate(outer_rows, axis=0)
    outer_scale = 1.0 + jnp.sum(outer, axis=1, keepdims=True)
    oi, oc = iota((hop, front), 0), iota((hop, front), 1)
    self_col = quo(oi, half) * cap + rem(oi, half)
    outer_self = (outer + flag(oc == self_col, F32)).astype(BF16)
    outer_a = dot(outer_self, regroup(Z, Q, cap, transpose=True)).astype(BF16)

    hop_valid = validity(half)
    tiles = []
    for cbk in range(row_blocks):
        m = jnp.zeros((tile, tile), jnp.int32)
        for k in range(K):
            m = m + imask[0, k] * (itile_ref[0, k] == cbk).astype(jnp.int32)
        tiles.append(m.astype(F32) * hop_valid[:, cbk * tile:(cbk + 1) * tile])
    inner32 = jnp.concatenate(tiles, axis=1)
    inner_degree = jnp.maximum(jnp.sum(inner32, axis=1, keepdims=True), 1.0)
    inner = inner32.astype(BF16)

    label_row = labels_ref[...]
    label_col = jnp.sum(
        jnp.where(iota((seeds, seeds), 0) == iota((seeds, seeds), 1), label_row, 0), axis=1, keepdims=True
    )
    one_hot = flag(label_col == iota((seeds, classes), 1), F32)

    ex_fa1.recv()
    fa2s[...] = dot(move_a[...], fa1r[...].reshape(front, DH)).astype(BF16).reshape(fa2s.shape)
    ex_fa2 = along_q(lambda t: fa2s.at[t], lambda f: fa2r.at[f], blocks(fa2r, Q), fa2_ss, fa2_rs)
    ex_fa2.start()
    fa2r[q] = fa2s[q]
    ex_fb1.recv()
    fb2s[...] = dot(move_b[...], fb1r[...].reshape(front, DH)).astype(BF16).reshape(fb2s.shape)
    ex_fb2 = along_z(lambda t: fb2s.at[t], lambda f: fb2r.at[f], blocks(fb2r, Z), fb2_ss, fb2_rs)
    ex_fb2.start()
    fb2r[z] = fb2s[z]

    ex_w3.recv()
    w4 = to_sibling(w_all.at[:, :, c], w_all.at[:, :, c], w4_ss, w4_rs)
    w4_in = to_sibling(w_all.at[:, :, sib], w_all.at[:, :, sib], w4_ss, w4_rs)
    w4.start()

    swap_a[...] = regroup(Z, Q, half)
    swap_b[...] = regroup(Q, Z, half)
    ex_wx.recv()

    def places(x_of, j_of, z_of, q_of):
        n = X * hop
        pick = flag(iota((LW, n), 0) == z_of * S8 + j_of)
        ids = jnp.zeros((1, n), F32)
        for k in range(X):
            here = (iota((Q * 8, n), 0) == q_of * 8) & (x_of == k)
            ids = ids + jnp.sum(jnp.where(here, dot(wx[k], pick), 0.0), axis=0, keepdims=True)
        return flag(iota((rows, n), 0).astype(F32) == ids)

    s = iota((1, X * hop), 1)
    place_a[...] = places(
        rem(quo(s, half * Z), X), rem(s, half), rem(quo(s, half), Z), quo(s, half * Z * X)
    )
    place_b[...] = places(
        quo(s, half * Q * Z), rem(s, half), rem(quo(s, half * Q), Z), rem(quo(s, half), Q)
    )

    ex_fa2.recv()
    agg[0] = (dot(outer_a, fa2r[...].reshape(front, DH)) / outer_scale).astype(BF16)
    w4_in.wait_recv()
    pre[...] = dot(agg[0], w_all[:, :, :, :, :DH].reshape(HID, DH), 1, 1)
    ex_fb2.recv()
    agg[1] = (dot(outer_self, fb2r[...].reshape(front, DH)) / outer_scale).astype(BF16)
    ga = to_sibling(agg.at[sib], agr, ga_ss, ga_rs)
    ga.start()

    pre[...] = pre[...] + dot(agg[1], w_all[:, :, :, :, DH:].reshape(HID, DH), 1, 1)
    hidden = jnp.maximum(pre[...], 0.0).astype(BF16)
    agg_two = (dot(inner, hidden) / inner_degree).astype(BF16)
    logits = dot(agg_two, cls[...], 1, 1)
    exponent = jnp.exp(logits - jnp.max(logits, axis=1, keepdims=True))
    softmax = exponent / jnp.sum(exponent, axis=1, keepdims=True)
    logit_grad = ((softmax - one_hot) / seeds).astype(BF16)
    agg_grad = dot(logit_grad, cls[...]) / inner_degree
    high = agg_grad.astype(BF16)
    low = (agg_grad - high.astype(F32)).astype(BF16)
    hidden_diff = dot(inner, high, 0, 0) + dot(inner, low, 0, 0)

    pg[...] = jnp.where(pre[...] > 0.0, hidden_diff, 0.0).astype(BF16)
    g0 = to_sibling(pg, pgr, g0_ss, g0_rs)
    g0.start()

    diff16 = hidden_diff.astype(BF16)
    xw = HID // X
    xh = xw // 2
    for t in range(X):
        na1s[t * Z:(t + 1) * Z] = diff16[:, t * xw:t * xw + xh].reshape(Z, Q * half, xh)
    ex_na1 = along_xz(lambda t: na1s.at[t], lambda f: na1r.at[f], blocks(na1r, X * Z), na1_ss, na1_rs)
    ex_na1.start()
    me_xz = x * Z + z
    na1r[me_xz] = na1s[me_xz]
    second = jnp.concatenate([diff16[:, t * xw + xh:(t + 1) * xw] for t in range(X)], axis=1)
    nb1s[...] = dot(swap_a[...], second).astype(BF16).reshape(nb1s.shape)
    ex_nb1 = along_q(lambda t: nb1s.at[t], lambda f: nb1r.at[f], blocks(nb1r, Q), nb1_ss, nb1_rs)
    ex_nb1.start()
    nb1r[q] = nb1s[q]

    widen = flag(iota((classes, CP), 0) == iota((classes, CP), 1))
    class_rows = dot(dot(logit_grad, widen).astype(BF16), agg_two, 0, 0)
    left, right = class_rows[:, :HH], class_rows[:, HH:]
    cs0[...] = jnp.where(c == 0, right, left).astype(BF16)
    cmine[...] = jnp.where(c == 0, left, right)
    c0 = to_sibling(cs0, cr0, c0_ss, c0_rs)
    c0.start()

    gmine = dot(pg[...], agg[c], 0, 0)
    ga.wait_recv()
    g0.wait_recv()
    gmine = gmine + dot(pgr[...], agr[...], 0, 0)
    gs1[...] = gmine.astype(BF16).reshape(gs1.shape)
    ex_g1 = along_x(lambda t: gs1.at[:, t], lambda f: gr1.at[f], blocks(gr1, X), g1_ss, g1_rs)
    ex_g1.start()
    gr1[x] = gs1[:, x]

    c0.wait_recv()
    cmine[...] = cmine[...] + cr0[...].astype(F32)
    for t in range(X):
        cs1[t] = cmine[:, t * cw:(t + 1) * cw].astype(BF16)
    ex_c1 = along_x(lambda t: cs1.at[t], lambda f: cr1.at[f], blocks(cr1, X), c1_ss, c1_rs)
    ex_c1.start()
    cr1[x] = cs1[x]

    ex_na1.recv()
    came = jnp.concatenate([na1r[t * Z:(t + 1) * Z].reshape(hop, xh) for t in range(X)], axis=1)
    came = dot(swap_a[...], came).astype(BF16)
    for t in range(X):
        na2s[:, t] = came[:, t * xh:(t + 1) * xh].reshape(Q, Z * half, xh)
    ex_na2 = along_q(lambda t: na2s.at[t], lambda f: na2r.at[f], blocks(na2r, Q), na2_ss, na2_rs)
    ex_na2.start()
    na2r[q] = na2s[q]
    ex_nb1.recv()
    came = dot(swap_b[...], nb1r[...].reshape(hop, X * xh)).astype(BF16)
    for t in range(X):
        nb2s[t * Z:(t + 1) * Z] = came[:, t * xh:(t + 1) * xh].reshape(Z, Q * half, xh)
    ex_nb2 = along_xz(lambda t: nb2s.at[t], lambda f: nb2r.at[f], blocks(nb2r, X * Z), nb2_ss, nb2_rs)
    ex_nb2.start()
    nb2r[me_xz] = nb2s[me_xz]

    def total(ref, n):
        acc = ref[0].astype(F32)
        for k in range(1, n):
            acc = acc + ref[k].astype(F32)
        return acc

    ex_g1.recv()
    gs2[...] = total(gr1, X).astype(BF16)
    ex_g2 = along_z(lambda t: gs2.at[t], lambda f: gr2.at[f], blocks(gr2, Z), g2_ss, g2_rs)
    ex_g2.start()
    gr2[z] = gs2[z]

    ex_c1.recv()
    cs2[...] = total(cr1, X).astype(BF16).reshape(cs2.shape)

    def to_blocks(act):
        def step(t, carry):
            @pl.when(t != z)
            def _():
                act(t)
            return carry
        lax.fori_loop(0, nb, step, 0)

    to_blocks(lambda t: copy(cs2.at[t], cr2.at[z], c2_ss, c2_rs, t, q, x).start())
    summing = z < nb

    ex_c2 = along_z(None, None, blocks(cr2, Z), c2_ss, c2_rs)
    ex_c3 = along_y(lambda t: cs3, lambda f: cr3.at[f], blocks(cr3, Y), c3_ss, c3_rs)
    ex_c4 = along_z(lambda t: cfin, lambda f: ca4.at[f], blocks(cr2, Z), c4_ss, c4_rs)

    @pl.when(summing)
    def _():
        cr2[z] = cs2[z]
        ex_c2.recv()
        cs3[...] = total(cr2, Z).astype(BF16)
        ex_c3.start()
        cr3[y] = cs3[...]

    ex_g2.recv()
    gs3[...] = total(gr2, Z).astype(BF16).reshape(gs3.shape)

    def g3_copy(yl):
        return copy(gs3.at[yl], gr3.at[y], g3_ss.at[yl], g3_rs, z, (x * YL + yl) * C + c, x)

    for yl in range(YL):
        @pl.when(x * YL + yl != y)
        def _():
            g3_copy(yl).start()
    owning = y // YL == x

    @pl.when(summing)
    def _():
        ex_c3.recv()
        cfin[...] = total(cr3, Y).astype(BF16)
        ex_c4.start()
        ca4[z] = cfin[...]

    ex_na2.recv()
    node_out[:, :xh] = dot(place_a[...], na2r[...].reshape(X * hop, xh)).astype(BF16)
    ex_nb2.recv()
    node_out[:, xh:] = dot(place_b[...], nb2r[...].reshape(X * hop, xh)).astype(BF16)

    def g4_copy(xx, cc):
        return copy(gs4.at[cc], gr4.at[c], g4_ss.at[xx * C + cc], g4_rs.at[c], z, y * C + cc, xx)

    def g4_each(act):
        for xx in range(X):
            for cc in range(C):
                @pl.when(owning & jnp.logical_not((x == xx) & (c == cc)))
                def _():
                    act(xx, cc)

    @pl.when(owning)
    def _():
        gr3[y] = gs3[y % YL]
        copy(blocks(gr3, Y), blocks(gr3, Y), g3_ss.at[0], g3_rs, z, q, x).wait_recv()
        gs4[...] = total(gr3, Y).reshape(gs4.shape)
        gr4[c] = gs4[c]

    g4_each(lambda xx, cc: g4_copy(xx, cc).start())

    @pl.when(summing)
    def _():
        some = ca4.at[pl.ds(0, nb - 1)]
        copy(some, some, c4_ss, c4_rs, z, q, x).wait_recv()

    @pl.when(jnp.logical_not(summing))
    def _():
        copy(ca4, ca4, c4_ss, c4_rs, z, q, x).wait_recv()

    me_xc = x * C + c
    ex_c5 = along_xc(lambda t: ca4, lambda f: ca5.at[f], blocks(ca5, X * C), c5_ss, c5_rs)
    ex_c5.start()
    ca5[me_xc] = ca4[...]

    for cc in range(C):
        @pl.when(jnp.logical_not(owning & (c == cc)))
        def _():
            copy(gs4.at[0], gr4.at[cc], g4_ss.at[0], g4_rs.at[cc], z, y * C + cc, y // YL).wait_recv()
        hidden_out[:, cc * DH:(cc + 1) * DH] = gr4[cc]

    ex_c5.recv()
    for t in range(X):
        for cc in range(C):
            class_out[:, cc * HH + t * cw:cc * HH + (t + 1) * cw] = ca5[t * C + cc].reshape(CP, cw)

    for ex in (ex_i1, ex_i2, ex_wx, ex_w2, ex_w3, ex_fa1, ex_fb1, ex_fa2, ex_fb2, ex_na1, ex_nb1, ex_na2, ex_nb2,
               ex_g1, ex_g2, ex_c1, ex_c5):
        ex.sent()
    w1_each(lambda t: w1_copy(t).wait_send())
    for one in (w4, ga, g0, c0):
        one.wait_send()

    @pl.when(summing)
    def _():
        some = cs2.at[pl.ds(0, nb - 1)]
        copy(some, some, c2_ss, c2_rs, z, q, x).wait_send()
        ex_c3.sent()
        ex_c4.sent()

    @pl.when(jnp.logical_not(summing))
    def _():
        copy(cs2, cs2, c2_ss, c2_rs, z, q, x).wait_send()

    for yl in range(YL):
        @pl.when(x * YL + yl != y)
        def _():
            g3_copy(yl).wait_send()
    g4_each(lambda xx, cc: g4_copy(xx, cc).wait_send())


def on_device(
    grid, features, hidden_weight, class_weight, request_ids, request_counts,
    outer_tiles, outer_masks, inner_tiles, inner_masks, labels,
):
    Z, Y, C, X = grid
    Q = Y * C
    NO = Z * Q
    cap = request_ids.shape[1]
    half = cap // 2
    rows, D = features.shape
    classes, HID = class_weight.shape
    tile = outer_masks.shape[2]
    hop = NO * half
    DH, HH, YL = D // 2, HID // 2, Y // X
    cb = 32 if classes > 32 else 8
    nb = -(-classes // cb)
    CP, cw = nb * cb, HID // (C * X)
    LW = max(Z * 8, 128)
    dims = (Z, Y, C, X, cap, tile, rows, classes)
    vm, dma = pltpu.VMEM, pltpu.SemaphoreType.DMA
    xh = HID // X // 2
    scratch = [
        vm(features.shape, BF16), vm(outer_masks.shape, jnp.int32), vm(inner_masks.shape, jnp.int32),
        vm(class_weight.shape, BF16),
        vm((8, NO), F32), vm((Z, 8, NO), F32), vm((Q, 8, LW), F32), vm((Q, 8, LW), F32),
        vm((X, Q * 8, LW), BF16), vm((rows, X * hop), BF16), vm((rows, X * hop), BF16),
        vm((16, DH), BF16), vm((C, 16, DH), BF16), vm((Z, X, C, 16, D), BF16),
        vm((Z, cap * Q, DH), BF16), vm((Z, cap * Q, DH), BF16), vm((Q, cap * Z, DH), BF16), vm((Q, cap * Z, DH), BF16),
        vm((Q, cap * Z, DH), BF16), vm((Q, cap * Z, DH), BF16), vm((Z, cap * Q, DH), BF16), vm((Z, cap * Q, DH), BF16),
        vm((cap * NO, cap * NO), BF16), vm((cap * NO, cap * NO), BF16), vm((hop, hop), BF16), vm((hop, hop), BF16),
        vm((2, hop, DH), BF16), vm((hop, DH), BF16), vm((hop, HID), F32), vm((hop, HID), BF16), vm((hop, HID), BF16),
        vm((X * Z, Q * half, xh), BF16), vm((X * Z, Q * half, xh), BF16),
        vm((Q, X, Z * half, xh), BF16), vm((Q, X, Z * half, xh), BF16),
        vm((Q, Z * half, HH), BF16), vm((Q, Z * half, HH), BF16),
        vm((X * Z, Q * half, xh), BF16), vm((X * Z, Q * half, xh), BF16),
        vm((Z, X, YL * 16, DH), BF16), vm((X, Z, YL * 16, DH), BF16),
        vm((Z, YL * 16, DH), BF16), vm((Z, YL * 16, DH), BF16),
        vm((YL, 16, DH), BF16), vm((Y, 16, DH), BF16), vm((C, 8, DH), F32), vm((C, 8, DH), F32),
        vm((CP, HH), F32), vm((CP, HH), BF16), vm((CP, HH), BF16),
        vm((X, CP, cw), BF16), vm((X, CP, cw), BF16), vm((nb, cb, cw), BF16), vm((Z, cb, cw), BF16),
        vm((cb, cw), BF16), vm((Y, cb, cw), BF16), vm((cb, cw), BF16), vm((nb, cb, cw), BF16),
        vm((X * C, nb, cb, cw), BF16),
        dma((4,)),
        *[dma] * 6,
        dma((Y,)), dma((C,)), *[dma] * 6,
        *[dma] * 16,
        *[dma] * 8, dma((YL,)), dma, dma((X * C,)), dma((C,)),
        *[dma] * 12,
    ]
    hbm = pl.BlockSpec(memory_space=pl.ANY)
    vmem = pl.BlockSpec(memory_space=pltpu.VMEM)
    smem = pl.BlockSpec(memory_space=pltpu.SMEM)
    hidden_grad, class_grad, node_grad = pl.pallas_call(
        functools.partial(kernel, dims),
        out_shape=(
            jax.ShapeDtypeStruct(hidden_weight.shape, F32),
            jax.ShapeDtypeStruct((CP, HID), BF16),
            jax.ShapeDtypeStruct((rows, HID // X), BF16),
        ),
        in_specs=[hbm, vmem, hbm, vmem, vmem, smem, hbm, smem, hbm, vmem],
        out_specs=(vmem, vmem, vmem),
        scratch_shapes=scratch,
        compiler_params=pltpu.CompilerParams(
            collective_id=0, has_side_effects=True, vmem_limit_bytes=56 * 1024 * 1024
        ),
        cost_estimate=pl.CostEstimate(flops=2_000_000_000, bytes_accessed=3_000_000, transcendentals=20_000),
    )(
        features, hidden_weight, class_weight, request_ids.T, request_counts.T,
        outer_tiles, outer_masks, inner_tiles, inner_masks, labels.reshape(1, -1),
    )
    return hidden_grad, class_grad[:classes].astype(F32), node_grad


def solution(mesh):
    grid = GRIDS[(mesh.shape["owner"], mesh.shape["rep"])]
    placed = (
        P("owner", None),
        P("owner", None),
        P(),
        P(("owner", "rep"), None),
        P(("owner", "rep"), None),
        P(("owner", "rep"), None),
        P(("owner", "rep"), None, None, None),
        P(("owner", "rep"), None),
        P(("owner", "rep"), None, None, None),
        P(("owner", "rep")),
    )
    return jax.shard_map(
        functools.partial(on_device, grid),
        mesh=mesh,
        in_specs=placed,
        out_specs=(P("owner", None), P(), P("owner", "rep")),
        check_vma=False,
    )
```

```python
import functools

import jax
import jax.numpy as jnp
from jax import lax
from jax.experimental import pallas as pl
from jax.experimental.pallas import tpu as pltpu
from jax.sharding import PartitionSpec as P

MESH = pl.DeviceIdType.MESH
F32 = jnp.float32
BF16 = jnp.bfloat16

GRIDS = {(128, 4): (8, 8, 2, 4), (32, 4): (2, 8, 2, 4)}


def iota(shape, dim):
    return lax.broadcasted_iota(jnp.int32, shape, dim)


def quo(a, n):
    return lax.shift_right_logical(a, jnp.full_like(a, n.bit_length() - 1))


def rem(a, n):
    return lax.bitwise_and(a, jnp.full_like(a, n - 1))


def flag(cond, dtype=BF16):
    return jnp.where(cond, 1.0, 0.0).astype(F32).astype(dtype)


def dot(a, b, ca=1, cb=0):
    return lax.dot_general(a, b, (((ca,), (cb,)), ((), ())), preferred_element_type=F32)


def regroup(outer, middle, inner, transpose=False):
    n = outer * middle * inner
    o, i = iota((n, n), 0), iota((n, n), 1)
    if transpose:
        o, i = i, o
    m, rest = quo(o, outer * inner), rem(o, outer * inner)
    a, b = quo(rest, inner), rem(rest, inner)
    return flag(i == a * (middle * inner) + m * inner + b)


def kernel(
    dims,
    feat_hbm, weight_ref, cls_hbm, ids_ref, counts_ref, otile_ref, omask_hbm, itile_ref, imask_hbm, labels_ref,
    hidden_out, class_out, node_out,
    feat, omask, imask, cls,
    i1s, i1r, i2s, i2r, wx, place_a, place_b,
    ws, wr, w_all,
    fa1s, fa1r, fa2s, fa2r, fb1s, fb1r, fb2s, fb2r, move_a, move_b, swap_a, swap_b,
    agg, agr, pre, pg, pgr,
    na1s, na1r, na2s, na2r, nb1s, nb1r, nb2s, nb2r,
    gs1, gra, grb, gsa, gsb, grl, grr, gs2, gr2, gs3, gr3, gs4, gr4,
    cs1, cr1, cs2, cr2, cs3, cr3, cfin, ca4, ca5,
    local_sem,
    i1_ss, i1_rs, i2_ss, i2_rs, wx_ss, wx_rs,
    w1_ss, w1_rs, w2_ss, w2_rs, w3_ss, w3_rs, w4_ss, w4_rs,
    fa1_ss, fa1_rs, fa2_ss, fa2_rs, fb1_ss, fb1_rs, fb2_ss, fb2_rs,
    na1_ss, na1_rs, na2_ss, na2_rs, nb1_ss, nb1_rs, nb2_ss, nb2_rs,
    ga_ss, ga_rs, g0_ss, g0_rs, g1_ss, g1_rs, g2_ss, g2_rs, g3_ss, g3_rs, g4_ss, g4_rs,
    c1_ss, c1_rs, c2_ss, c2_rs, c3_ss, c3_rs, c4_ss, c4_rs, c5_ss, c5_rs,
):
    Z, Y, C, X, cap, tile, rows, classes = dims
    Q = Y * C
    NO = Z * Q
    half = cap // 2
    hop, front = NO * half, NO * cap
    D, HID = feat.shape[1], pre.shape[1]
    DH, HH = D // 2, HID // 2
    YL = Y // X
    nb, cb, cw = cs2.shape
    CP = nb * cb
    seeds = labels_ref.shape[1]
    row_blocks, col_blocks, K = hop // tile, front // tile, otile_ref.shape[1]
    LW = i2s.shape[2]
    S8 = 8

    me_o = lax.axis_index("owner")
    x = lax.axis_index("rep")
    z = me_o // Q
    q = me_o % Q
    y = q // C
    c = q % C
    sib = C - 1 - c

    def copy(src, dst, ss, rs, zz, qq, xx):
        return pltpu.make_async_remote_copy(
            src_ref=src, dst_ref=dst, send_sem=ss, recv_sem=rs,
            device_id=(zz * Q + qq, xx), device_id_type=MESH,
        )

    def each(n, body):
        def step(i, carry):
            body(i)
            return carry
        lax.fori_loop(1, n, step, 0)

    class Exchange:
        def __init__(self, n, me, at, src, dst, bulk, ss, rs):
            self.n, self.me, self.at, self.src, self.dst, self.bulk, self.ss, self.rs = n, me, at, src, dst, bulk, ss, rs

        def start(self):
            def send(d):
                to = lax.bitwise_and(self.me + d, self.n - 1)
                copy(self.src(to), self.dst(self.me), self.ss, self.rs, *self.at(to)).start()
            each(self.n, send)

        def all(self):
            return copy(self.bulk, self.bulk, self.ss, self.rs, *self.at(lax.bitwise_and(self.me + 1, self.n - 1)))

        def recv(self):
            self.all().wait_recv()

        def sent(self):
            self.all().wait_send()

    def along_z(*rest):
        return Exchange(Z, z, lambda t: (t, q, x), *rest)

    def along_q(*rest):
        return Exchange(Q, q, lambda t: (z, t, x), *rest)

    def along_y(*rest):
        return Exchange(Y, y, lambda t: (z, t * C + c, x), *rest)

    def along_x(*rest):
        return Exchange(X, x, lambda t: (z, q, t), *rest)

    def along_xz(*rest):
        return Exchange(X * Z, x * Z + z, lambda t: (lax.bitwise_and(t, Z - 1), q, t // Z), *rest)

    def along_xc(*rest):
        return Exchange(X * C, x * C + c, lambda t: (z, y * C + lax.bitwise_and(t, C - 1), t // C), *rest)

    def blocks(ref, n):
        return ref.at[pl.ds(0, n - 1)]

    def to_sibling(src, dst, ss, rs):
        return copy(src, dst, ss, rs, z, y * C + sib, x)

    loads = [
        pltpu.make_async_copy(feat_hbm, feat, local_sem.at[0]),
        pltpu.make_async_copy(omask_hbm, omask, local_sem.at[1]),
        pltpu.make_async_copy(imask_hbm, imask, local_sem.at[2]),
        pltpu.make_async_copy(cls_hbm, cls, local_sem.at[3]),
    ]
    for load in loads:
        load.start()

    barrier = pltpu.get_barrier_semaphore()

    def greet(zz, qq, xx):
        pl.semaphore_signal(barrier, inc=1, device_id=(zz * Q + qq, xx), device_id_type=MESH)

    def greet_xz(d):
        t = lax.bitwise_and(x * Z + z + d, X * Z - 1)
        greet(lax.bitwise_and(t, Z - 1), q, t // Z)

    each(Q, lambda d: greet(z, lax.bitwise_and(q + d, Q - 1), x))
    each(X * Z, greet_xz)
    each(X, lambda d: greet(z, y * C + sib, lax.bitwise_and(x + d, X - 1)))

    i1s[...] = jnp.zeros_like(i1s)
    i1s[0:cap, :] = ids_ref[...].astype(F32)
    w32 = weight_ref[...].astype(F32)
    ws[...] = jnp.concatenate([w32[:, :DH], w32[:, DH:]], axis=0).astype(BF16)

    pl.semaphore_wait(barrier, (Q - 1) + (X * Z - 1) + (X - 1))

    ex_i1 = along_z(lambda t: i1s, lambda f: i1r.at[f], blocks(i1r, Z), i1_ss, i1_rs)
    ex_i1.start()
    i1r[z] = i1s[...]

    w_core = y % C

    def w1_copy(t):
        return copy(ws, wr.at[c], w1_ss.at[t], w1_rs.at[c], z, t * C + w_core, x)

    def w1_each(act):
        def step(t, carry):
            @pl.when((y // C == x) & jnp.logical_not((t == y) & (w_core == c)))
            def _():
                act(t)
            return carry
        lax.fori_loop(0, Y, step, 0)

    w1_each(lambda t: w1_copy(t).start())
    y_mine = x * C + c

    ex_i1.recv()
    marks = flag(iota((Q, NO), 1) == z * Q + iota((Q, NO), 0))
    asked = i1r[...].reshape(Z * S8, NO).astype(BF16)
    if LW > Z * S8:
        asked = jnp.concatenate([asked] * (LW // (Z * S8)), axis=0)
    for_q = dot(marks, asked, 1, 1)
    for k in range(Q):
        i2s[k] = jnp.broadcast_to(for_q[k:k + 1, :], (8, LW))
    ex_i2 = along_q(lambda t: i2s.at[t], lambda f: i2r.at[f], blocks(i2r, Q), i2_ss, i2_rs)
    ex_i2.start()
    i2r[q] = i2s[q]

    for c0 in range(C):
        own = (y == y_mine) & (c == c0)

        @pl.when(own)
        def _():
            wr[c0] = ws[...]

        @pl.when(jnp.logical_not(own))
        def _():
            copy(ws, wr.at[c0], w1_ss.at[0], w1_rs.at[c0], z, y_mine * C + c0, x).wait_recv()
    for hcol in range(2):
        cols = slice(hcol * DH, (hcol + 1) * DH)
        w_all[z, x, c, :, cols] = jnp.concatenate(
            [wr[c0, hcol * 8:(hcol + 1) * 8, :].astype(F32) for c0 in range(C)], axis=0
        ).astype(BF16)
    ex_w2 = along_z(
        lambda t: w_all.at[z, x, c], lambda f: w_all.at[f, x, c], w_all.at[pl.ds(0, Z - 1), x, c], w2_ss, w2_rs
    )
    ex_w2.start()

    for load in loads[:1]:
        load.wait()
    lane_q = iota((front, Q * 8), 1)

    ex_i2.recv()
    wanted = i2r[...].reshape(Q * 8, LW).astype(BF16)

    wx[x] = wanted
    ex_wx = along_x(lambda t: wx.at[x], lambda f: wx.at[f], blocks(wx, X), wx_ss, wx_rs)

    def picked(col_of, q_of):
        spread = dot(flag(iota((front, LW), 1) == col_of), wanted, 1, 1)
        ids = jnp.sum(jnp.where(lane_q == q_of * 8, spread, 0.0), axis=1, keepdims=True)
        return flag(ids == iota((front, rows), 1).astype(F32))

    chunks, wide = fa1s.shape[0], fa1s.shape[3]
    r = iota((front, 1), 0)
    pick_a = picked(quo(r, cap * Q) * S8 + quo(rem(r, cap * Q), Q), rem(r, Q))
    rows_a = dot(pick_a, feat[:, :DH]).astype(BF16)
    ex_fa1, ex_fb1, ex_fa2, ex_fb2 = [], [], [], []
    for k in range(chunks):
        at = slice(k * wide, (k + 1) * wide)
        fa1s[k] = rows_a[:, at].reshape(fa1s.shape[1:])
        ex_fa1.append(along_z(
            lambda t, k=k: fa1s.at[k, t], lambda f, k=k: fa1r.at[k, f], blocks(fa1r.at[k], Z), fa1_ss.at[k], fa1_rs.at[k]))
        ex_fb1.append(along_q(
            lambda t, k=k: fb1s.at[k, t], lambda f, k=k: fb1r.at[k, f], blocks(fb1r.at[k], Q), fb1_ss.at[k], fb1_rs.at[k]))
        ex_fa2.append(along_q(
            lambda t, k=k: fa2s.at[k, t], lambda f, k=k: fa2r.at[k, f], blocks(fa2r.at[k], Q), fa2_ss.at[k], fa2_rs.at[k]))
        ex_fb2.append(along_z(
            lambda t, k=k: fb2s.at[k, t], lambda f, k=k: fb2r.at[k, f], blocks(fb2r.at[k], Z), fb2_ss.at[k], fb2_rs.at[k]))
    ex_fa1[0].start()
    pick_b = picked(rem(r, Z) * S8 + quo(rem(r, cap * Z), Z), quo(r, cap * Z))
    rows_b = dot(pick_b, feat[:, DH:]).astype(BF16)
    for k in range(chunks):
        at = slice(k * wide, (k + 1) * wide)
        fb1s[k] = rows_b[:, at].reshape(fb1s.shape[1:])
    ex_fb1[0].start()
    for k in range(1, chunks):
        ex_fa1[k].start()
        ex_fb1[k].start()
    for k in range(chunks):
        fa1r[k, z] = fa1s[k, z]
        fb1r[k, q] = fb1s[k, q]
    ex_wx.start()
    move_a[...] = regroup(Z * cap, Q, 1)
    move_b[...] = regroup(Q * cap, Z, 1)

    ex_w2.recv()
    ex_w3 = along_x(
        lambda t: w_all.at[:, x, c], lambda f: w_all.at[:, f, c], w_all.at[:, pl.ds(0, X - 1), c], w3_ss, w3_rs
    )
    ex_w3.start()

    for load in loads[1:]:
        load.wait()
    counts = counts_ref[...].astype(F32)
    counts8 = jnp.concatenate([counts, jnp.zeros((6, NO), F32)], axis=0).astype(BF16)

    def validity(slots):
        n = NO * slots
        at = iota((NO, n), 1)
        per = dot(counts8, flag(iota((NO, n), 0) == quo(at, slots)))
        j = rem(iota((1, n), 1), slots).astype(F32)
        first = flag(j < per[0:1, :], F32)
        second = flag(j - half < per[1:2, :], F32)
        return jnp.where(j < half, first, second)

    valid = validity(cap)
    outer_rows = []
    for b in range(row_blocks):
        tiles = []
        for cbk in range(col_blocks):
            m = jnp.zeros((tile, tile), jnp.int32)
            for k in range(K):
                m = m + omask[b, k] * (otile_ref[b, k] == cbk).astype(jnp.int32)
            tiles.append(m.astype(F32) * valid[:, cbk * tile:(cbk + 1) * tile])
        outer_rows.append(jnp.concatenate(tiles, axis=1))
    outer = jnp.concatenate(outer_rows, axis=0)
    outer_scale = 1.0 + jnp.sum(outer, axis=1, keepdims=True)
    oi, oc = iota((hop, front), 0), iota((hop, front), 1)
    self_col = quo(oi, half) * cap + rem(oi, half)
    outer_self = (outer + flag(oc == self_col, F32)).astype(BF16)
    outer_a = dot(outer_self, regroup(Z, Q, cap, transpose=True)).astype(BF16)

    hop_valid = validity(half)
    tiles = []
    for cbk in range(row_blocks):
        m = jnp.zeros((tile, tile), jnp.int32)
        for k in range(K):
            m = m + imask[0, k] * (itile_ref[0, k] == cbk).astype(jnp.int32)
        tiles.append(m.astype(F32) * hop_valid[:, cbk * tile:(cbk + 1) * tile])
    inner32 = jnp.concatenate(tiles, axis=1)
    inner_degree = jnp.maximum(jnp.sum(inner32, axis=1, keepdims=True), 1.0)
    inner = inner32.astype(BF16)

    label_row = labels_ref[...]
    label_col = jnp.sum(
        jnp.where(iota((seeds, seeds), 0) == iota((seeds, seeds), 1), label_row, 0), axis=1, keepdims=True
    )
    one_hot = flag(label_col == iota((seeds, classes), 1), F32)

    for k in range(chunks):
        ex_fa1[k].recv()
        fa2s[k] = dot(move_a[...], fa1r[k].reshape(front, wide)).astype(BF16).reshape(fa2s.shape[1:])
        ex_fa2[k].start()
        fa2r[k, q] = fa2s[k, q]
        ex_fb1[k].recv()
        fb2s[k] = dot(move_b[...], fb1r[k].reshape(front, wide)).astype(BF16).reshape(fb2s.shape[1:])
        ex_fb2[k].start()
        fb2r[k, z] = fb2s[k, z]

    ex_w3.recv()
    w4 = to_sibling(w_all.at[:, :, c], w_all.at[:, :, c], w4_ss, w4_rs)
    w4_in = to_sibling(w_all.at[:, :, sib], w_all.at[:, :, sib], w4_ss, w4_rs)
    w4.start()

    swap_a[...] = regroup(Z, Q, half)
    swap_b[...] = regroup(Q, Z, half)
    ex_wx.recv()

    def places(x_of, j_of, z_of, q_of):
        n = X * hop
        pick = flag(iota((LW, n), 0) == z_of * S8 + j_of)
        ids = jnp.zeros((1, n), F32)
        for k in range(X):
            here = (iota((Q * 8, n), 0) == q_of * 8) & (x_of == k)
            ids = ids + jnp.sum(jnp.where(here, dot(wx[k], pick), 0.0), axis=0, keepdims=True)
        return flag(iota((rows, n), 0).astype(F32) == ids)

    s = iota((1, X * hop), 1)
    place_a[...] = places(
        rem(quo(s, half * Z), X), rem(s, half), rem(quo(s, half), Z), quo(s, half * Z * X)
    )
    place_b[...] = places(
        quo(s, half * Q * Z), rem(s, half), rem(quo(s, half * Q), Z), rem(quo(s, half), Q)
    )

    for k in range(chunks):
        at = slice(k * wide, (k + 1) * wide)
        ex_fa2[k].recv()
        agg[0, :, at] = (dot(outer_a, fa2r[k].reshape(front, wide)) / outer_scale).astype(BF16)
        if k < chunks - 1:
            ex_fb2[k].recv()
            agg[1, :, at] = (dot(outer_self, fb2r[k].reshape(front, wide)) / outer_scale).astype(BF16)
    w4_in.wait_recv()
    pre[...] = dot(agg[0], w_all[:, :, :, :, :DH].reshape(HID, DH), 1, 1)
    ex_fb2[-1].recv()
    agg[1, :, DH - wide:] = (dot(outer_self, fb2r[chunks - 1].reshape(front, wide)) / outer_scale).astype(BF16)
    ga = to_sibling(agg.at[sib], agr, ga_ss, ga_rs)
    ga.start()

    pre[...] = pre[...] + dot(agg[1], w_all[:, :, :, :, DH:].reshape(HID, DH), 1, 1)
    hidden = jnp.maximum(pre[...], 0.0).astype(BF16)
    agg_two = (dot(inner, hidden) / inner_degree).astype(BF16)
    logits = dot(agg_two, cls[...], 1, 1)
    exponent = jnp.exp(logits - jnp.max(logits, axis=1, keepdims=True))
    softmax = exponent / jnp.sum(exponent, axis=1, keepdims=True)
    logit_grad = ((softmax - one_hot) / seeds).astype(BF16)
    widen = flag(iota((classes, CP), 0) == iota((classes, CP), 1))
    class_rows = dot(dot(logit_grad, widen).astype(BF16), agg_two, 0, 0).astype(BF16)
    for t in range(X):
        for cc in range(C):
            cs1[t * C + cc] = class_rows[:, cc * HH + t * cw:cc * HH + (t + 1) * cw]
    me_xc = x * C + c
    ex_c1 = along_xc(lambda t: cs1.at[t], lambda f: cr1.at[f], blocks(cr1, X * C), c1_ss, c1_rs)
    ex_c1.start()
    cr1[me_xc] = cs1[me_xc]

    agg_grad = dot(logit_grad, cls[...]) / inner_degree
    high = agg_grad.astype(BF16)
    low = (agg_grad - high.astype(F32)).astype(BF16)
    hidden_diff = dot(inner, high, 0, 0) + dot(inner, low, 0, 0)

    pg[...] = jnp.where(pre[...] > 0.0, hidden_diff, 0.0).astype(BF16)
    g0 = to_sibling(pg, pgr, g0_ss, g0_rs)
    g0.start()

    diff16 = hidden_diff.astype(BF16)
    xw = HID // X
    xh = xw // 2
    for t in range(X):
        na1s[t * Z:(t + 1) * Z] = diff16[:, t * xw:t * xw + xh].reshape(Z, Q * half, xh)
    ex_na1 = along_xz(lambda t: na1s.at[t], lambda f: na1r.at[f], blocks(na1r, X * Z), na1_ss, na1_rs)
    ex_na1.start()
    me_xz = x * Z + z
    na1r[me_xz] = na1s[me_xz]
    second = jnp.concatenate([diff16[:, t * xw + xh:(t + 1) * xw] for t in range(X)], axis=1)
    nb1s[...] = dot(swap_a[...], second).astype(BF16).reshape(nb1s.shape)
    ex_nb1 = along_q(lambda t: nb1s.at[t], lambda f: nb1r.at[f], blocks(nb1r, Q), nb1_ss, nb1_rs)
    ex_nb1.start()
    nb1r[q] = nb1s[q]

    def total(ref, n):
        acc = ref[0].astype(F32)
        for k in range(1, n):
            acc = acc + ref[k].astype(F32)
        return acc

    gmine = dot(pg[...], agg[c], 0, 0)
    ga.wait_recv()
    g0.wait_recv()
    gmine = (gmine + dot(pgr[...], agr[...], 0, 0)).astype(BF16).reshape(Z, X, YL * 16, DH)
    for t in range(X):
        gs1[t] = gmine[:, t]
    right, left, across = (lax.bitwise_and(x + d, X - 1) for d in (1, X - 1, 2))
    lower, upper = pl.ds(0, Z // 2), pl.ds(Z // 2, Z // 2)

    def g1(k, src, dst, to):
        return copy(src, dst, g1_ss.at[k], g1_rs.at[k], z, q, to)

    r1, l1 = g1(0, gs1.at[across, lower], gra, right), g1(1, gs1.at[across, upper], grb, left)
    r2, l2 = g1(2, gs1.at[right, upper], grl.at[upper], right), g1(3, gs1.at[left, lower], grr.at[lower], left)
    r3, l3 = g1(4, gsa, grl.at[lower], right), g1(5, gsb, grr.at[upper], left)
    for one in (r1, l1, r2, l2):
        one.start()

    ex_c1.recv()
    cs2[...] = total(cr1, X * C).astype(BF16).reshape(cs2.shape)

    def to_blocks(act):
        def step(t, carry):
            @pl.when(t != z)
            def _():
                act(t)
            return carry
        lax.fori_loop(0, nb, step, 0)

    to_blocks(lambda t: copy(cs2.at[t], cr2.at[z], c2_ss, c2_rs, t, q, x).start())
    summing = z < nb
    ex_c2 = along_z(None, None, blocks(cr2, Z), c2_ss, c2_rs)
    ex_c3 = along_y(lambda t: cs3, lambda f: cr3.at[f], blocks(cr3, Y), c3_ss, c3_rs)
    ex_c4 = along_z(lambda t: cfin, lambda f: ca4.at[f], blocks(cr2, Z), c4_ss, c4_rs)

    r1.wait_recv()
    gsa[...] = (gs1[right, lower].astype(F32) + gra[...].astype(F32)).astype(BF16)
    r3.start()
    l1.wait_recv()
    gsb[...] = (gs1[left, upper].astype(F32) + grb[...].astype(F32)).astype(BF16)
    l3.start()

    ex_na1.recv()
    came = jnp.concatenate([na1r[t * Z:(t + 1) * Z].reshape(hop, xh) for t in range(X)], axis=1)
    came = dot(swap_a[...], came).astype(BF16)
    for t in range(X):
        na2s[:, t] = came[:, t * xh:(t + 1) * xh].reshape(Q, Z * half, xh)
    ex_na2 = along_q(lambda t: na2s.at[t], lambda f: na2r.at[f], blocks(na2r, Q), na2_ss, na2_rs)
    ex_na2.start()
    na2r[q] = na2s[q]
    ex_nb1.recv()
    came = dot(swap_b[...], nb1r[...].reshape(hop, X * xh)).astype(BF16)
    for t in range(X):
        nb2s[t * Z:(t + 1) * Z] = came[:, t * xh:(t + 1) * xh].reshape(Z, Q * half, xh)
    ex_nb2 = along_xz(lambda t: nb2s.at[t], lambda f: nb2r.at[f], blocks(nb2r, X * Z), nb2_ss, nb2_rs)
    ex_nb2.start()
    nb2r[me_xz] = nb2s[me_xz]

    @pl.when(summing)
    def _():
        cr2[z] = cs2[z]
        ex_c2.recv()
        cs3[...] = total(cr2, Z).astype(BF16)
        ex_c3.start()
        cr3[y] = cs3[...]

    for one in (r2, l2, r3, l3):
        one.wait_recv()
    gs2[...] = (gs1[x].astype(F32) + grl[...].astype(F32) + grr[...].astype(F32)).astype(BF16)
    ex_g2 = along_z(lambda t: gs2.at[t], lambda f: gr2.at[f], blocks(gr2, Z), g2_ss, g2_rs)
    ex_g2.start()
    gr2[z] = gs2[z]

    @pl.when(summing)
    def _():
        ex_c3.recv()
        cfin[...] = total(cr3, Y).astype(BF16)
        ex_c4.start()
        ca4[z] = cfin[...]

    ex_g2.recv()
    gs3[...] = total(gr2, Z).astype(BF16).reshape(gs3.shape)

    def g3_copy(yl):
        return copy(gs3.at[yl], gr3.at[y], g3_ss.at[yl], g3_rs, z, (x * YL + yl) * C + c, x)

    for yl in range(YL):
        @pl.when(x * YL + yl != y)
        def _():
            g3_copy(yl).start()
    owning = y // YL == x

    @pl.when(summing)
    def _():
        some = ca4.at[pl.ds(0, nb - 1)]
        copy(some, some, c4_ss, c4_rs, z, q, x).wait_recv()

    @pl.when(jnp.logical_not(summing))
    def _():
        copy(ca4, ca4, c4_ss, c4_rs, z, q, x).wait_recv()

    ex_c5 = along_xc(lambda t: ca4, lambda f: ca5.at[f], blocks(ca5, X * C), c5_ss, c5_rs)
    ex_c5.start()
    ca5[me_xc] = ca4[...]

    ex_na2.recv()
    node_out[:, :xh] = dot(place_a[...], na2r[...].reshape(X * hop, xh)).astype(BF16)

    def g4_copy(xx, cc):
        return copy(gs4.at[cc], gr4.at[c], g4_ss.at[xx * C + cc], g4_rs.at[c], z, y * C + cc, xx)

    def g4_each(act):
        for xx in range(X):
            for cc in range(C):
                @pl.when(owning & jnp.logical_not((x == xx) & (c == cc)))
                def _():
                    act(xx, cc)

    @pl.when(owning)
    def _():
        gr3[y] = gs3[y % YL]
        copy(blocks(gr3, Y), blocks(gr3, Y), g3_ss.at[0], g3_rs, z, q, x).wait_recv()
        gs4[...] = total(gr3, Y).reshape(gs4.shape)
        gr4[c] = gs4[c]

    g4_each(lambda xx, cc: g4_copy(xx, cc).start())

    ex_nb2.recv()
    node_out[:, xh:] = dot(place_b[...], nb2r[...].reshape(X * hop, xh)).astype(BF16)

    ex_c5.recv()
    for t in range(X):
        for cc in range(C):
            class_out[:, cc * HH + t * cw:cc * HH + (t + 1) * cw] = ca5[t * C + cc].reshape(CP, cw)

    for cc in range(C):
        @pl.when(jnp.logical_not(owning & (c == cc)))
        def _():
            copy(gs4.at[0], gr4.at[cc], g4_ss.at[0], g4_rs.at[cc], z, y * C + cc, y // YL).wait_recv()
        hidden_out[:, cc * DH:(cc + 1) * DH] = gr4[cc]

    for ex in (ex_i1, ex_i2, ex_wx, ex_w2, ex_w3, *ex_fa1, *ex_fb1, *ex_fa2, *ex_fb2, ex_na1, ex_nb1, ex_na2, ex_nb2,
               ex_g2, ex_c1, ex_c5):
        ex.sent()
    w1_each(lambda t: w1_copy(t).wait_send())
    for one in (w4, ga, g0, r1, l1, r2, l2, r3, l3):
        one.wait_send()

    @pl.when(summing)
    def _():
        some = cs2.at[pl.ds(0, nb - 1)]
        copy(some, some, c2_ss, c2_rs, z, q, x).wait_send()
        ex_c3.sent()
        ex_c4.sent()

    @pl.when(jnp.logical_not(summing))
    def _():
        copy(cs2, cs2, c2_ss, c2_rs, z, q, x).wait_send()

    for yl in range(YL):
        @pl.when(x * YL + yl != y)
        def _():
            g3_copy(yl).wait_send()
    g4_each(lambda xx, cc: g4_copy(xx, cc).wait_send())


def on_device(
    grid, features, hidden_weight, class_weight, request_ids, request_counts,
    outer_tiles, outer_masks, inner_tiles, inner_masks, labels,
):
    Z, Y, C, X = grid
    Q = Y * C
    NO = Z * Q
    cap = request_ids.shape[1]
    half = cap // 2
    rows, D = features.shape
    classes, HID = class_weight.shape
    tile = outer_masks.shape[2]
    hop = NO * half
    DH, HH, YL = D // 2, HID // 2, Y // X
    cb = 32 if classes > 32 else 8
    nb = -(-classes // cb)
    CP, cw = nb * cb, HID // (C * X)
    LW = max(Z * 8, 128)
    dims = (Z, Y, C, X, cap, tile, rows, classes)
    vm, dma = pltpu.VMEM, pltpu.SemaphoreType.DMA
    xh, nk = HID // X // 2, DH // 128
    scratch = [
        vm(features.shape, BF16), vm(outer_masks.shape, jnp.int32), vm(inner_masks.shape, jnp.int32),
        vm(class_weight.shape, BF16),
        vm((8, NO), F32), vm((Z, 8, NO), F32), vm((Q, 8, LW), F32), vm((Q, 8, LW), F32),
        vm((X, Q * 8, LW), BF16), vm((rows, X * hop), BF16), vm((rows, X * hop), BF16),
        vm((16, DH), BF16), vm((C, 16, DH), BF16), vm((Z, X, C, 16, D), BF16),
        *[vm((nk, Z, cap * Q, DH // nk), BF16)] * 2, *[vm((nk, Q, cap * Z, DH // nk), BF16)] * 2,
        *[vm((nk, Q, cap * Z, DH // nk), BF16)] * 2, *[vm((nk, Z, cap * Q, DH // nk), BF16)] * 2,
        vm((cap * NO, cap * NO), BF16), vm((cap * NO, cap * NO), BF16), vm((hop, hop), BF16), vm((hop, hop), BF16),
        vm((2, hop, DH), BF16), vm((hop, DH), BF16), vm((hop, HID), F32), vm((hop, HID), BF16), vm((hop, HID), BF16),
        vm((X * Z, Q * half, xh), BF16), vm((X * Z, Q * half, xh), BF16),
        vm((Q, X, Z * half, xh), BF16), vm((Q, X, Z * half, xh), BF16),
        vm((Q, Z * half, HH), BF16), vm((Q, Z * half, HH), BF16),
        vm((X * Z, Q * half, xh), BF16), vm((X * Z, Q * half, xh), BF16),
        vm((X, Z, YL * 16, DH), BF16), *[vm((Z // 2, YL * 16, DH), BF16)] * 4, *[vm((Z, YL * 16, DH), BF16)] * 2,
        vm((Z, YL * 16, DH), BF16), vm((Z, YL * 16, DH), BF16),
        vm((YL, 16, DH), BF16), vm((Y, 16, DH), BF16), vm((C, 8, DH), F32), vm((C, 8, DH), F32),
        vm((X * C, CP, cw), BF16), vm((X * C, CP, cw), BF16), vm((nb, cb, cw), BF16), vm((Z, cb, cw), BF16),
        vm((cb, cw), BF16), vm((Y, cb, cw), BF16), vm((cb, cw), BF16), vm((nb, cb, cw), BF16),
        vm((X * C, nb, cb, cw), BF16),
        dma((4,)),
        *[dma] * 6,
        dma((Y,)), dma((C,)), *[dma] * 6,
        *[dma((nk,))] * 8, *[dma] * 8,
        *[dma] * 4, dma((6,)), dma((6,)), dma, dma, dma((YL,)), dma, dma((X * C,)), dma((C,)),
        *[dma] * 10,
    ]
    hbm = pl.BlockSpec(memory_space=pl.ANY)
    vmem = pl.BlockSpec(memory_space=pltpu.VMEM)
    smem = pl.BlockSpec(memory_space=pltpu.SMEM)
    hidden_grad, class_grad, node_grad = pl.pallas_call(
        functools.partial(kernel, dims),
        out_shape=(
            jax.ShapeDtypeStruct(hidden_weight.shape, F32),
            jax.ShapeDtypeStruct((CP, HID), BF16),
            jax.ShapeDtypeStruct((rows, HID // X), BF16),
        ),
        in_specs=[hbm, vmem, hbm, vmem, vmem, smem, hbm, smem, hbm, vmem],
        out_specs=(vmem, vmem, vmem),
        scratch_shapes=scratch,
        compiler_params=pltpu.CompilerParams(
            collective_id=0, has_side_effects=True, vmem_limit_bytes=56 * 1024 * 1024
        ),
        cost_estimate=pl.CostEstimate(flops=2_000_000_000, bytes_accessed=3_000_000, transcendentals=20_000),
    )(
        features, hidden_weight, class_weight, request_ids.T, request_counts.T,
        outer_tiles, outer_masks, inner_tiles, inner_masks, labels.reshape(1, -1),
    )
    return hidden_grad, class_grad[:classes].astype(F32), node_grad


def solution(mesh):
    grid = GRIDS[(mesh.shape["owner"], mesh.shape["rep"])]
    placed = (
        P("owner", None),
        P("owner", None),
        P(),
        P(("owner", "rep"), None),
        P(("owner", "rep"), None),
        P(("owner", "rep"), None),
        P(("owner", "rep"), None, None, None),
        P(("owner", "rep"), None),
        P(("owner", "rep"), None, None, None),
        P(("owner", "rep")),
    )
    return jax.shard_map(
        functools.partial(on_device, grid),
        mesh=mesh,
        in_specs=placed,
        out_specs=(P("owner", None), P(), P("owner", "rep")),
        check_vma=False,
    )
```

```python
import functools

import jax
import jax.numpy as jnp
from jax import lax
from jax.experimental import pallas as pl
from jax.experimental.pallas import tpu as pltpu
from jax.sharding import PartitionSpec as P

MESH = pl.DeviceIdType.MESH
F32 = jnp.float32
BF16 = jnp.bfloat16

GRIDS = {(128, 4): (8, 8, 2, 4), (32, 4): (2, 8, 2, 4)}


def iota(shape, dim):
    return lax.broadcasted_iota(jnp.int32, shape, dim)


def quo(a, n):
    return lax.shift_right_logical(a, jnp.full_like(a, n.bit_length() - 1))


def rem(a, n):
    return lax.bitwise_and(a, jnp.full_like(a, n - 1))


def flag(cond, dtype=BF16):
    return jnp.where(cond, 1.0, 0.0).astype(F32).astype(dtype)


def dot(a, b, ca=1, cb=0):
    return lax.dot_general(a, b, (((ca,), (cb,)), ((), ())), preferred_element_type=F32)


def regroup(outer, middle, inner, transpose=False):
    n = outer * middle * inner
    o, i = iota((n, n), 0), iota((n, n), 1)
    if transpose:
        o, i = i, o
    m, rest = quo(o, outer * inner), rem(o, outer * inner)
    a, b = quo(rest, inner), rem(rest, inner)
    return flag(i == a * (middle * inner) + m * inner + b)


def kernel(
    dims,
    feat_hbm, weight_hbm, cls_hbm, ids_hbm, counts_hbm, otile_ref, omask_hbm, itile_ref, imask_hbm, labels_hbm,
    hidden_out, class_out, node_out,
    feat, omask, imask, cls, weight_ref, ids_ref, counts_ref, labels_ref,
    i1s, i1r, i2s, i2r, wx, place_a, place_b,
    ws, wr, w_all,
    fa1s, fa1r, fa2s, fa2r, fb1s, fb1r, fb2s, fb2r, move_a, move_b, swap_a, swap_b,
    agg, agr, pre, pgt, pgtr, diff,
    na1s, na1r, na2s, na2r, nb1s, nb1r, nb2s, nb2r,
    gs1, gra, grb, gsa, gsb, grl, grr, gs2, gr2, gs3, gr3, gs4, gr4,
    cs1, cr1, cs2, cr2, cs3, cr3, cfin, ca4, ca5,
    local_sem,
    i1_ss, i1_rs, i2_ss, i2_rs, wx_ss, wx_rs,
    w1_ss, w1_rs, w2_ss, w2_rs, w3_ss, w3_rs, w4_ss, w4_rs,
    fa1_ss, fa1_rs, fa2_ss, fa2_rs, fb1_ss, fb1_rs, fb2_ss, fb2_rs,
    na1_ss, na1_rs, na2_ss, na2_rs, nb1_ss, nb1_rs, nb2_ss, nb2_rs,
    ga_ss, ga_rs, g0_ss, g0_rs, g1_ss, g1_rs, g2_ss, g2_rs, g3_ss, g3_rs, g4_ss, g4_rs,
    c1_ss, c1_rs, c2_ss, c2_rs, c3_ss, c3_rs, c4_ss, c4_rs, c5_ss, c5_rs,
):
    Z, Y, C, X, cap, tile, rows, classes = dims
    Q = Y * C
    NO = Z * Q
    half = cap // 2
    hop, front = NO * half, NO * cap
    D, HID = feat.shape[1], pre.shape[1]
    DH, HH = D // 2, HID // 2
    YL = Y // X
    nb, cb, cw = cs2.shape
    CP = nb * cb
    seeds = labels_ref.shape[1]
    row_blocks, col_blocks, K = hop // tile, front // tile, otile_ref.shape[1]
    LW = i2s.shape[2]
    S8 = 8

    me_o = lax.axis_index("owner")
    x = lax.axis_index("rep")
    z = me_o // Q
    q = me_o % Q
    y = q // C
    c = q % C
    sib = C - 1 - c

    def copy(src, dst, ss, rs, zz, qq, xx):
        return pltpu.make_async_remote_copy(
            src_ref=src, dst_ref=dst, send_sem=ss, recv_sem=rs,
            device_id=(zz * Q + qq, xx), device_id_type=MESH,
        )

    def each(n, body):
        def step(i, carry):
            body(i)
            return carry
        lax.fori_loop(1, n, step, 0)

    class Exchange:
        def __init__(self, n, me, at, src, dst, bulk, ss, rs):
            self.n, self.me, self.at, self.src, self.dst, self.bulk, self.ss, self.rs = n, me, at, src, dst, bulk, ss, rs

        def start(self):
            def send(d):
                to = lax.bitwise_and(self.me + d, self.n - 1)
                copy(self.src(to), self.dst(self.me), self.ss, self.rs, *self.at(to)).start()
            each(self.n, send)

        def all(self):
            return copy(self.bulk, self.bulk, self.ss, self.rs, *self.at(lax.bitwise_and(self.me + 1, self.n - 1)))

        def recv(self):
            self.all().wait_recv()

        def sent(self):
            self.all().wait_send()

    def along_z(*rest):
        return Exchange(Z, z, lambda t: (t, q, x), *rest)

    def along_q(*rest):
        return Exchange(Q, q, lambda t: (z, t, x), *rest)

    def along_y(*rest):
        return Exchange(Y, y, lambda t: (z, t * C + c, x), *rest)

    def along_x(*rest):
        return Exchange(X, x, lambda t: (z, q, t), *rest)

    def along_xz(*rest):
        return Exchange(X * Z, x * Z + z, lambda t: (lax.bitwise_and(t, Z - 1), q, t // Z), *rest)

    def along_xc(*rest):
        return Exchange(X * C, x * C + c, lambda t: (z, y * C + lax.bitwise_and(t, C - 1), t // C), *rest)

    def blocks(ref, n):
        return ref.at[pl.ds(0, n - 1)]

    def to_sibling(src, dst, ss, rs):
        return copy(src, dst, ss, rs, z, y * C + sib, x)

    staged = (
        (ids_hbm, ids_ref), (weight_hbm, weight_ref), (feat_hbm, feat), (counts_hbm, counts_ref),
        (omask_hbm, omask), (imask_hbm, imask), (labels_hbm, labels_ref), (cls_hbm, cls),
    )
    loads = [pltpu.make_async_copy(src, dst, local_sem.at[k]) for k, (src, dst) in enumerate(staged)]
    for load in loads:
        load.start()

    barrier = pltpu.get_barrier_semaphore()

    def greet(zz, qq, xx):
        pl.semaphore_signal(barrier, inc=1, device_id=(zz * Q + qq, xx), device_id_type=MESH)

    def greet_xz(d):
        t = lax.bitwise_and(x * Z + z + d, X * Z - 1)
        greet(lax.bitwise_and(t, Z - 1), q, t // Z)

    each(Q, lambda d: greet(z, lax.bitwise_and(q + d, Q - 1), x))
    each(X * Z, greet_xz)
    each(X, lambda d: greet(z, y * C + sib, lax.bitwise_and(x + d, X - 1)))

    i1s[...] = jnp.zeros_like(i1s)
    for load in loads[:2]:
        load.wait()
    i1s[0:cap, :] = ids_ref[...].astype(F32)
    w32 = weight_ref[...].astype(F32)
    ws[...] = jnp.concatenate([w32[:, :DH], w32[:, DH:]], axis=0).astype(BF16)

    pl.semaphore_wait(barrier, (Q - 1) + (X * Z - 1) + (X - 1))

    ex_i1 = along_z(lambda t: i1s, lambda f: i1r.at[f], blocks(i1r, Z), i1_ss, i1_rs)
    ex_i1.start()
    i1r[z] = i1s[...]

    w_core = y % C

    def w1_copy(t):
        return copy(ws, wr.at[c], w1_ss.at[t], w1_rs.at[c], z, t * C + w_core, x)

    def w1_each(act):
        def step(t, carry):
            @pl.when((y // C == x) & jnp.logical_not((t == y) & (w_core == c)))
            def _():
                act(t)
            return carry
        lax.fori_loop(0, Y, step, 0)

    w1_each(lambda t: w1_copy(t).start())
    y_mine = x * C + c

    ex_i1.recv()
    marks = flag(iota((Q, NO), 1) == z * Q + iota((Q, NO), 0))
    asked = i1r[...].reshape(Z * S8, NO).astype(BF16)
    if LW > Z * S8:
        asked = jnp.concatenate([asked] * (LW // (Z * S8)), axis=0)
    for_q = dot(marks, asked, 1, 1)
    for k in range(Q):
        i2s[k] = jnp.broadcast_to(for_q[k:k + 1, :], (8, LW))
    ex_i2 = along_q(lambda t: i2s.at[t], lambda f: i2r.at[f], blocks(i2r, Q), i2_ss, i2_rs)
    ex_i2.start()
    i2r[q] = i2s[q]

    for c0 in range(C):
        own = (y == y_mine) & (c == c0)

        @pl.when(own)
        def _():
            wr[c0] = ws[...]

        @pl.when(jnp.logical_not(own))
        def _():
            copy(ws, wr.at[c0], w1_ss.at[0], w1_rs.at[c0], z, y_mine * C + c0, x).wait_recv()
    for hcol in range(2):
        cols = slice(hcol * DH, (hcol + 1) * DH)
        w_all[z, x, c, :, cols] = jnp.concatenate(
            [wr[c0, hcol * 8:(hcol + 1) * 8, :].astype(F32) for c0 in range(C)], axis=0
        ).astype(BF16)
    ex_w2 = along_z(
        lambda t: w_all.at[z, x, c], lambda f: w_all.at[f, x, c], w_all.at[pl.ds(0, Z - 1), x, c], w2_ss, w2_rs
    )
    ex_w2.start()

    loads[2].wait()
    lane_q = iota((front, Q * 8), 1)

    ex_i2.recv()
    wanted = i2r[...].reshape(Q * 8, LW).astype(BF16)

    wx[x] = wanted
    ex_wx = along_x(lambda t: wx.at[x], lambda f: wx.at[f], blocks(wx, X), wx_ss, wx_rs)

    def picked(col_of, q_of):
        spread = dot(flag(iota((front, LW), 1) == col_of), wanted, 1, 1)
        ids = jnp.sum(jnp.where(lane_q == q_of * 8, spread, 0.0), axis=1, keepdims=True)
        return flag(ids == iota((front, rows), 1).astype(F32))

    chunks, wide = fa1s.shape[0], fa1s.shape[3]
    r = iota((front, 1), 0)
    pick_a = picked(quo(r, cap * Q) * S8 + quo(rem(r, cap * Q), Q), rem(r, Q))

    def column_blocks(first):
        return jnp.concatenate([feat[:, b * wide:(b + 1) * wide] for b in range(first, 2 * chunks, 2)], axis=1)

    rows_a = dot(pick_a, column_blocks(0)).astype(BF16)
    ex_fa1, ex_fb1, ex_fa2, ex_fb2 = [], [], [], []
    for k in range(chunks):
        at = slice(k * wide, (k + 1) * wide)
        fa1s[k] = rows_a[:, at].reshape(fa1s.shape[1:])
        ex_fa1.append(along_z(
            lambda t, k=k: fa1s.at[k, t], lambda f, k=k: fa1r.at[k, f], blocks(fa1r.at[k], Z), fa1_ss.at[k], fa1_rs.at[k]))
        ex_fb1.append(along_q(
            lambda t, k=k: fb1s.at[k, t], lambda f, k=k: fb1r.at[k, f], blocks(fb1r.at[k], Q), fb1_ss.at[k], fb1_rs.at[k]))
        ex_fa2.append(along_q(
            lambda t, k=k: fa2s.at[k, t], lambda f, k=k: fa2r.at[k, f], blocks(fa2r.at[k], Q), fa2_ss.at[k], fa2_rs.at[k]))
        ex_fb2.append(along_z(
            lambda t, k=k: fb2s.at[k, t], lambda f, k=k: fb2r.at[k, f], blocks(fb2r.at[k], Z), fb2_ss.at[k], fb2_rs.at[k]))
    ex_fa1[0].start()
    pick_b = picked(rem(r, Z) * S8 + quo(rem(r, cap * Z), Z), quo(r, cap * Z))
    rows_b = dot(pick_b, column_blocks(1)).astype(BF16)
    for k in range(chunks):
        at = slice(k * wide, (k + 1) * wide)
        fb1s[k] = rows_b[:, at].reshape(fb1s.shape[1:])
    ex_fb1[0].start()
    for k in range(1, chunks):
        ex_fa1[k].start()
        ex_fb1[k].start()
    for k in range(chunks):
        fa1r[k, z] = fa1s[k, z]
        fb1r[k, q] = fb1s[k, q]
    ex_wx.start()
    move_a[...] = regroup(Z * cap, Q, 1)
    move_b[...] = regroup(Q * cap, Z, 1)

    ex_w2.recv()
    ex_w3 = along_x(
        lambda t: w_all.at[:, x, c], lambda f: w_all.at[:, f, c], w_all.at[:, pl.ds(0, X - 1), c], w3_ss, w3_rs
    )
    ex_w3.start()

    for load in loads[3:]:
        load.wait()
    counts = counts_ref[...].astype(F32)
    counts8 = jnp.concatenate([counts, jnp.zeros((6, NO), F32)], axis=0).astype(BF16)

    def validity(slots):
        n = NO * slots
        at = iota((NO, n), 1)
        per = dot(counts8, flag(iota((NO, n), 0) == quo(at, slots)))
        j = rem(iota((1, n), 1), slots).astype(F32)
        first = flag(j < per[0:1, :], F32)
        second = flag(j - half < per[1:2, :], F32)
        return jnp.where(j < half, first, second)

    valid = validity(cap)
    outer_rows = []
    for b in range(row_blocks):
        tiles = []
        for cbk in range(col_blocks):
            m = jnp.zeros((tile, tile), jnp.int32)
            for k in range(K):
                m = m + omask[b, k] * (otile_ref[b, k] == cbk).astype(jnp.int32)
            tiles.append(m.astype(F32) * valid[:, cbk * tile:(cbk + 1) * tile])
        outer_rows.append(jnp.concatenate(tiles, axis=1))
    outer = jnp.concatenate(outer_rows, axis=0)
    outer_scale = 1.0 + jnp.sum(outer, axis=1, keepdims=True)
    oi, oc = iota((hop, front), 0), iota((hop, front), 1)
    self_col = quo(oi, half) * cap + rem(oi, half)
    outer_self = (outer + flag(oc == self_col, F32)).astype(BF16)
    outer_a = dot(outer_self, regroup(Z, Q, cap, transpose=True)).astype(BF16)

    hop_valid = validity(half)
    tiles = []
    for cbk in range(row_blocks):
        m = jnp.zeros((tile, tile), jnp.int32)
        for k in range(K):
            m = m + imask[0, k] * (itile_ref[0, k] == cbk).astype(jnp.int32)
        tiles.append(m.astype(F32) * hop_valid[:, cbk * tile:(cbk + 1) * tile])
    inner32 = jnp.concatenate(tiles, axis=1)
    inner_degree = jnp.maximum(jnp.sum(inner32, axis=1, keepdims=True), 1.0)
    inner = inner32.astype(BF16)
    inner_twice = jnp.concatenate([inner32.T, inner32.T], axis=1).astype(BF16)

    label_row = labels_ref[...]
    label_col = jnp.sum(
        jnp.where(iota((seeds, seeds), 0) == iota((seeds, seeds), 1), label_row, 0), axis=1, keepdims=True
    )
    one_hot = flag(label_col == iota((seeds, classes), 1), F32)

    for k in range(chunks):
        ex_fa1[k].recv()
        fa2s[k] = dot(move_a[...], fa1r[k].reshape(front, wide)).astype(BF16).reshape(fa2s.shape[1:])
        ex_fa2[k].start()
        fa2r[k, q] = fa2s[k, q]
        ex_fb1[k].recv()
        fb2s[k] = dot(move_b[...], fb1r[k].reshape(front, wide)).astype(BF16).reshape(fb2s.shape[1:])
        ex_fb2[k].start()
        fb2r[k, z] = fb2s[k, z]

    ex_w3.recv()
    w4 = to_sibling(w_all.at[:, :, c], w_all.at[:, :, c], w4_ss, w4_rs)
    w4_in = to_sibling(w_all.at[:, :, sib], w_all.at[:, :, sib], w4_ss, w4_rs)
    w4.start()

    swap_a[...] = regroup(Z, Q, half)
    swap_b[...] = regroup(Q, Z, half)
    ex_wx.recv()

    def places(x_of, j_of, z_of, q_of):
        n = X * hop
        pick = flag(iota((LW, n), 0) == z_of * S8 + j_of)
        ids = jnp.zeros((1, n), F32)
        for k in range(X):
            here = (iota((Q * 8, n), 0) == q_of * 8) & (x_of == k)
            ids = ids + jnp.sum(jnp.where(here, dot(wx[k], pick), 0.0), axis=0, keepdims=True)
        return flag(iota((rows, n), 0).astype(F32) == ids)

    s = iota((1, X * hop), 1)
    def plane(d):
        return lax.bitwise_and(x + X - d, jnp.full_like(d, X - 1))

    place_a[...] = places(
        plane(quo(s, half * Z * 2 * Q) * 2 + rem(quo(s, half * Z), 2)),
        rem(s, half), rem(quo(s, half), Z), rem(quo(s, half * Z * 2), Q)
    )
    place_b[...] = places(
        plane(quo(s, half * Q * Z)), rem(s, half), rem(quo(s, half * Q), Z), rem(quo(s, half), Q)
    )

    for k in range(chunks):
        ex_fa2[k].recv()
        part_a = (dot(outer_a, fa2r[k].reshape(front, wide)) / outer_scale).astype(BF16)
        ex_fb2[k].recv()
        part_b = (dot(outer_self, fb2r[k].reshape(front, wide)) / outer_scale).astype(BF16)
        for b, part in ((2 * k, part_a), (2 * k + 1, part_b)):
            agg[b // chunks, :, (b % chunks) * wide:(b % chunks + 1) * wide] = part
        if k == 0:
            w4_in.wait_recv()
        part = dot(
            jnp.concatenate([part_a, part_b], axis=1),
            w_all[:, :, :, :, 2 * k * wide:2 * (k + 1) * wide].reshape(HID, 2 * wide), 1, 1)
        pre[...] = part if k == 0 else pre[...] + part
    ga = to_sibling(agg.at[sib], agr, ga_ss, ga_rs)
    ga.start()

    hidden = jnp.maximum(pre[...], 0.0).astype(BF16)
    agg_two = (dot(inner, hidden) / inner_degree).astype(BF16)
    logits = dot(agg_two, cls[...], 1, 1)
    exponent = jnp.exp(logits - jnp.max(logits, axis=1, keepdims=True))
    softmax = exponent / jnp.sum(exponent, axis=1, keepdims=True)
    logit_grad = ((softmax - one_hot) / seeds).astype(BF16)
    widen = flag(iota((classes, CP), 0) == iota((classes, CP), 1))
    class_rows = dot(dot(logit_grad, widen).astype(BF16), agg_two, 0, 0).astype(BF16)
    for t in range(X):
        for cc in range(C):
            cs1[t * C + cc] = class_rows[:, cc * HH + t * cw:cc * HH + (t + 1) * cw]
    me_xc = x * C + c
    ex_c1 = along_xc(lambda t: cs1.at[t], lambda f: cr1.at[f], blocks(cr1, X * C), c1_ss, c1_rs)
    ex_c1.start()
    cr1[me_xc] = cs1[me_xc]

    agg_grad = dot(logit_grad, cls[...]) / inner_degree
    high = agg_grad.astype(BF16)
    low = (agg_grad - high.astype(F32)).astype(BF16)
    hidden_diff = dot(inner_twice, jnp.concatenate([high, low], axis=0))
    pgt[...] = jnp.where(pre[...] > 0.0, hidden_diff, 0.0).T.astype(BF16)
    g0 = to_sibling(pgt, pgtr, g0_ss, g0_rs)
    g0.start()

    diff[...] = hidden_diff.astype(BF16)
    xw = HID // X
    xh = xw // 2
    pair = 2 * Z

    def xz_leg(group, src, dst, ss, rs):
        def step(t, carry):
            d, zz = 2 * group + t // Z, lax.bitwise_and(z + t, Z - 1)
            copy(src(d, zz), dst.at[d * Z + z], ss, rs, zz, q, lax.bitwise_and(x + d, X - 1)).start()
            return carry
        lax.fori_loop(0 if group else 1, pair, step, 0)

    def wait_blocks(ref, n, ss, rs):
        some = ref.at[pl.ds(0, n)]
        return copy(some, some, ss, rs, z, q, lax.bitwise_and(x + 1, X - 1))

    for t in range(X):
        na1s[t * Z:(t + 1) * Z] = diff[:, t * xw:t * xw + xh].reshape(Z, Q * half, xh)
    for d in range(X):
        cols = pl.ds(pl.multiple_of(lax.bitwise_and(x + d, X - 1) * xw + xh, xh), xh)
        nb1s[d // 2, :, :, (d % 2) * xh:(d % 2 + 1) * xh] = (
            dot(swap_a[...], diff[:, cols]).astype(BF16).reshape(Q, Z * half, xh))
    ex_nb1 = [
        along_q(lambda t, g=g: nb1s.at[g, t], lambda f, g=g: nb1r.at[g, f], blocks(nb1r.at[g], Q), nb1_ss.at[g], nb1_rs.at[g])
        for g in range(2)
    ]
    ex_na2 = [
        along_q(lambda t, g=g: na2s.at[g, t], lambda f, g=g: na2r.at[g, f], blocks(na2r.at[g], Q), na2_ss.at[g], na2_rs.at[g])
        for g in range(2)
    ]
    for g in range(2):
        xz_leg(g, lambda d, zz: na1s.at[lax.bitwise_and(x + d, X - 1) * Z + zz], na1r, na1_ss.at[g], na1_rs.at[g])
        ex_nb1[g].start()
        nb1r[g, q] = nb1s[g, q]
    na1r[z] = na1s[x * Z + z]

    def total(ref, n):
        acc = ref[0].astype(F32)
        for k in range(1, n):
            acc = acc + ref[k].astype(F32)
        return acc

    gmine = dot(pgt[...], agg[c])
    ga.wait_recv()
    g0.wait_recv()
    gmine = (gmine + dot(pgtr[...], agr[...])).astype(BF16).reshape(Z, X, YL * 16, DH)
    for k in range(chunks):
        for t in range(X):
            gs1[k, t] = gmine[:, t, :, k * wide:(k + 1) * wide]
    right, left, across = (lax.bitwise_and(x + d, X - 1) for d in (1, X - 1, 2))
    lower, upper = pl.ds(0, Z // 2), pl.ds(Z // 2, Z // 2)

    def g1(k, n, src, dst, to):
        return copy(src, dst, g1_ss.at[k, n], g1_rs.at[k, n], z, q, to)

    ring = [(
        g1(k, 0, gs1.at[k, across, lower], gra.at[k], right), g1(k, 1, gs1.at[k, across, upper], grb.at[k], left),
        g1(k, 2, gs1.at[k, right, upper], grl.at[k, upper], right), g1(k, 3, gs1.at[k, left, lower], grr.at[k, lower], left),
        g1(k, 4, gsa.at[k], grl.at[k, lower], right), g1(k, 5, gsb.at[k], grr.at[k, upper], left),
    ) for k in range(chunks)]
    for k in range(chunks):
        for one in ring[k][:4]:
            one.start()

    ex_c1.recv()
    cs2[...] = total(cr1, X * C).astype(BF16).reshape(cs2.shape)

    def to_blocks(act):
        def step(t, carry):
            @pl.when(t != y)
            def _():
                act(t)
            return carry
        lax.fori_loop(0, nb, step, 0)

    to_blocks(lambda t: copy(cs2.at[t], cr2.at[y], c2_ss, c2_rs, z, t * C + c, x).start())
    summing = y < nb
    ex_c2 = along_y(None, None, blocks(cr2, Y), c2_ss, c2_rs)
    ex_c3 = along_z(lambda t: cs3, lambda f: cr3.at[f], blocks(cr3, Z), c3_ss, c3_rs)
    ex_c4 = along_y(lambda t: cfin, lambda f: ca4.at[f], blocks(cr2, Y), c4_ss, c4_rs)

    for k in range(chunks):
        r1, l1, r2, l2, r3, l3 = ring[k]
        r1.wait_recv()
        gsa[k] = (gs1[k, right, lower].astype(F32) + gra[k].astype(F32)).astype(BF16)
        r3.start()
        l1.wait_recv()
        gsb[k] = (gs1[k, left, upper].astype(F32) + grb[k].astype(F32)).astype(BF16)
        l3.start()

    for g in range(2):
        wait_blocks(na1r, pair if g else pair - 1, na1_ss.at[g], na1_rs.at[g]).wait_recv()
        came = jnp.concatenate([na1r[d * Z:(d + 1) * Z].reshape(hop, xh) for d in (2 * g, 2 * g + 1)], axis=1)
        came = dot(swap_a[...], came).astype(BF16)
        for t in range(2):
            na2s[g, :, t] = came[:, t * xh:(t + 1) * xh].reshape(Q, Z * half, xh)
        ex_na2[g].start()
        na2r[g, q] = na2s[g, q]
        ex_nb1[g].recv()
        came = dot(swap_b[...], nb1r[g].reshape(hop, 2 * xh)).astype(BF16)
        for t in range(2):
            nb2s[(2 * g + t) * Z:(2 * g + t + 1) * Z] = came[:, t * xh:(t + 1) * xh].reshape(Z, Q * half, xh)
        xz_leg(g, lambda d, zz: nb2s.at[d * Z + zz], nb2r, nb2_ss, nb2_rs)
    nb2r[z] = nb2s[z]

    @pl.when(summing)
    def _():
        cr2[y] = cs2[y]
        ex_c2.recv()
        cs3[...] = total(cr2, Y).astype(BF16)
        ex_c3.start()
        cr3[z] = cs3[...]

    ex_g2 = []
    for k in range(chunks):
        for one in ring[k][2:]:
            one.wait_recv()
        gs2[k] = (gs1[k, x].astype(F32) + grl[k].astype(F32) + grr[k].astype(F32)).astype(BF16)
        ex_g2.append(along_z(
            lambda t, k=k: gs2.at[k, t], lambda f, k=k: gr2.at[k, f], blocks(gr2.at[k], Z), g2_ss.at[k], g2_rs.at[k]))
        ex_g2[k].start()
        gr2[k, z] = gs2[k, z]

    @pl.when(summing)
    def _():
        ex_c3.recv()
        cfin[...] = total(cr3, Z).astype(BF16)
        ex_c4.start()
        ca4[y] = cfin[...]

    for k in range(chunks):
        ex_g2[k].recv()
        gs3[:, :, k * wide:(k + 1) * wide] = total(gr2.at[k], Z).astype(BF16).reshape(YL, 16, wide)

    def g3_copy(yl):
        return copy(gs3.at[yl], gr3.at[y], g3_ss.at[yl], g3_rs, z, (x * YL + yl) * C + c, x)

    for yl in range(YL):
        @pl.when(x * YL + yl != y)
        def _():
            g3_copy(yl).start()
    owning = y // YL == x

    @pl.when(summing)
    def _():
        some = ca4.at[pl.ds(0, nb - 1)]
        copy(some, some, c4_ss, c4_rs, z, q, x).wait_recv()

    @pl.when(jnp.logical_not(summing))
    def _():
        copy(ca4, ca4, c4_ss, c4_rs, z, q, x).wait_recv()

    ex_c5 = along_xc(lambda t: ca4, lambda f: ca5.at[f], blocks(ca5, X * C), c5_ss, c5_rs)
    ex_c5.start()
    ca5[me_xc] = ca4[...]

    for g in range(2):
        ex_na2[g].recv()
    node_out[:, :xh] = dot(place_a[...], na2r[...].reshape(X * hop, xh)).astype(BF16)

    def g4_copy(xx, cc):
        return copy(gs4.at[cc], gr4.at[c], g4_ss.at[xx * C + cc], g4_rs.at[c], z, y * C + cc, xx)

    def g4_each(act):
        for xx in range(X):
            for cc in range(C):
                @pl.when(owning & jnp.logical_not((x == xx) & (c == cc)))
                def _():
                    act(xx, cc)

    @pl.when(owning)
    def _():
        gr3[y] = gs3[y % YL]
        copy(blocks(gr3, Y), blocks(gr3, Y), g3_ss.at[0], g3_rs, z, q, x).wait_recv()
        gs4[...] = total(gr3, Y).reshape(gs4.shape)
        gr4[c] = gs4[c]

    g4_each(lambda xx, cc: g4_copy(xx, cc).start())

    wait_blocks(nb2r, 2 * pair - 1, nb2_ss, nb2_rs).wait_recv()
    node_out[:, xh:] = dot(place_b[...], nb2r[...].reshape(X * hop, xh)).astype(BF16)

    ex_c5.recv()
    class_out[...] = ca5[...].reshape(class_out.shape)

    for cc in range(C):
        @pl.when(jnp.logical_not(owning & (c == cc)))
        def _():
            copy(gs4.at[0], gr4.at[cc], g4_ss.at[0], g4_rs.at[cc], z, y * C + cc, y // YL).wait_recv()
        hidden_out[:, cc * DH:(cc + 1) * DH] = gr4[cc]

    for ex in (ex_i1, ex_i2, ex_wx, ex_w2, ex_w3, *ex_fa1, *ex_fb1, *ex_fa2, *ex_fb2, *ex_nb1, *ex_na2, *ex_g2, ex_c1, ex_c5):
        ex.sent()
    w1_each(lambda t: w1_copy(t).wait_send())
    for one in (w4, ga, g0, *[leg for legs in ring for leg in legs]):
        one.wait_send()
    for g in range(2):
        wait_blocks(na1r, pair if g else pair - 1, na1_ss.at[g], na1_rs.at[g]).wait_send()
    wait_blocks(nb2r, 2 * pair - 1, nb2_ss, nb2_rs).wait_send()

    @pl.when(summing)
    def _():
        some = cs2.at[pl.ds(0, nb - 1)]
        copy(some, some, c2_ss, c2_rs, z, q, x).wait_send()
        ex_c3.sent()
        ex_c4.sent()

    @pl.when(jnp.logical_not(summing))
    def _():
        copy(cs2, cs2, c2_ss, c2_rs, z, q, x).wait_send()

    for yl in range(YL):
        @pl.when(x * YL + yl != y)
        def _():
            g3_copy(yl).wait_send()
    g4_each(lambda xx, cc: g4_copy(xx, cc).wait_send())


def finish(class_dims, hidden_in, class_in, node_in, hidden_out, class_out, node_out, parts, spread, sem):
    X, C, classes = class_dims
    passed = [
        pltpu.make_async_copy(class_in, parts, sem.at[0]),
        pltpu.make_async_copy(hidden_in, hidden_out, sem.at[1]),
        pltpu.make_async_copy(node_in, node_out, sem.at[2]),
    ]
    for one in passed:
        one.start()
    passed[0].wait()
    cw = parts.shape[2]
    for t in range(X):
        for c in range(C):
            at = (c * X + t) * cw
            spread[:, at:at + cw] = parts[t * C + c].astype(F32)[:classes]
    last = pltpu.make_async_copy(spread, class_out, sem.at[3])
    last.start()
    for one in passed[1:]:
        one.wait()
    last.wait()


def on_device(
    grid, features, hidden_weight, class_weight, request_ids, request_counts,
    outer_tiles, outer_masks, inner_tiles, inner_masks, labels,
):
    Z, Y, C, X = grid
    Q = Y * C
    NO = Z * Q
    cap = request_ids.shape[1]
    half = cap // 2
    rows, D = features.shape
    classes, HID = class_weight.shape
    tile = outer_masks.shape[2]
    hop = NO * half
    DH, HH, YL = D // 2, HID // 2, Y // X
    cb = 32 if classes > 32 else 8
    nb = -(-classes // cb)
    CP, cw = nb * cb, HID // (C * X)
    LW = max(Z * 8, 128)
    dims = (Z, Y, C, X, cap, tile, rows, classes)
    vm, dma = pltpu.VMEM, pltpu.SemaphoreType.DMA
    xh, nk = HID // X // 2, DH // 128
    scratch = [
        vm(features.shape, BF16), vm(outer_masks.shape, jnp.int32), vm(inner_masks.shape, jnp.int32),
        vm(class_weight.shape, BF16), vm(hidden_weight.shape, BF16),
        vm((cap, NO), jnp.int32), vm((2, NO), jnp.int32), vm((1, labels.shape[0]), jnp.int32),
        vm((8, NO), F32), vm((Z, 8, NO), F32), vm((Q, 8, LW), F32), vm((Q, 8, LW), F32),
        vm((X, Q * 8, LW), BF16), vm((rows, X * hop), BF16), vm((rows, X * hop), BF16),
        vm((16, DH), BF16), vm((C, 16, DH), BF16), vm((Z, X, C, 16, D), BF16),
        *[vm((nk, Z, cap * Q, DH // nk), BF16)] * 2, *[vm((nk, Q, cap * Z, DH // nk), BF16)] * 2,
        *[vm((nk, Q, cap * Z, DH // nk), BF16)] * 2, *[vm((nk, Z, cap * Q, DH // nk), BF16)] * 2,
        vm((cap * NO, cap * NO), BF16), vm((cap * NO, cap * NO), BF16), vm((hop, hop), BF16), vm((hop, hop), BF16),
        vm((2, hop, DH), BF16), vm((hop, DH), BF16), vm((hop, HID), F32), vm((HID, hop), BF16), vm((HID, hop), BF16),
        vm((hop, HID), BF16),
        vm((X * Z, Q * half, xh), BF16), vm((X * Z, Q * half, xh), BF16),
        *[vm((2, Q, 2, Z * half, xh), BF16)] * 2, *[vm((2, Q, Z * half, 2 * xh), BF16)] * 2,
        vm((X * Z, Q * half, xh), BF16), vm((X * Z, Q * half, xh), BF16),
        vm((nk, X, Z, YL * 16, DH // nk), BF16), *[vm((nk, Z // 2, YL * 16, DH // nk), BF16)] * 4,
        *[vm((nk, Z, YL * 16, DH // nk), BF16)] * 4,
        vm((YL, 16, DH), BF16), vm((Y, 16, DH), BF16), vm((C, 8, DH), F32), vm((C, 8, DH), F32),
        vm((X * C, CP, cw), BF16), vm((X * C, CP, cw), BF16), vm((nb, cb, cw), BF16), vm((Y, cb, cw), BF16),
        vm((cb, cw), BF16), vm((Z, cb, cw), BF16), vm((cb, cw), BF16), vm((nb, cb, cw), BF16),
        vm((X * C, nb, cb, cw), BF16),
        dma((8,)),
        *[dma] * 6,
        dma((Y,)), dma((C,)), *[dma] * 6,
        *[dma((nk,))] * 8, *[dma((2,))] * 6, dma, dma,
        *[dma] * 4, dma((nk, 6)), dma((nk, 6)), dma((nk,)), dma((nk,)), dma((YL,)), dma, dma((X * C,)), dma((C,)),
        *[dma] * 10,
    ]
    hbm = pl.BlockSpec(memory_space=pl.ANY)
    vmem = pl.BlockSpec(memory_space=pltpu.VMEM)
    smem = pl.BlockSpec(memory_space=pltpu.SMEM)
    hidden_grad, class_grad, node_grad = pl.pallas_call(
        functools.partial(kernel, dims),
        out_shape=(
            jax.ShapeDtypeStruct(hidden_weight.shape, F32),
            jax.ShapeDtypeStruct((X * C, CP, cw), BF16),
            jax.ShapeDtypeStruct((rows, HID // X), BF16),
        ),
        in_specs=[hbm, hbm, hbm, hbm, hbm, smem, hbm, smem, hbm, hbm],
        out_specs=(vmem, vmem, vmem),
        scratch_shapes=scratch,
        compiler_params=pltpu.CompilerParams(
            collective_id=0, has_side_effects=True, vmem_limit_bytes=56 * 1024 * 1024
        ),
        cost_estimate=pl.CostEstimate(flops=2_000_000_000, bytes_accessed=3_000_000, transcendentals=20_000),
    )(
        features, hidden_weight, class_weight, request_ids.T, request_counts.T,
        outer_tiles, outer_masks, inner_tiles, inner_masks, labels.reshape(1, -1),
    )
    return pl.pallas_call(
        functools.partial(finish, (X, C, classes)),
        out_shape=(
            jax.ShapeDtypeStruct(hidden_grad.shape, F32),
            jax.ShapeDtypeStruct(class_weight.shape, F32),
            jax.ShapeDtypeStruct(node_grad.shape, BF16),
        ),
        in_specs=[hbm] * 3,
        out_specs=(hbm,) * 3,
        scratch_shapes=[vm((X * C, CP, cw), BF16), vm(class_weight.shape, F32), dma((4,))],
        cost_estimate=pl.CostEstimate(flops=0, bytes_accessed=1_300_000, transcendentals=0),
    )(hidden_grad, class_grad, node_grad)


def solution(mesh):
    grid = GRIDS[(mesh.shape["owner"], mesh.shape["rep"])]
    placed = (
        P("owner", None),
        P("owner", None),
        P(),
        P(("owner", "rep"), None),
        P(("owner", "rep"), None),
        P(("owner", "rep"), None),
        P(("owner", "rep"), None, None, None),
        P(("owner", "rep"), None),
        P(("owner", "rep"), None, None, None),
        P(("owner", "rep")),
    )
    return jax.shard_map(
        functools.partial(on_device, grid),
        mesh=mesh,
        in_specs=placed,
        out_specs=(P("owner", None), P(), P("owner", "rep")),
        check_vma=False,
    )
```

```python
import functools

import jax
import jax.numpy as jnp
from jax import lax
from jax.experimental import pallas as pl
from jax.experimental.pallas import tpu as pltpu
from jax.sharding import PartitionSpec as P

MESH = pl.DeviceIdType.MESH
F32 = jnp.float32
BF16 = jnp.bfloat16

GRIDS = {(128, 4): (8, 8, 2, 4), (32, 4): (2, 8, 2, 4)}


def iota(shape, dim):
    return lax.broadcasted_iota(jnp.int32, shape, dim)


def quo(a, n):
    return lax.shift_right_logical(a, jnp.full_like(a, n.bit_length() - 1))


def rem(a, n):
    return lax.bitwise_and(a, jnp.full_like(a, n - 1))


def flag(cond, dtype=BF16):
    return jnp.where(cond, 1.0, 0.0).astype(F32).astype(dtype)


def dot(a, b, ca=1, cb=0):
    return lax.dot_general(a, b, (((ca,), (cb,)), ((), ())), preferred_element_type=F32)


def regroup(outer, middle, inner, transpose=False):
    n = outer * middle * inner
    o, i = iota((n, n), 0), iota((n, n), 1)
    if transpose:
        o, i = i, o
    m, rest = quo(o, outer * inner), rem(o, outer * inner)
    a, b = quo(rest, inner), rem(rest, inner)
    return flag(i == a * (middle * inner) + m * inner + b)


def kernel(
    dims,
    feat_hbm, weight_hbm, cls_hbm, ids_hbm, counts_hbm, otile_ref, omask_hbm, itile_ref, imask_hbm, labels_hbm,
    hidden_out, class_out, node_out,
    feat, omask, imask, cls, weight_ref, ids_ref, counts_ref, labels_ref,
    i1s, i1r, i2s, i2r, wx, place_a, place_b,
    ws, wr, w_all,
    fa1s, fa1r, fa2s, fa2r, fb1s, fb1r, fb2s, fb2r, move_a, move_b, swap_a, swap_b,
    agg, agr, pre, pgt, pgtr, diff,
    na1s, na1r, na2s, na2r, nb1s, nb1r, nb2s, nb2r,
    gs1, gra, grb, gsa, gsb, grl, grr, gs2, gr2, gs3, gr3, gs4, gr4,
    cs1, cr1, cs2, cr2, cs3, cr3, cfin, ca4, ca5,
    local_sem,
    i1_ss, i1_rs, i2_ss, i2_rs, wx_ss, wx_rs,
    w1_ss, w1_rs, w2_ss, w2_rs, w3_ss, w3_rs, w4_ss, w4_rs,
    fa1_ss, fa1_rs, fa2_ss, fa2_rs, fb1_ss, fb1_rs, fb2_ss, fb2_rs,
    na1_ss, na1_rs, na2_ss, na2_rs, nb1_ss, nb1_rs, nb2_ss, nb2_rs,
    ga_ss, ga_rs, g0_ss, g0_rs, g1_ss, g1_rs, g2_ss, g2_rs, g3_ss, g3_rs, g4_ss, g4_rs,
    c1_ss, c1_rs, c2_ss, c2_rs, c3_ss, c3_rs, c4_ss, c4_rs, c5_ss, c5_rs,
):
    Z, Y, C, X, cap, tile, rows, classes = dims
    Q = Y * C
    NO = Z * Q
    half = cap // 2
    hop, front = NO * half, NO * cap
    D, HID = feat.shape[1], pre.shape[1]
    DH, HH = D // 2, HID // 2
    YL = Y // X
    nb, cb, cw = cs2.shape
    CP = nb * cb
    seeds = labels_ref.shape[1]
    row_blocks, col_blocks, K = hop // tile, front // tile, otile_ref.shape[1]
    LW = i2s.shape[2]
    S8 = 8

    me_o = lax.axis_index("owner")
    x = lax.axis_index("rep")
    z = me_o // Q
    q = me_o % Q
    y = q // C
    c = q % C
    sib = C - 1 - c

    def copy(src, dst, ss, rs, zz, qq, xx):
        return pltpu.make_async_remote_copy(
            src_ref=src, dst_ref=dst, send_sem=ss, recv_sem=rs,
            device_id=(zz * Q + qq, xx), device_id_type=MESH,
        )

    def each(n, body):
        def step(i, carry):
            body(i)
            return carry
        lax.fori_loop(1, n, step, 0, unroll=True)

    class Exchange:
        def __init__(self, n, me, at, src, dst, bulk, ss, rs):
            self.n, self.me, self.at, self.src, self.dst, self.bulk, self.ss, self.rs = n, me, at, src, dst, bulk, ss, rs

        def start(self):
            def send(d):
                to = lax.bitwise_and(self.me + d, self.n - 1)
                copy(self.src(to), self.dst(self.me), self.ss, self.rs, *self.at(to)).start()
            each(self.n, send)

        def all(self):
            return copy(self.bulk, self.bulk, self.ss, self.rs, *self.at(lax.bitwise_and(self.me + 1, self.n - 1)))

        def recv(self):
            self.all().wait_recv()

        def sent(self):
            self.all().wait_send()

    def along_z(*rest):
        return Exchange(Z, z, lambda t: (t, q, x), *rest)

    def along_q(*rest):
        return Exchange(Q, q, lambda t: (z, t, x), *rest)

    def along_y(*rest):
        return Exchange(Y, y, lambda t: (z, t * C + c, x), *rest)

    def along_x(*rest):
        return Exchange(X, x, lambda t: (z, q, t), *rest)

    def along_xz(*rest):
        return Exchange(X * Z, x * Z + z, lambda t: (lax.bitwise_and(t, Z - 1), q, t // Z), *rest)

    def along_xc(*rest):
        return Exchange(X * C, x * C + c, lambda t: (z, y * C + lax.bitwise_and(t, C - 1), t // C), *rest)

    def blocks(ref, n):
        return ref.at[pl.ds(0, n - 1)]

    def to_sibling(src, dst, ss, rs):
        return copy(src, dst, ss, rs, z, y * C + sib, x)

    staged = (
        (ids_hbm, ids_ref), (weight_hbm, weight_ref), (feat_hbm, feat), (counts_hbm, counts_ref),
        (omask_hbm, omask), (imask_hbm, imask), (labels_hbm, labels_ref), (cls_hbm, cls),
    )
    loads = [pltpu.make_async_copy(src, dst, local_sem.at[k]) for k, (src, dst) in enumerate(staged)]
    for load in loads:
        load.start()

    barrier = pltpu.get_barrier_semaphore()

    def greet(zz, qq, xx):
        pl.semaphore_signal(barrier, inc=1, device_id=(zz * Q + qq, xx), device_id_type=MESH)

    def greet_xz(d):
        t = lax.bitwise_and(x * Z + z + d, X * Z - 1)
        greet(lax.bitwise_and(t, Z - 1), q, t // Z)

    each(Q, lambda d: greet(z, lax.bitwise_and(q + d, Q - 1), x))
    each(X * Z, greet_xz)
    each(X, lambda d: greet(z, y * C + sib, lax.bitwise_and(x + d, X - 1)))

    i1s[...] = jnp.zeros_like(i1s)
    for load in loads[:2]:
        load.wait()
    i1s[0:cap, :] = ids_ref[...].astype(F32)
    w32 = weight_ref[...].astype(F32)
    ws[...] = jnp.concatenate([w32[:, :DH], w32[:, DH:]], axis=0).astype(BF16)

    pl.semaphore_wait(barrier, (Q - 1) + (X * Z - 1) + (X - 1))

    ex_i1 = along_z(lambda t: i1s, lambda f: i1r.at[f], blocks(i1r, Z), i1_ss, i1_rs)
    ex_i1.start()
    i1r[z] = i1s[...]

    w_core = y % C

    def w1_copy(t):
        return copy(ws, wr.at[c], w1_ss.at[t], w1_rs.at[c], z, t * C + w_core, x)

    def w1_each(act):
        def step(t, carry):
            @pl.when((y // C == x) & jnp.logical_not((t == y) & (w_core == c)))
            def _():
                act(t)
            return carry
        lax.fori_loop(0, Y, step, 0, unroll=True)

    w1_each(lambda t: w1_copy(t).start())
    y_mine = x * C + c

    ex_i1.recv()
    marks = flag(iota((Q, NO), 1) == z * Q + iota((Q, NO), 0))
    asked = i1r[...].reshape(Z * S8, NO).astype(BF16)
    if LW > Z * S8:
        asked = jnp.concatenate([asked] * (LW // (Z * S8)), axis=0)
    for_q = dot(marks, asked, 1, 1)
    for k in range(Q):
        i2s[k] = jnp.broadcast_to(for_q[k:k + 1, :], (8, LW))
    ex_i2 = along_q(lambda t: i2s.at[t], lambda f: i2r.at[f], blocks(i2r, Q), i2_ss, i2_rs)
    ex_i2.start()
    i2r[q] = i2s[q]

    for c0 in range(C):
        own = (y == y_mine) & (c == c0)

        @pl.when(own)
        def _():
            wr[c0] = ws[...]

        @pl.when(jnp.logical_not(own))
        def _():
            copy(ws, wr.at[c0], w1_ss.at[0], w1_rs.at[c0], z, y_mine * C + c0, x).wait_recv()
    for hcol in range(2):
        cols = slice(hcol * DH, (hcol + 1) * DH)
        w_all[z, x, c, :, cols] = jnp.concatenate(
            [wr[c0, hcol * 8:(hcol + 1) * 8, :].astype(F32) for c0 in range(C)], axis=0
        ).astype(BF16)
    ex_w2 = along_z(
        lambda t: w_all.at[z, x, c], lambda f: w_all.at[f, x, c], w_all.at[pl.ds(0, Z - 1), x, c], w2_ss, w2_rs
    )
    ex_w2.start()

    loads[2].wait()
    lane_q = iota((front, Q * 8), 1)

    ex_i2.recv()
    wanted = i2r[...].reshape(Q * 8, LW).astype(BF16)

    wx[x] = wanted
    ex_wx = along_x(lambda t: wx.at[x], lambda f: wx.at[f], blocks(wx, X), wx_ss, wx_rs)

    def picked(col_of, q_of):
        spread = dot(flag(iota((front, LW), 1) == col_of), wanted, 1, 1)
        ids = jnp.sum(jnp.where(lane_q == q_of * 8, spread, 0.0), axis=1, keepdims=True)
        return flag(ids == iota((front, rows), 1).astype(F32))

    chunks, wide = fa1s.shape[0], fa1s.shape[3]
    r = iota((front, 1), 0)
    pick_a = picked(quo(r, cap * Q) * S8 + quo(rem(r, cap * Q), Q), rem(r, Q))

    def column_blocks(first):
        return jnp.concatenate([feat[:, b * wide:(b + 1) * wide] for b in range(first, 2 * chunks, 2)], axis=1)

    rows_a = dot(pick_a, column_blocks(0)).astype(BF16)
    ex_fa1, ex_fb1, ex_fa2, ex_fb2 = [], [], [], []
    for k in range(chunks):
        at = slice(k * wide, (k + 1) * wide)
        fa1s[k] = rows_a[:, at].reshape(fa1s.shape[1:])
        ex_fa1.append(along_z(
            lambda t, k=k: fa1s.at[k, t], lambda f, k=k: fa1r.at[k, f], blocks(fa1r.at[k], Z), fa1_ss.at[k], fa1_rs.at[k]))
        ex_fb1.append(along_q(
            lambda t, k=k: fb1s.at[k, t], lambda f, k=k: fb1r.at[k, f], blocks(fb1r.at[k], Q), fb1_ss.at[k], fb1_rs.at[k]))
        ex_fa2.append(along_q(
            lambda t, k=k: fa2s.at[k, t], lambda f, k=k: fa2r.at[k, f], blocks(fa2r.at[k], Q), fa2_ss.at[k], fa2_rs.at[k]))
        ex_fb2.append(along_z(
            lambda t, k=k: fb2s.at[k, t], lambda f, k=k: fb2r.at[k, f], blocks(fb2r.at[k], Z), fb2_ss.at[k], fb2_rs.at[k]))
    ex_fa1[0].start()
    pick_b = picked(rem(r, Z) * S8 + quo(rem(r, cap * Z), Z), quo(r, cap * Z))
    rows_b = dot(pick_b, column_blocks(1)).astype(BF16)
    for k in range(chunks):
        at = slice(k * wide, (k + 1) * wide)
        fb1s[k] = rows_b[:, at].reshape(fb1s.shape[1:])
    ex_fb1[0].start()
    for k in range(1, chunks):
        ex_fa1[k].start()
        ex_fb1[k].start()
    for k in range(chunks):
        fa1r[k, z] = fa1s[k, z]
        fb1r[k, q] = fb1s[k, q]
    ex_wx.start()
    move_a[...] = regroup(Z * cap, Q, 1)
    move_b[...] = regroup(Q * cap, Z, 1)

    ex_w2.recv()
    ex_w3 = along_x(
        lambda t: w_all.at[:, x, c], lambda f: w_all.at[:, f, c], w_all.at[:, pl.ds(0, X - 1), c], w3_ss, w3_rs
    )
    ex_w3.start()

    for load in loads[3:]:
        load.wait()
    counts = counts_ref[...].astype(F32)
    counts8 = jnp.concatenate([counts, jnp.zeros((6, NO), F32)], axis=0).astype(BF16)

    def validity(slots):
        n = NO * slots
        at = iota((NO, n), 1)
        per = dot(counts8, flag(iota((NO, n), 0) == quo(at, slots)))
        j = rem(iota((1, n), 1), slots).astype(F32)
        first = flag(j < per[0:1, :], F32)
        second = flag(j - half < per[1:2, :], F32)
        return jnp.where(j < half, first, second)

    valid = validity(cap)
    outer_rows = []
    for b in range(row_blocks):
        tiles = []
        for cbk in range(col_blocks):
            m = jnp.zeros((tile, tile), jnp.int32)
            for k in range(K):
                m = m + omask[b, k] * (otile_ref[b, k] == cbk).astype(jnp.int32)
            tiles.append(m.astype(F32) * valid[:, cbk * tile:(cbk + 1) * tile])
        outer_rows.append(jnp.concatenate(tiles, axis=1))
    outer = jnp.concatenate(outer_rows, axis=0)
    outer_scale = 1.0 + jnp.sum(outer, axis=1, keepdims=True)
    oi, oc = iota((hop, front), 0), iota((hop, front), 1)
    self_col = quo(oi, half) * cap + rem(oi, half)
    outer_self = (outer + flag(oc == self_col, F32)).astype(BF16)
    outer_a = dot(outer_self, regroup(Z, Q, cap, transpose=True)).astype(BF16)

    hop_valid = validity(half)
    tiles = []
    for cbk in range(row_blocks):
        m = jnp.zeros((tile, tile), jnp.int32)
        for k in range(K):
            m = m + imask[0, k] * (itile_ref[0, k] == cbk).astype(jnp.int32)
        tiles.append(m.astype(F32) * hop_valid[:, cbk * tile:(cbk + 1) * tile])
    inner32 = jnp.concatenate(tiles, axis=1)
    inner_degree = jnp.maximum(jnp.sum(inner32, axis=1, keepdims=True), 1.0)
    inner = inner32.astype(BF16)
    inner_twice = jnp.concatenate([inner32.T, inner32.T], axis=1).astype(BF16)

    label_row = labels_ref[...]
    label_col = jnp.sum(
        jnp.where(iota((seeds, seeds), 0) == iota((seeds, seeds), 1), label_row, 0), axis=1, keepdims=True
    )
    one_hot = flag(label_col == iota((seeds, classes), 1), F32)

    for k in range(chunks):
        ex_fa1[k].recv()
        fa2s[k] = dot(move_a[...], fa1r[k].reshape(front, wide)).astype(BF16).reshape(fa2s.shape[1:])
        ex_fa2[k].start()
        fa2r[k, q] = fa2s[k, q]
        ex_fb1[k].recv()
        fb2s[k] = dot(move_b[...], fb1r[k].reshape(front, wide)).astype(BF16).reshape(fb2s.shape[1:])
        ex_fb2[k].start()
        fb2r[k, z] = fb2s[k, z]

    ex_w3.recv()
    w4 = to_sibling(w_all.at[:, :, c], w_all.at[:, :, c], w4_ss, w4_rs)
    w4_in = to_sibling(w_all.at[:, :, sib], w_all.at[:, :, sib], w4_ss, w4_rs)
    w4.start()

    swap_a[...] = regroup(Z, Q, half)
    swap_b[...] = regroup(Q, Z, half)
    ex_wx.recv()

    def places(x_of, j_of, z_of, q_of):
        n = X * hop
        pick = flag(iota((LW, n), 0) == z_of * S8 + j_of)
        ids = jnp.zeros((1, n), F32)
        for k in range(X):
            here = (iota((Q * 8, n), 0) == q_of * 8) & (x_of == k)
            ids = ids + jnp.sum(jnp.where(here, dot(wx[k], pick), 0.0), axis=0, keepdims=True)
        return flag(iota((rows, n), 0).astype(F32) == ids)

    s = iota((1, X * hop), 1)
    def plane(d):
        return lax.bitwise_and(x + X - d, jnp.full_like(d, X - 1))

    place_a[...] = places(
        plane(rem(quo(s, half * Z), X)), rem(s, half), rem(quo(s, half), Z), quo(s, half * Z * X)
    )
    place_b[...] = places(
        plane(quo(s, half * Q * Z)), rem(s, half), rem(quo(s, half * Q), Z), rem(quo(s, half), Q)
    )

    for k in range(chunks):
        ex_fa2[k].recv()
        part_a = (dot(outer_a, fa2r[k].reshape(front, wide)) / outer_scale).astype(BF16)
        ex_fb2[k].recv()
        part_b = (dot(outer_self, fb2r[k].reshape(front, wide)) / outer_scale).astype(BF16)
        for b, part in ((2 * k, part_a), (2 * k + 1, part_b)):
            agg[b // chunks, :, (b % chunks) * wide:(b % chunks + 1) * wide] = part
        if k == 0:
            w4_in.wait_recv()
        part = dot(
            jnp.concatenate([part_a, part_b], axis=1),
            w_all[:, :, :, :, 2 * k * wide:2 * (k + 1) * wide].reshape(HID, 2 * wide), 1, 1)
        pre[...] = part if k == 0 else pre[...] + part
    ga = to_sibling(agg.at[sib], agr, ga_ss, ga_rs)
    ga.start()

    hidden = jnp.maximum(pre[...], 0.0).astype(BF16)
    agg_two = (dot(inner, hidden) / inner_degree).astype(BF16)
    logits = dot(agg_two, cls[...], 1, 1)
    exponent = jnp.exp(logits - jnp.max(logits, axis=1, keepdims=True))
    softmax = exponent / jnp.sum(exponent, axis=1, keepdims=True)
    logit_grad = ((softmax - one_hot) / seeds).astype(BF16)
    widen = flag(iota((classes, CP), 0) == iota((classes, CP), 1))
    class_rows = dot(dot(logit_grad, widen).astype(BF16), agg_two, 0, 0).astype(BF16)
    for t in range(X):
        for cc in range(C):
            cs1[t * C + cc] = class_rows[:, cc * HH + t * cw:cc * HH + (t + 1) * cw]
    me_xc = x * C + c
    ex_c1 = along_xc(lambda t: cs1.at[t], lambda f: cr1.at[f], blocks(cr1, X * C), c1_ss, c1_rs)
    ex_c1.start()
    cr1[me_xc] = cs1[me_xc]

    agg_grad = dot(logit_grad, cls[...]) / inner_degree
    high = agg_grad.astype(BF16)
    low = (agg_grad - high.astype(F32)).astype(BF16)
    hidden_diff = dot(inner_twice, jnp.concatenate([high, low], axis=0))
    pgt[...] = jnp.where(pre[...] > 0.0, hidden_diff, 0.0).T.astype(BF16)
    g0 = to_sibling(pgt, pgtr, g0_ss, g0_rs)
    g0.start()

    diff[...] = hidden_diff.astype(BF16)
    xw = HID // X
    xh = xw // 2

    def xz_leg(src, dst, ss, rs):
        def send(t):
            d, zz = t // Z, lax.bitwise_and(z + t, Z - 1)
            copy(src(d, zz), dst.at[d * Z + z], ss, rs, zz, q, lax.bitwise_and(x + d, X - 1)).start()
        each(X * Z, send)

    def wait_blocks(ref, n, ss, rs):
        some = ref.at[pl.ds(0, n)]
        return copy(some, some, ss, rs, z, q, lax.bitwise_and(x + 1, X - 1))

    for t in range(X):
        na1s[t * Z:(t + 1) * Z] = diff[:, t * xw:t * xw + xh].reshape(Z, Q * half, xh)
    xz_leg(lambda d, zz: na1s.at[lax.bitwise_and(x + d, X - 1) * Z + zz], na1r, na1_ss, na1_rs)
    second = jnp.concatenate([
        diff[:, pl.ds(pl.multiple_of(lax.bitwise_and(x + d, X - 1) * xw + xh, xh), xh)] for d in range(X)
    ], axis=1)
    nb1s[...] = dot(swap_a[...], second).astype(BF16).reshape(nb1s.shape)
    ex_nb1 = along_q(lambda t: nb1s.at[t], lambda f: nb1r.at[f], blocks(nb1r, Q), nb1_ss, nb1_rs)
    ex_nb1.start()
    ex_na2 = along_q(lambda t: na2s.at[t], lambda f: na2r.at[f], blocks(na2r, Q), na2_ss, na2_rs)
    na1r[z] = na1s[x * Z + z]
    nb1r[q] = nb1s[q]

    def total(ref, n):
        acc = ref[0].astype(F32)
        for k in range(1, n):
            acc = acc + ref[k].astype(F32)
        return acc

    gmine = dot(pgt[...], agg[c])
    ga.wait_recv()
    g0.wait_recv()
    gmine = (gmine + dot(pgtr[...], agr[...])).astype(BF16).reshape(Z, X, YL * 16, DH)
    parts, span = gs1.shape[0], gs1.shape[4]
    for k in range(parts):
        for t in range(X):
            gs1[k, t] = gmine[:, t, :, k * span:(k + 1) * span]
    right, left, across = (lax.bitwise_and(x + d, X - 1) for d in (1, X - 1, 2))
    lower, upper = pl.ds(0, Z // 2), pl.ds(Z // 2, Z // 2)

    def g1(k, n, src, dst, to):
        return copy(src, dst, g1_ss.at[k, n], g1_rs.at[k, n], z, q, to)

    ring = [(
        g1(k, 0, gs1.at[k, across, lower], gra.at[k], right), g1(k, 1, gs1.at[k, across, upper], grb.at[k], left),
        g1(k, 2, gs1.at[k, right, upper], grl.at[k, upper], right), g1(k, 3, gs1.at[k, left, lower], grr.at[k, lower], left),
        g1(k, 4, gsa.at[k], grl.at[k, lower], right), g1(k, 5, gsb.at[k], grr.at[k, upper], left),
    ) for k in range(parts)]
    for k in range(parts):
        for one in ring[k][:4]:
            one.start()

    ex_c1.recv()
    cs2[...] = total(cr1, X * C).astype(BF16).reshape(cs2.shape)

    def to_blocks(act):
        def step(t, carry):
            @pl.when(t != y)
            def _():
                act(t)
            return carry
        lax.fori_loop(0, nb, step, 0, unroll=True)

    to_blocks(lambda t: copy(cs2.at[t], cr2.at[y], c2_ss, c2_rs, z, t * C + c, x).start())
    summing = y < nb
    ex_c2 = along_y(None, None, blocks(cr2, Y), c2_ss, c2_rs)
    ex_c3 = along_z(lambda t: cs3, lambda f: cr3.at[f], blocks(cr3, Z), c3_ss, c3_rs)
    ex_c4 = along_y(lambda t: cfin, lambda f: ca4.at[f], blocks(cr2, Y), c4_ss, c4_rs)

    for k in range(parts):
        r1, l1, r2, l2, r3, l3 = ring[k]
        r1.wait_recv()
        gsa[k] = (gs1[k, right, lower].astype(F32) + gra[k].astype(F32)).astype(BF16)
        r3.start()
        l1.wait_recv()
        gsb[k] = (gs1[k, left, upper].astype(F32) + grb[k].astype(F32)).astype(BF16)
        l3.start()

    wait_blocks(na1r, X * Z - 1, na1_ss, na1_rs).wait_recv()
    came = jnp.concatenate([na1r[d * Z:(d + 1) * Z].reshape(hop, xh) for d in range(X)], axis=1)
    came = dot(swap_a[...], came).astype(BF16)
    for d in range(X):
        na2s[:, d] = came[:, d * xh:(d + 1) * xh].reshape(Q, Z * half, xh)
    ex_na2.start()
    na2r[q] = na2s[q]
    ex_nb1.recv()
    came = dot(swap_b[...], nb1r[...].reshape(hop, X * xh)).astype(BF16)
    for d in range(X):
        nb2s[d * Z:(d + 1) * Z] = came[:, d * xh:(d + 1) * xh].reshape(Z, Q * half, xh)
    xz_leg(lambda d, zz: nb2s.at[d * Z + zz], nb2r, nb2_ss, nb2_rs)
    nb2r[z] = nb2s[z]

    @pl.when(summing)
    def _():
        cr2[y] = cs2[y]
        ex_c2.recv()
        cs3[...] = total(cr2, Y).astype(BF16)
        ex_c3.start()
        cr3[z] = cs3[...]

    ex_g2 = []
    for k in range(parts):
        for one in ring[k][2:]:
            one.wait_recv()
        gs2[k] = (gs1[k, x].astype(F32) + grl[k].astype(F32) + grr[k].astype(F32)).astype(BF16)
        ex_g2.append(along_z(
            lambda t, k=k: gs2.at[k, t], lambda f, k=k: gr2.at[k, f], blocks(gr2.at[k], Z), g2_ss.at[k], g2_rs.at[k]))
        ex_g2[k].start()
        gr2[k, z] = gs2[k, z]

    @pl.when(summing)
    def _():
        ex_c3.recv()
        cfin[...] = total(cr3, Z).astype(BF16)
        ex_c4.start()
        ca4[y] = cfin[...]

    for k in range(parts):
        ex_g2[k].recv()
        gs3[:, :, k * span:(k + 1) * span] = total(gr2.at[k], Z).astype(BF16).reshape(YL, 16, span)

    def g3_copy(yl):
        return copy(gs3.at[yl], gr3.at[y], g3_ss.at[yl], g3_rs, z, (x * YL + yl) * C + c, x)

    for yl in range(YL):
        @pl.when(x * YL + yl != y)
        def _():
            g3_copy(yl).start()
    owning = y // YL == x

    @pl.when(summing)
    def _():
        some = ca4.at[pl.ds(0, nb - 1)]
        copy(some, some, c4_ss, c4_rs, z, q, x).wait_recv()

    @pl.when(jnp.logical_not(summing))
    def _():
        copy(ca4, ca4, c4_ss, c4_rs, z, q, x).wait_recv()

    ex_c5 = along_xc(lambda t: ca4, lambda f: ca5.at[f], blocks(ca5, X * C), c5_ss, c5_rs)
    ex_c5.start()
    ca5[me_xc] = ca4[...]

    ex_na2.recv()
    node_out[:, :xh] = dot(place_a[...], na2r[...].reshape(X * hop, xh)).astype(BF16)

    def g4_copy(xx, cc):
        return copy(gs4.at[cc], gr4.at[c], g4_ss.at[xx * C + cc], g4_rs.at[c], z, y * C + cc, xx)

    def g4_each(act):
        for xx in range(X):
            for cc in range(C):
                @pl.when(owning & jnp.logical_not((x == xx) & (c == cc)))
                def _():
                    act(xx, cc)

    @pl.when(owning)
    def _():
        gr3[y] = gs3[y % YL]
        copy(blocks(gr3, Y), blocks(gr3, Y), g3_ss.at[0], g3_rs, z, q, x).wait_recv()
        gs4[...] = total(gr3, Y).reshape(gs4.shape)
        gr4[c] = gs4[c]

    g4_each(lambda xx, cc: g4_copy(xx, cc).start())

    wait_blocks(nb2r, X * Z - 1, nb2_ss, nb2_rs).wait_recv()
    node_out[:, xh:] = dot(place_b[...], nb2r[...].reshape(X * hop, xh)).astype(BF16)

    ex_c5.recv()
    for t in range(X):
        for cc in range(C):
            at = cc * HH + t * cw
            class_out[:, at:at + cw] = ca5[t * C + cc].reshape(CP, cw).astype(F32)[:classes]

    for cc in range(C):
        @pl.when(jnp.logical_not(owning & (c == cc)))
        def _():
            copy(gs4.at[0], gr4.at[cc], g4_ss.at[0], g4_rs.at[cc], z, y * C + cc, y // YL).wait_recv()
        hidden_out[:, cc * DH:(cc + 1) * DH] = gr4[cc]

    for ex in (ex_i1, ex_i2, ex_wx, ex_w2, ex_w3, *ex_fa1, *ex_fb1, *ex_fa2, *ex_fb2, ex_nb1, ex_na2, *ex_g2, ex_c1, ex_c5):
        ex.sent()
    w1_each(lambda t: w1_copy(t).wait_send())
    for one in (w4, ga, g0, *[leg for legs in ring for leg in legs]):
        one.wait_send()
    wait_blocks(na1r, X * Z - 1, na1_ss, na1_rs).wait_send()
    wait_blocks(nb2r, X * Z - 1, nb2_ss, nb2_rs).wait_send()

    @pl.when(summing)
    def _():
        some = cs2.at[pl.ds(0, nb - 1)]
        copy(some, some, c2_ss, c2_rs, z, q, x).wait_send()
        ex_c3.sent()
        ex_c4.sent()

    @pl.when(jnp.logical_not(summing))
    def _():
        copy(cs2, cs2, c2_ss, c2_rs, z, q, x).wait_send()

    for yl in range(YL):
        @pl.when(x * YL + yl != y)
        def _():
            g3_copy(yl).wait_send()
    g4_each(lambda xx, cc: g4_copy(xx, cc).wait_send())


def on_device(
    grid, features, hidden_weight, class_weight, request_ids, request_counts,
    outer_tiles, outer_masks, inner_tiles, inner_masks, labels,
):
    Z, Y, C, X = grid
    Q = Y * C
    NO = Z * Q
    cap = request_ids.shape[1]
    half = cap // 2
    rows, D = features.shape
    classes, HID = class_weight.shape
    tile = outer_masks.shape[2]
    hop = NO * half
    DH, HH, YL = D // 2, HID // 2, Y // X
    cb = 32 if classes > 32 else 8
    nb = -(-classes // cb)
    CP, cw = nb * cb, HID // (C * X)
    LW = max(Z * 8, 128)
    dims = (Z, Y, C, X, cap, tile, rows, classes)
    vm, dma = pltpu.VMEM, pltpu.SemaphoreType.DMA
    xh, nk, gk = HID // X // 2, DH // 128, 1
    scratch = [
        vm(features.shape, BF16), vm(outer_masks.shape, jnp.int32), vm(inner_masks.shape, jnp.int32),
        vm(class_weight.shape, BF16), vm(hidden_weight.shape, BF16),
        vm((cap, NO), jnp.int32), vm((2, NO), jnp.int32), vm((1, labels.shape[0]), jnp.int32),
        vm((8, NO), F32), vm((Z, 8, NO), F32), vm((Q, 8, LW), F32), vm((Q, 8, LW), F32),
        vm((X, Q * 8, LW), BF16), vm((rows, X * hop), BF16), vm((rows, X * hop), BF16),
        vm((16, DH), BF16), vm((C, 16, DH), BF16), vm((Z, X, C, 16, D), BF16),
        *[vm((nk, Z, cap * Q, DH // nk), BF16)] * 2, *[vm((nk, Q, cap * Z, DH // nk), BF16)] * 2,
        *[vm((nk, Q, cap * Z, DH // nk), BF16)] * 2, *[vm((nk, Z, cap * Q, DH // nk), BF16)] * 2,
        vm((cap * NO, cap * NO), BF16), vm((cap * NO, cap * NO), BF16), vm((hop, hop), BF16), vm((hop, hop), BF16),
        vm((2, hop, DH), BF16), vm((hop, DH), BF16), vm((hop, HID), F32), vm((HID, hop), BF16), vm((HID, hop), BF16),
        vm((hop, HID), BF16),
        vm((X * Z, Q * half, xh), BF16), vm((X * Z, Q * half, xh), BF16),
        *[vm((Q, X, Z * half, xh), BF16)] * 2, *[vm((Q, Z * half, HH), BF16)] * 2,
        vm((X * Z, Q * half, xh), BF16), vm((X * Z, Q * half, xh), BF16),
        vm((gk, X, Z, YL * 16, DH // gk), BF16), *[vm((gk, Z // 2, YL * 16, DH // gk), BF16)] * 4,
        *[vm((gk, Z, YL * 16, DH // gk), BF16)] * 4,
        vm((YL, 16, DH), BF16), vm((Y, 16, DH), BF16), vm((C, 8, DH), F32), vm((C, 8, DH), F32),
        vm((X * C, CP, cw), BF16), vm((X * C, CP, cw), BF16), vm((nb, cb, cw), BF16), vm((Y, cb, cw), BF16),
        vm((cb, cw), BF16), vm((Z, cb, cw), BF16), vm((cb, cw), BF16), vm((nb, cb, cw), BF16),
        vm((X * C, nb, cb, cw), BF16),
        dma((8,)),
        *[dma] * 6,
        dma((Y,)), dma((C,)), *[dma] * 6,
        *[dma((nk,))] * 8, *[dma] * 8,
        *[dma] * 4, dma((gk, 6)), dma((gk, 6)), dma((gk,)), dma((gk,)), dma((YL,)), dma, dma((X * C,)), dma((C,)),
        *[dma] * 10,
    ]
    hbm = pl.BlockSpec(memory_space=pl.ANY)
    vmem = pl.BlockSpec(memory_space=pltpu.VMEM)
    smem = pl.BlockSpec(memory_space=pltpu.SMEM)
    return pl.pallas_call(
        functools.partial(kernel, dims),
        out_shape=(
            jax.ShapeDtypeStruct(hidden_weight.shape, F32),
            jax.ShapeDtypeStruct(class_weight.shape, F32),
            jax.ShapeDtypeStruct((rows, HID // X), BF16),
        ),
        in_specs=[hbm, hbm, hbm, hbm, hbm, smem, hbm, smem, hbm, hbm],
        out_specs=(vmem, vmem, vmem),
        scratch_shapes=scratch,
        compiler_params=pltpu.CompilerParams(
            collective_id=0, has_side_effects=True, vmem_limit_bytes=56 * 1024 * 1024
        ),
        cost_estimate=pl.CostEstimate(flops=2_000_000_000, bytes_accessed=3_000_000, transcendentals=20_000),
    )(
        features, hidden_weight, class_weight, request_ids.T, request_counts.T,
        outer_tiles, outer_masks, inner_tiles, inner_masks, labels.reshape(1, -1),
    )


def solution(mesh):
    grid = GRIDS[(mesh.shape["owner"], mesh.shape["rep"])]
    placed = (
        P("owner", None),
        P("owner", None),
        P(),
        P(("owner", "rep"), None),
        P(("owner", "rep"), None),
        P(("owner", "rep"), None),
        P(("owner", "rep"), None, None, None),
        P(("owner", "rep"), None),
        P(("owner", "rep"), None, None, None),
        P(("owner", "rep")),
    )
    return jax.shard_map(
        functools.partial(on_device, grid),
        mesh=mesh,
        in_specs=placed,
        out_specs=(P("owner", None), P(), P("owner", "rep")),
        check_vma=False,
    )
```

```python
import functools

import jax
import jax.numpy as jnp
from jax import lax
from jax.experimental import pallas as pl
from jax.experimental.pallas import tpu as pltpu
from jax.sharding import PartitionSpec as P

MESH = pl.DeviceIdType.MESH
F32 = jnp.float32
BF16 = jnp.bfloat16

GRIDS = {(128, 4): (8, 8, 2, 4), (32, 4): (2, 8, 2, 4)}


def iota(shape, dim):
    return lax.broadcasted_iota(jnp.int32, shape, dim)


def quo(a, n):
    return lax.shift_right_logical(a, jnp.full_like(a, n.bit_length() - 1))


def rem(a, n):
    return lax.bitwise_and(a, jnp.full_like(a, n - 1))


def flag(cond, dtype=BF16):
    return jnp.where(cond, 1.0, 0.0).astype(F32).astype(dtype)


def dot(a, b, ca=1, cb=0):
    return lax.dot_general(a, b, (((ca,), (cb,)), ((), ())), preferred_element_type=F32)


def regroup(outer, middle, inner, transpose=False):
    n = outer * middle * inner
    o, i = iota((n, n), 0), iota((n, n), 1)
    if transpose:
        o, i = i, o
    m, rest = quo(o, outer * inner), rem(o, outer * inner)
    a, b = quo(rest, inner), rem(rest, inner)
    return flag(i == a * (middle * inner) + m * inner + b)


def kernel(
    dims,
    feat_hbm, weight_hbm, cls_hbm, ids_hbm, counts_hbm, otile_ref, omask_hbm, itile_ref, imask_hbm, labels_hbm,
    hidden_out, class_out, node_out,
    feat, omask, imask, cls, weight_ref, ids_ref, counts_ref, labels_ref,
    i1s, i1r, i2s, i2r, wx, place_a, place_b,
    ws, wr, w_all,
    fa1s, fa1r, fa2s, fa2r, fb1s, fb1r, fb2s, fb2r, move_a, move_b, swap_a, swap_b,
    agg, agr, pre, pgt, pgtr, diff,
    na1s, na1r, na2s, na2r, nb1s, nb1r, nb2s, nb2r,
    gs1, gra, grb, gsa, gsb, grl, grr, gs2, gr2, gs3, gr3, gs4, gr4,
    cmine, cs0, cr0, cs1, cr1, cs2, cr2, cs3, cr3, cfin, ca4, ca5, ca6,
    local_sem,
    i1_ss, i1_rs, i2_ss, i2_rs, wx_ss, wx_rs,
    w1_ss, w1_rs, w2_ss, w2_rs, w3_ss, w3_rs, w4_ss, w4_rs,
    fa1_ss, fa1_rs, fa2_ss, fa2_rs, fb1_ss, fb1_rs, fb2_ss, fb2_rs,
    na1_ss, na1_rs, na2_ss, na2_rs, nb1_ss, nb1_rs, nb2_ss, nb2_rs,
    ga_ss, ga_rs, g0_ss, g0_rs, g1_ss, g1_rs, g2_ss, g2_rs, g3_ss, g3_rs, g4_ss, g4_rs,
    c0_ss, c0_rs, c1_ss, c1_rs, c2_ss, c2_rs, c3_ss, c3_rs, c4_ss, c4_rs, c5_ss, c5_rs, c6_ss, c6_rs,
):
    Z, Y, C, X, cap, tile, rows, classes = dims
    Q = Y * C
    NO = Z * Q
    half = cap // 2
    hop, front = NO * half, NO * cap
    D, HID = feat.shape[1], pre.shape[1]
    DH, HH = D // 2, HID // 2
    YL = Y // X
    nb, cb, cw = cs2.shape
    CP = nb * cb
    seeds = labels_ref.shape[1]
    row_blocks, col_blocks, K = hop // tile, front // tile, otile_ref.shape[1]
    LW = i2s.shape[2]
    S8 = 8

    me_o = lax.axis_index("owner")
    x = lax.axis_index("rep")
    z = me_o // Q
    q = me_o % Q
    y = q // C
    c = q % C
    sib = C - 1 - c

    def copy(src, dst, ss, rs, zz, qq, xx):
        return pltpu.make_async_remote_copy(
            src_ref=src, dst_ref=dst, send_sem=ss, recv_sem=rs,
            device_id=(zz * Q + qq, xx), device_id_type=MESH,
        )

    def each(n, body):
        def step(i, carry):
            body(i)
            return carry
        lax.fori_loop(1, n, step, 0)

    class Exchange:
        def __init__(self, n, me, at, src, dst, bulk, ss, rs):
            self.n, self.me, self.at, self.src, self.dst, self.bulk, self.ss, self.rs = n, me, at, src, dst, bulk, ss, rs

        def start(self):
            def send(d):
                to = lax.bitwise_and(self.me + d, self.n - 1)
                copy(self.src(to), self.dst(self.me), self.ss, self.rs, *self.at(to)).start()
            each(self.n, send)

        def all(self):
            return copy(self.bulk, self.bulk, self.ss, self.rs, *self.at(lax.bitwise_and(self.me + 1, self.n - 1)))

        def recv(self):
            self.all().wait_recv()

        def sent(self):
            self.all().wait_send()

    def along_z(*rest):
        return Exchange(Z, z, lambda t: (t, q, x), *rest)

    def along_q(*rest):
        return Exchange(Q, q, lambda t: (z, t, x), *rest)

    def along_y(*rest):
        return Exchange(Y, y, lambda t: (z, t * C + c, x), *rest)

    def along_x(*rest):
        return Exchange(X, x, lambda t: (z, q, t), *rest)

    def blocks(ref, n):
        return ref.at[pl.ds(0, n - 1)]

    def to_sibling(src, dst, ss, rs):
        return copy(src, dst, ss, rs, z, y * C + sib, x)

    staged = (
        (ids_hbm, ids_ref), (weight_hbm, weight_ref), (feat_hbm, feat), (counts_hbm, counts_ref),
        (omask_hbm, omask), (imask_hbm, imask), (labels_hbm, labels_ref), (cls_hbm, cls),
    )
    loads = [pltpu.make_async_copy(src, dst, local_sem.at[k]) for k, (src, dst) in enumerate(staged)]
    for load in loads:
        load.start()

    barrier = pltpu.get_barrier_semaphore()

    def greet(zz, qq, xx):
        pl.semaphore_signal(barrier, inc=1, device_id=(zz * Q + qq, xx), device_id_type=MESH)

    each(Z, lambda d: greet(lax.bitwise_and(z + d, Z - 1), q, x))
    each(Q, lambda d: greet(z, lax.bitwise_and(q + d, Q - 1), x))
    each(X, lambda d: greet(z, q, lax.bitwise_and(x + d, X - 1)))

    i1s[...] = jnp.zeros_like(i1s)
    for load in loads[:2]:
        load.wait()
    i1s[0:cap, :] = ids_ref[...].astype(F32)
    w32 = weight_ref[...].astype(F32)
    ws[...] = jnp.concatenate([w32[:, :DH], w32[:, DH:]], axis=0).astype(BF16)

    pl.semaphore_wait(barrier, (Z - 1) + (Q - 1) + (X - 1))

    ex_i1 = along_z(lambda t: i1s, lambda f: i1r.at[f], blocks(i1r, Z), i1_ss, i1_rs)
    ex_i1.start()
    i1r[z] = i1s[...]

    w_core = y % C

    def w1_copy(t):
        return copy(ws, wr.at[c], w1_ss.at[t], w1_rs.at[c], z, t * C + w_core, x)

    def w1_each(act):
        def step(t, carry):
            @pl.when((y // C == x) & jnp.logical_not((t == y) & (w_core == c)))
            def _():
                act(t)
            return carry
        lax.fori_loop(0, Y, step, 0)

    w1_each(lambda t: w1_copy(t).start())
    y_mine = x * C + c

    ex_i1.recv()
    marks = flag(iota((Q, NO), 1) == z * Q + iota((Q, NO), 0))
    asked = i1r[...].reshape(Z * S8, NO).astype(BF16)
    if LW > Z * S8:
        asked = jnp.concatenate([asked] * (LW // (Z * S8)), axis=0)
    for_q = dot(marks, asked, 1, 1)
    for k in range(Q):
        i2s[k] = jnp.broadcast_to(for_q[k:k + 1, :], (8, LW))
    ex_i2 = along_q(lambda t: i2s.at[t], lambda f: i2r.at[f], blocks(i2r, Q), i2_ss, i2_rs)
    ex_i2.start()
    i2r[q] = i2s[q]

    for c0 in range(C):
        own = (y == y_mine) & (c == c0)

        @pl.when(own)
        def _():
            wr[c0] = ws[...]

        @pl.when(jnp.logical_not(own))
        def _():
            copy(ws, wr.at[c0], w1_ss.at[0], w1_rs.at[c0], z, y_mine * C + c0, x).wait_recv()
    for hcol in range(2):
        cols = slice(hcol * DH, (hcol + 1) * DH)
        w_all[z, x, c, :, cols] = jnp.concatenate(
            [wr[c0, hcol * 8:(hcol + 1) * 8, :].astype(F32) for c0 in range(C)], axis=0
        ).astype(BF16)
    ex_w2 = along_z(
        lambda t: w_all.at[z, x, c], lambda f: w_all.at[f, x, c], w_all.at[pl.ds(0, Z - 1), x, c], w2_ss, w2_rs
    )
    ex_w2.start()

    loads[2].wait()
    lane_q = iota((front, Q * 8), 1)

    ex_i2.recv()
    wanted = i2r[...].reshape(Q * 8, LW).astype(BF16)

    wx[x] = wanted
    ex_wx = along_x(lambda t: wx.at[x], lambda f: wx.at[f], blocks(wx, X), wx_ss, wx_rs)

    def picked(col_of, q_of):
        spread = dot(flag(iota((front, LW), 1) == col_of), wanted, 1, 1)
        ids = jnp.sum(jnp.where(lane_q == q_of * 8, spread, 0.0), axis=1, keepdims=True)
        return flag(ids == iota((front, rows), 1).astype(F32))

    chunks, wide = fa1s.shape[0], fa1s.shape[3]
    r = iota((front, 1), 0)
    pick_a = picked(quo(r, cap * Q) * S8 + quo(rem(r, cap * Q), Q), rem(r, Q))

    def column_blocks(first):
        return jnp.concatenate([feat[:, b * wide:(b + 1) * wide] for b in range(first, 2 * chunks, 2)], axis=1)

    rows_a = dot(pick_a, column_blocks(0)).astype(BF16)
    ex_fa1, ex_fb1, ex_fa2, ex_fb2 = [], [], [], []
    for k in range(chunks):
        at = slice(k * wide, (k + 1) * wide)
        fa1s[k] = rows_a[:, at].reshape(fa1s.shape[1:])
        ex_fa1.append(along_z(
            lambda t, k=k: fa1s.at[k, t], lambda f, k=k: fa1r.at[k, f], blocks(fa1r.at[k], Z), fa1_ss.at[k], fa1_rs.at[k]))
        ex_fb1.append(along_q(
            lambda t, k=k: fb1s.at[k, t], lambda f, k=k: fb1r.at[k, f], blocks(fb1r.at[k], Q), fb1_ss.at[k], fb1_rs.at[k]))
        ex_fa2.append(along_q(
            lambda t, k=k: fa2s.at[k, t], lambda f, k=k: fa2r.at[k, f], blocks(fa2r.at[k], Q), fa2_ss.at[k], fa2_rs.at[k]))
        ex_fb2.append(along_z(
            lambda t, k=k: fb2s.at[k, t], lambda f, k=k: fb2r.at[k, f], blocks(fb2r.at[k], Z), fb2_ss.at[k], fb2_rs.at[k]))
    ex_fa1[0].start()
    pick_b = picked(rem(r, Z) * S8 + quo(rem(r, cap * Z), Z), quo(r, cap * Z))
    rows_b = dot(pick_b, column_blocks(1)).astype(BF16)
    for k in range(chunks):
        at = slice(k * wide, (k + 1) * wide)
        fb1s[k] = rows_b[:, at].reshape(fb1s.shape[1:])
    ex_fb1[0].start()
    for k in range(1, chunks):
        ex_fa1[k].start()
        ex_fb1[k].start()
    for k in range(chunks):
        fa1r[k, z] = fa1s[k, z]
        fb1r[k, q] = fb1s[k, q]
    ex_wx.start()
    move_a[...] = regroup(Z * cap, Q, 1)
    move_b[...] = regroup(Q * cap, Z, 1)

    ex_w2.recv()
    ex_w3 = along_x(
        lambda t: w_all.at[:, x, c], lambda f: w_all.at[:, f, c], w_all.at[:, pl.ds(0, X - 1), c], w3_ss, w3_rs
    )
    ex_w3.start()

    for load in loads[3:]:
        load.wait()
    counts = counts_ref[...].astype(F32)
    counts8 = jnp.concatenate([counts, jnp.zeros((6, NO), F32)], axis=0).astype(BF16)

    def validity(slots):
        n = NO * slots
        at = iota((NO, n), 1)
        per = dot(counts8, flag(iota((NO, n), 0) == quo(at, slots)))
        j = rem(iota((1, n), 1), slots).astype(F32)
        first = flag(j < per[0:1, :], F32)
        second = flag(j - half < per[1:2, :], F32)
        return jnp.where(j < half, first, second)

    valid = validity(cap)
    outer_rows = []
    for b in range(row_blocks):
        tiles = []
        for cbk in range(col_blocks):
            m = jnp.zeros((tile, tile), jnp.int32)
            for k in range(K):
                m = m + omask[b, k] * (otile_ref[b, k] == cbk).astype(jnp.int32)
            tiles.append(m.astype(F32) * valid[:, cbk * tile:(cbk + 1) * tile])
        outer_rows.append(jnp.concatenate(tiles, axis=1))
    outer = jnp.concatenate(outer_rows, axis=0)
    outer_scale = 1.0 + jnp.sum(outer, axis=1, keepdims=True)
    oi, oc = iota((hop, front), 0), iota((hop, front), 1)
    self_col = quo(oi, half) * cap + rem(oi, half)
    outer_self = (outer + flag(oc == self_col, F32)).astype(BF16)
    outer_a = dot(outer_self, regroup(Z, Q, cap, transpose=True)).astype(BF16)

    hop_valid = validity(half)
    tiles = []
    for cbk in range(row_blocks):
        m = jnp.zeros((tile, tile), jnp.int32)
        for k in range(K):
            m = m + imask[0, k] * (itile_ref[0, k] == cbk).astype(jnp.int32)
        tiles.append(m.astype(F32) * hop_valid[:, cbk * tile:(cbk + 1) * tile])
    inner32 = jnp.concatenate(tiles, axis=1)
    inner_degree = jnp.maximum(jnp.sum(inner32, axis=1, keepdims=True), 1.0)
    inner = inner32.astype(BF16)
    inner_twice = jnp.concatenate([inner32.T, inner32.T], axis=1).astype(BF16)

    label_row = labels_ref[...]
    label_col = jnp.sum(
        jnp.where(iota((seeds, seeds), 0) == iota((seeds, seeds), 1), label_row, 0), axis=1, keepdims=True
    )
    one_hot = flag(label_col == iota((seeds, classes), 1), F32)

    for k in range(chunks):
        ex_fa1[k].recv()
        fa2s[k] = dot(move_a[...], fa1r[k].reshape(front, wide)).astype(BF16).reshape(fa2s.shape[1:])
        ex_fa2[k].start()
        fa2r[k, q] = fa2s[k, q]
        ex_fb1[k].recv()
        fb2s[k] = dot(move_b[...], fb1r[k].reshape(front, wide)).astype(BF16).reshape(fb2s.shape[1:])
        ex_fb2[k].start()
        fb2r[k, z] = fb2s[k, z]

    ex_w3.recv()
    w4 = to_sibling(w_all.at[:, :, c], w_all.at[:, :, c], w4_ss, w4_rs)
    w4_in = to_sibling(w_all.at[:, :, sib], w_all.at[:, :, sib], w4_ss, w4_rs)
    w4.start()

    swap_a[...] = regroup(Z, Q, half)
    swap_b[...] = regroup(Q, Z, half)
    ex_wx.recv()

    def places(x_of, j_of, z_of, q_of):
        n = X * hop
        pick = flag(iota((LW, n), 0) == z_of * S8 + j_of)
        ids = jnp.zeros((1, n), F32)
        for k in range(X):
            here = (iota((Q * 8, n), 0) == q_of * 8) & (x_of == k)
            ids = ids + jnp.sum(jnp.where(here, dot(wx[k], pick), 0.0), axis=0, keepdims=True)
        return flag(iota((rows, n), 0).astype(F32) == ids)

    s = iota((1, X * hop), 1)
    def plane(d):
        return lax.bitwise_and(x + X - d, jnp.full_like(d, X - 1))

    place_a[...] = places(
        plane(quo(s, half * Z * Q)), rem(s, half), rem(quo(s, half), Z), rem(quo(s, half * Z), Q)
    )
    place_b[...] = places(
        plane(quo(s, half * Q * Z)), rem(s, half), rem(quo(s, half * Q), Z), rem(quo(s, half), Q)
    )

    for k in range(chunks):
        ex_fa2[k].recv()
        part_a = (dot(outer_a, fa2r[k].reshape(front, wide)) / outer_scale).astype(BF16)
        ex_fb2[k].recv()
        part_b = (dot(outer_self, fb2r[k].reshape(front, wide)) / outer_scale).astype(BF16)
        for b, part in ((2 * k, part_a), (2 * k + 1, part_b)):
            agg[b // chunks, :, (b % chunks) * wide:(b % chunks + 1) * wide] = part
        if k == 0:
            w4_in.wait_recv()
        part = dot(
            jnp.concatenate([part_a, part_b], axis=1),
            w_all[:, :, :, :, 2 * k * wide:2 * (k + 1) * wide].reshape(HID, 2 * wide), 1, 1)
        pre[...] = part if k == 0 else pre[...] + part
    ga = to_sibling(agg.at[sib], agr, ga_ss, ga_rs)
    ga.start()

    hidden = jnp.maximum(pre[...], 0.0).astype(BF16)
    agg_two = (dot(inner, hidden) / inner_degree).astype(BF16)
    logits = dot(agg_two, cls[...], 1, 1)
    exponent = jnp.exp(logits - jnp.max(logits, axis=1, keepdims=True))
    softmax = exponent / jnp.sum(exponent, axis=1, keepdims=True)
    logit_grad = ((softmax - one_hot) / seeds).astype(BF16)
    agg_grad = dot(logit_grad, cls[...]) / inner_degree
    high = agg_grad.astype(BF16)
    low = (agg_grad - high.astype(F32)).astype(BF16)
    hidden_diff = dot(inner_twice, jnp.concatenate([high, low], axis=0))
    pgt[...] = jnp.where(pre[...] > 0.0, hidden_diff, 0.0).T.astype(BF16)
    g0 = to_sibling(pgt, pgtr, g0_ss, g0_rs)
    g0.start()

    diff[...] = hidden_diff.astype(BF16)
    xw = HID // X
    xh = xw // 2
    for t in range(X):
        na1s[:, :, t * xh:(t + 1) * xh] = diff[:, t * xw:t * xw + xh].reshape(Z, Q * half, xh)
    ex_na1 = along_z(lambda t: na1s.at[t], lambda f: na1r.at[f], blocks(na1r, Z), na1_ss, na1_rs)
    ex_na1.start()
    na1r[z] = na1s[z]
    second = jnp.concatenate([diff[:, t * xw + xh:(t + 1) * xw] for t in range(X)], axis=1)
    nb1s[...] = dot(swap_a[...], second).astype(BF16).reshape(nb1s.shape)
    ex_nb1 = along_q(lambda t: nb1s.at[t], lambda f: nb1r.at[f], blocks(nb1r, Q), nb1_ss, nb1_rs)
    ex_nb1.start()
    nb1r[q] = nb1s[q]

    def planes_leg(n, me, at, src, dst, ss, rs):
        def send(t):
            d, to = t // n, lax.bitwise_and(me + t, n - 1)
            xx = lax.bitwise_and(x + d, X - 1)
            copy(src.at[xx * n + to], dst.at[d * n + me], ss, rs, *at(to), xx).start()
        each(X * n, send)

    def planes_all(ref, ss, rs):
        some = blocks(ref, ref.shape[0])
        return copy(some, some, ss, rs, z, q, lax.bitwise_and(x + 1, X - 1))

    widen = flag(iota((classes, CP), 0) == iota((classes, CP), 1))
    class_rows = dot(dot(logit_grad, widen).astype(BF16), agg_two, 0, 0)
    cs0[...] = jnp.where(c == 0, class_rows[:, HH:], class_rows[:, :HH]).astype(BF16)
    c0 = to_sibling(cs0, cr0, c0_ss, c0_rs)
    c0.start()
    cmine[...] = jnp.where(c == 0, class_rows[:, :HH], class_rows[:, HH:])

    def total(ref, n):
        acc = ref[0].astype(F32)
        for k in range(1, n):
            acc = acc + ref[k].astype(F32)
        return acc

    gmine = dot(pgt[...], agg[c])
    ga.wait_recv()
    g0.wait_recv()
    gmine = (gmine + dot(pgtr[...], agr[...])).astype(BF16).reshape(Z, X, YL * 16, DH)
    parts, span = gs1.shape[0], gs1.shape[4]
    for k in range(parts):
        for t in range(X):
            gs1[k, t] = gmine[:, t, :, k * span:(k + 1) * span]
    right, left, across = (lax.bitwise_and(x + d, X - 1) for d in (1, X - 1, 2))
    lower, upper = pl.ds(0, Z // 2), pl.ds(Z // 2, Z // 2)

    def g1(k, n, src, dst, to):
        return copy(src, dst, g1_ss.at[k, n], g1_rs.at[k, n], z, q, to)

    ring = [(
        g1(k, 0, gs1.at[k, across, lower], gra.at[k], right), g1(k, 1, gs1.at[k, across, upper], grb.at[k], left),
        g1(k, 2, gs1.at[k, right, upper], grl.at[k, upper], right), g1(k, 3, gs1.at[k, left, lower], grr.at[k, lower], left),
        g1(k, 4, gsa.at[k], grl.at[k, lower], right), g1(k, 5, gsb.at[k], grr.at[k, upper], left),
    ) for k in range(parts)]
    for k in range(parts):
        for one in ring[k][:4]:
            one.start()

    c0.wait_recv()
    cmine[...] = cmine[...] + cr0[...].astype(F32)
    for t in range(X):
        cs1[t] = cmine[:, t * cw:(t + 1) * cw].astype(BF16)
    ex_c1 = along_x(lambda t: cs1.at[t], lambda f: cr1.at[f], blocks(cr1, X), c1_ss, c1_rs)
    ex_c1.start()
    cr1[x] = cs1[x]

    def to_blocks(act):
        def step(t, carry):
            @pl.when(t != y)
            def _():
                act(t)
            return carry
        lax.fori_loop(0, nb, step, 0)

    summing = y < nb
    ex_c2 = along_y(None, None, blocks(cr2, Y), c2_ss, c2_rs)
    ex_c3 = along_z(lambda t: cs3, lambda f: cr3.at[f], blocks(cr3, Z), c3_ss, c3_rs)
    ex_c4 = along_y(lambda t: cfin, lambda f: ca4.at[f], blocks(cr2, Y), c4_ss, c4_rs)

    for k in range(parts):
        r1, l1, r2, l2, r3, l3 = ring[k]
        r1.wait_recv()
        gsa[k] = (gs1[k, right, lower].astype(F32) + gra[k].astype(F32)).astype(BF16)
        r3.start()
        l1.wait_recv()
        gsb[k] = (gs1[k, left, upper].astype(F32) + grb[k].astype(F32)).astype(BF16)
        l3.start()

    ex_na1.recv()
    came = dot(swap_a[...], na1r[...].reshape(hop, X * xh)).astype(BF16)
    for t in range(X):
        na2s[t * Q:(t + 1) * Q] = came[:, t * xh:(t + 1) * xh].reshape(Q, Z * half, xh)
    planes_leg(Q, q, lambda t: (z, t), na2s, na2r, na2_ss, na2_rs)
    na2r[q] = na2s[x * Q + q]

    ex_c1.recv()
    cs2[...] = total(cr1, X).astype(BF16).reshape(cs2.shape)
    to_blocks(lambda t: copy(cs2.at[t], cr2.at[y], c2_ss, c2_rs, z, t * C + c, x).start())

    ex_nb1.recv()
    came = dot(swap_b[...], nb1r[...].reshape(hop, X * xh)).astype(BF16)
    for t in range(X):
        nb2s[t * Z:(t + 1) * Z] = came[:, t * xh:(t + 1) * xh].reshape(Z, Q * half, xh)
    planes_leg(Z, z, lambda t: (t, q), nb2s, nb2r, nb2_ss, nb2_rs)
    nb2r[z] = nb2s[x * Z + z]

    @pl.when(summing)
    def _():
        cr2[y] = cs2[y]
        ex_c2.recv()
        cs3[...] = total(cr2, Y).astype(BF16)
        ex_c3.start()
        cr3[z] = cs3[...]

    ex_g2 = []
    for k in range(parts):
        for one in ring[k][2:]:
            one.wait_recv()
        gs2[k] = (gs1[k, x].astype(F32) + grl[k].astype(F32) + grr[k].astype(F32)).astype(BF16)
        ex_g2.append(along_z(
            lambda t, k=k: gs2.at[k, t], lambda f, k=k: gr2.at[k, f], blocks(gr2.at[k], Z), g2_ss.at[k], g2_rs.at[k]))
        ex_g2[k].start()
        gr2[k, z] = gs2[k, z]

    @pl.when(summing)
    def _():
        ex_c3.recv()
        cfin[...] = total(cr3, Z).astype(BF16)
        ex_c4.start()
        ca4[y] = cfin[...]

    for k in range(parts):
        ex_g2[k].recv()
        gs3[:, :, k * span:(k + 1) * span] = total(gr2.at[k], Z).astype(BF16).reshape(YL, 16, span)

    def g3_copy(yl):
        return copy(gs3.at[yl], gr3.at[y], g3_ss.at[yl], g3_rs, z, (x * YL + yl) * C + c, x)

    for yl in range(YL):
        @pl.when(x * YL + yl != y)
        def _():
            g3_copy(yl).start()
    owning = y // YL == x

    @pl.when(summing)
    def _():
        some = ca4.at[pl.ds(0, nb - 1)]
        copy(some, some, c4_ss, c4_rs, z, q, x).wait_recv()

    @pl.when(jnp.logical_not(summing))
    def _():
        copy(ca4, ca4, c4_ss, c4_rs, z, q, x).wait_recv()

    ex_c5 = along_x(lambda t: ca4, lambda f: ca5.at[f], blocks(ca5, X), c5_ss, c5_rs)
    ex_c5.start()
    ca5[x] = ca4[...]

    planes_all(na2r, na2_ss, na2_rs).wait_recv()
    node_out[:, :xh] = dot(place_a[...], na2r[...].reshape(X * hop, xh)).astype(BF16)

    def g4_copy(xx, cc):
        return copy(gs4.at[cc], gr4.at[c], g4_ss.at[xx * C + cc], g4_rs.at[c], z, y * C + cc, xx)

    def g4_each(act):
        for xx in range(X):
            for cc in range(C):
                @pl.when(owning & jnp.logical_not((x == xx) & (c == cc)))
                def _():
                    act(xx, cc)

    @pl.when(owning)
    def _():
        gr3[y] = gs3[y % YL]
        copy(blocks(gr3, Y), blocks(gr3, Y), g3_ss.at[0], g3_rs, z, q, x).wait_recv()
        gs4[...] = total(gr3, Y).reshape(gs4.shape)
        gr4[c] = gs4[c]

    g4_each(lambda xx, cc: g4_copy(xx, cc).start())

    ex_c5.recv()
    c6 = to_sibling(ca5, ca6, c6_ss, c6_rs)
    c6.start()

    planes_all(nb2r, nb2_ss, nb2_rs).wait_recv()
    node_out[:, xh:] = dot(place_b[...], nb2r[...].reshape(X * hop, xh)).astype(BF16)

    for cc in range(C):
        @pl.when(jnp.logical_not(owning & (c == cc)))
        def _():
            copy(gs4.at[0], gr4.at[cc], g4_ss.at[0], g4_rs.at[cc], z, y * C + cc, y // YL).wait_recv()
        hidden_out[:, cc * DH:(cc + 1) * DH] = gr4[cc]

    c6.wait_recv()
    for t in range(X):
        ours, theirs = ca5[t].reshape(CP, cw), ca6[t].reshape(CP, cw)
        for cc in range(C):
            class_out[:, cc * HH + t * cw:cc * HH + (t + 1) * cw] = jnp.where(c == cc, ours, theirs)

    for ex in (ex_i1, ex_i2, ex_wx, ex_w2, ex_w3, *ex_fa1, *ex_fb1, *ex_fa2, *ex_fb2, ex_na1, ex_nb1, *ex_g2, ex_c1, ex_c5):
        ex.sent()
    w1_each(lambda t: w1_copy(t).wait_send())
    for one in (w4, ga, g0, c0, c6, *[leg for legs in ring for leg in legs]):
        one.wait_send()
    planes_all(na2r, na2_ss, na2_rs).wait_send()
    planes_all(nb2r, nb2_ss, nb2_rs).wait_send()

    @pl.when(summing)
    def _():
        some = cs2.at[pl.ds(0, nb - 1)]
        copy(some, some, c2_ss, c2_rs, z, q, x).wait_send()
        ex_c3.sent()
        ex_c4.sent()

    @pl.when(jnp.logical_not(summing))
    def _():
        copy(cs2, cs2, c2_ss, c2_rs, z, q, x).wait_send()

    for yl in range(YL):
        @pl.when(x * YL + yl != y)
        def _():
            g3_copy(yl).wait_send()
    g4_each(lambda xx, cc: g4_copy(xx, cc).wait_send())


def on_device(
    grid, features, hidden_weight, class_weight, request_ids, request_counts,
    outer_tiles, outer_masks, inner_tiles, inner_masks, labels,
):
    Z, Y, C, X = grid
    Q = Y * C
    NO = Z * Q
    cap = request_ids.shape[1]
    half = cap // 2
    rows, D = features.shape
    classes, HID = class_weight.shape
    tile = outer_masks.shape[2]
    hop = NO * half
    DH, HH, YL = D // 2, HID // 2, Y // X
    cb = 32 if classes > 32 else 8
    nb = -(-classes // cb)
    CP, cw = nb * cb, HID // (C * X)
    LW = max(Z * 8, 128)
    dims = (Z, Y, C, X, cap, tile, rows, classes)
    vm, dma = pltpu.VMEM, pltpu.SemaphoreType.DMA
    xh, nk, gk = HID // X // 2, DH // 128, 1
    scratch = [
        vm(features.shape, BF16), vm(outer_masks.shape, jnp.int32), vm(inner_masks.shape, jnp.int32),
        vm(class_weight.shape, BF16), vm(hidden_weight.shape, BF16),
        vm((cap, NO), jnp.int32), vm((2, NO), jnp.int32), vm((1, labels.shape[0]), jnp.int32),
        vm((8, NO), F32), vm((Z, 8, NO), F32), vm((Q, 8, LW), F32), vm((Q, 8, LW), F32),
        vm((X, Q * 8, LW), BF16), vm((rows, X * hop), BF16), vm((rows, X * hop), BF16),
        vm((16, DH), BF16), vm((C, 16, DH), BF16), vm((Z, X, C, 16, D), BF16),
        *[vm((nk, Z, cap * Q, DH // nk), BF16)] * 2, *[vm((nk, Q, cap * Z, DH // nk), BF16)] * 2,
        *[vm((nk, Q, cap * Z, DH // nk), BF16)] * 2, *[vm((nk, Z, cap * Q, DH // nk), BF16)] * 2,
        vm((cap * NO, cap * NO), BF16), vm((cap * NO, cap * NO), BF16), vm((hop, hop), BF16), vm((hop, hop), BF16),
        vm((2, hop, DH), BF16), vm((hop, DH), BF16), vm((hop, HID), F32), vm((HID, hop), BF16), vm((HID, hop), BF16),
        vm((hop, HID), BF16),
        *[vm((Z, Q * half, HH), BF16)] * 2, *[vm((X * Q, Z * half, xh), BF16)] * 2, *[vm((Q, Z * half, HH), BF16)] * 2,
        vm((X * Z, Q * half, xh), BF16), vm((X * Z, Q * half, xh), BF16),
        vm((gk, X, Z, YL * 16, DH // gk), BF16), *[vm((gk, Z // 2, YL * 16, DH // gk), BF16)] * 4,
        *[vm((gk, Z, YL * 16, DH // gk), BF16)] * 4,
        vm((YL, 16, DH), BF16), vm((Y, 16, DH), BF16), vm((C, 8, DH), F32), vm((C, 8, DH), F32),
        vm((CP, HH), F32), vm((CP, HH), BF16), vm((CP, HH), BF16),
        vm((X, CP, cw), BF16), vm((X, CP, cw), BF16), vm((nb, cb, cw), BF16), vm((Y, cb, cw), BF16),
        vm((cb, cw), BF16), vm((Z, cb, cw), BF16), vm((cb, cw), BF16), vm((nb, cb, cw), BF16),
        vm((X, nb, cb, cw), BF16), vm((X, nb, cb, cw), BF16),
        dma((8,)),
        *[dma] * 6,
        dma((Y,)), dma((C,)), *[dma] * 6,
        *[dma((nk,))] * 8, *[dma] * 8,
        *[dma] * 4, dma((gk, 6)), dma((gk, 6)), dma((gk,)), dma((gk,)), dma((YL,)), dma, dma((X * C,)), dma((C,)),
        *[dma] * 14,
    ]
    hbm = pl.BlockSpec(memory_space=pl.ANY)
    vmem = pl.BlockSpec(memory_space=pltpu.VMEM)
    smem = pl.BlockSpec(memory_space=pltpu.SMEM)
    hidden_grad, class_grad, node_grad = pl.pallas_call(
        functools.partial(kernel, dims),
        out_shape=(
            jax.ShapeDtypeStruct(hidden_weight.shape, F32),
            jax.ShapeDtypeStruct((CP, HID), BF16),
            jax.ShapeDtypeStruct((rows, HID // X), BF16),
        ),
        in_specs=[hbm, hbm, hbm, hbm, hbm, smem, hbm, smem, hbm, hbm],
        out_specs=(vmem, vmem, vmem),
        scratch_shapes=scratch,
        compiler_params=pltpu.CompilerParams(
            collective_id=0, has_side_effects=True, vmem_limit_bytes=56 * 1024 * 1024
        ),
        cost_estimate=pl.CostEstimate(flops=2_000_000_000, bytes_accessed=3_000_000, transcendentals=20_000),
    )(
        features, hidden_weight, class_weight, request_ids.T, request_counts.T,
        outer_tiles, outer_masks, inner_tiles, inner_masks, labels.reshape(1, -1),
    )
    return hidden_grad, class_grad[:classes].astype(F32), node_grad


def solution(mesh):
    grid = GRIDS[(mesh.shape["owner"], mesh.shape["rep"])]
    placed = (
        P("owner", None),
        P("owner", None),
        P(),
        P(("owner", "rep"), None),
        P(("owner", "rep"), None),
        P(("owner", "rep"), None),
        P(("owner", "rep"), None, None, None),
        P(("owner", "rep"), None),
        P(("owner", "rep"), None, None, None),
        P(("owner", "rep")),
    )
    return jax.shard_map(
        functools.partial(on_device, grid),
        mesh=mesh,
        in_specs=placed,
        out_specs=(P("owner", None), P(), P("owner", "rep")),
        check_vma=False,
    )
```

```python
import functools

import jax
import jax.numpy as jnp
from jax import lax
from jax.experimental import pallas as pl
from jax.experimental.pallas import tpu as pltpu
from jax.sharding import PartitionSpec as P

MESH = pl.DeviceIdType.MESH
F32 = jnp.float32
BF16 = jnp.bfloat16

GRIDS = {(128, 4): (8, 8, 2, 4), (32, 4): (2, 8, 2, 4)}


def iota(shape, dim):
    return lax.broadcasted_iota(jnp.int32, shape, dim)


def quo(a, n):
    return lax.shift_right_logical(a, jnp.full_like(a, n.bit_length() - 1))


def rem(a, n):
    return lax.bitwise_and(a, jnp.full_like(a, n - 1))


def flag(cond, dtype=BF16):
    return jnp.where(cond, 1.0, 0.0).astype(F32).astype(dtype)


def dot(a, b, ca=1, cb=0):
    return lax.dot_general(a, b, (((ca,), (cb,)), ((), ())), preferred_element_type=F32)


def regroup(outer, middle, inner, transpose=False):
    n = outer * middle * inner
    o, i = iota((n, n), 0), iota((n, n), 1)
    if transpose:
        o, i = i, o
    m, rest = quo(o, outer * inner), rem(o, outer * inner)
    a, b = quo(rest, inner), rem(rest, inner)
    return flag(i == a * (middle * inner) + m * inner + b)


def kernel(
    dims,
    feat_hbm, weight_hbm, cls_hbm, ids_hbm, counts_hbm, otile_ref, omask_hbm, itile_ref, imask_hbm, labels_hbm,
    hidden_out, class_out, node_out,
    feat, omask, imask, cls, weight_ref, ids_ref, counts_ref, labels_ref,
    i1s, i1r, i2s, i2r, wx, place_a, place_b,
    ws, wr, w_all,
    fa1s, fa1r, fa2s, fa2r, fb1s, fb1r, fb2s, fb2r, move_a, move_b, swap_a, swap_b,
    agg, agr, pre, pgt, pgtr, diff,
    na1s, na1r, na2s, na2r, nb1s, nb1r, nb2s, nb2r,
    gs1, gra, grb, gsa, gsb, grl, grr, gs2, gr2, gs3, gr3, gs4, gr4,
    cs1, cr1, cs2, cr2, cs3, cr3, cfin, ca4, ca5,
    local_sem,
    i1_ss, i1_rs, i2_ss, i2_rs, wx_ss, wx_rs,
    w1_ss, w1_rs, w2_ss, w2_rs, w3_ss, w3_rs, w4_ss, w4_rs,
    fa1_ss, fa1_rs, fa2_ss, fa2_rs, fb1_ss, fb1_rs, fb2_ss, fb2_rs,
    na1_ss, na1_rs, na2_ss, na2_rs, nb1_ss, nb1_rs, nb2_ss, nb2_rs,
    ga_ss, ga_rs, g0_ss, g0_rs, g1_ss, g1_rs, g2_ss, g2_rs, g3_ss, g3_rs, g4_ss, g4_rs,
    c1_ss, c1_rs, c2_ss, c2_rs, c3_ss, c3_rs, c4_ss, c4_rs, c5_ss, c5_rs,
):
    Z, Y, C, X, cap, tile, rows, classes = dims
    Q = Y * C
    NO = Z * Q
    half = cap // 2
    hop, front = NO * half, NO * cap
    D, HID = feat.shape[1], pre.shape[1]
    DH, HH = D // 2, HID // 2
    YL = Y // X
    nb, cb, cw = cs2.shape
    CP = nb * cb
    seeds = labels_ref.shape[1]
    row_blocks, col_blocks, K = hop // tile, front // tile, otile_ref.shape[1]
    LW = i2s.shape[2]
    S8 = 8

    me_o = lax.axis_index("owner")
    x = lax.axis_index("rep")
    z = me_o // Q
    q = me_o % Q
    y = q // C
    c = q % C
    sib = C - 1 - c

    def copy(src, dst, ss, rs, zz, qq, xx):
        return pltpu.make_async_remote_copy(
            src_ref=src, dst_ref=dst, send_sem=ss, recv_sem=rs,
            device_id=(zz * Q + qq, xx), device_id_type=MESH,
        )

    def each(n, body):
        def step(i, carry):
            body(i)
            return carry
        lax.fori_loop(1, n, step, 0)

    class Exchange:
        def __init__(self, n, me, at, src, dst, bulk, ss, rs):
            self.n, self.me, self.at, self.src, self.dst, self.bulk, self.ss, self.rs = n, me, at, src, dst, bulk, ss, rs

        def start(self):
            def send(d):
                to = lax.bitwise_and(self.me + d, self.n - 1)
                copy(self.src(to), self.dst(self.me), self.ss, self.rs, *self.at(to)).start()
            each(self.n, send)

        def all(self):
            return copy(self.bulk, self.bulk, self.ss, self.rs, *self.at(lax.bitwise_and(self.me + 1, self.n - 1)))

        def recv(self):
            self.all().wait_recv()

        def sent(self):
            self.all().wait_send()

    def along_z(*rest):
        return Exchange(Z, z, lambda t: (t, q, x), *rest)

    def along_q(*rest):
        return Exchange(Q, q, lambda t: (z, t, x), *rest)

    def along_y(*rest):
        return Exchange(Y, y, lambda t: (z, t * C + c, x), *rest)

    def along_x(*rest):
        return Exchange(X, x, lambda t: (z, q, t), *rest)

    def along_xz(*rest):
        return Exchange(X * Z, x * Z + z, lambda t: (lax.bitwise_and(t, Z - 1), q, t // Z), *rest)

    def along_xc(*rest):
        return Exchange(X * C, x * C + c, lambda t: (z, y * C + lax.bitwise_and(t, C - 1), t // C), *rest)

    def blocks(ref, n):
        return ref.at[pl.ds(0, n - 1)]

    def to_sibling(src, dst, ss, rs):
        return copy(src, dst, ss, rs, z, y * C + sib, x)

    staged = (
        (ids_hbm, ids_ref), (weight_hbm, weight_ref), (feat_hbm, feat), (counts_hbm, counts_ref),
        (omask_hbm, omask), (imask_hbm, imask), (labels_hbm, labels_ref), (cls_hbm, cls),
    )
    loads = [pltpu.make_async_copy(src, dst, local_sem.at[k]) for k, (src, dst) in enumerate(staged)]
    for load in loads:
        load.start()

    barrier = pltpu.get_barrier_semaphore()

    def greet(zz, qq, xx):
        pl.semaphore_signal(barrier, inc=1, device_id=(zz * Q + qq, xx), device_id_type=MESH)

    each(Z, lambda d: greet(lax.bitwise_and(z + d, Z - 1), q, x))
    each(Q, lambda d: greet(z, lax.bitwise_and(q + d, Q - 1), x))
    each(X, lambda d: greet(z, q, lax.bitwise_and(x + d, X - 1)))

    i1s[...] = jnp.zeros_like(i1s)
    for load in loads[:2]:
        load.wait()
    i1s[0:cap, :] = ids_ref[...].astype(F32)
    w32 = weight_ref[...].astype(F32)
    ws[...] = jnp.concatenate([w32[:, :DH], w32[:, DH:]], axis=0).astype(BF16)

    pl.semaphore_wait(barrier, (Z - 1) + (Q - 1) + (X - 1))

    ex_i1 = along_z(lambda t: i1s, lambda f: i1r.at[f], blocks(i1r, Z), i1_ss, i1_rs)
    ex_i1.start()
    i1r[z] = i1s[...]

    w_core = y % C

    def w1_copy(t):
        return copy(ws, wr.at[c], w1_ss.at[t], w1_rs.at[c], z, t * C + w_core, x)

    def w1_each(act):
        def step(t, carry):
            @pl.when((y // C == x) & jnp.logical_not((t == y) & (w_core == c)))
            def _():
                act(t)
            return carry
        lax.fori_loop(0, Y, step, 0)

    w1_each(lambda t: w1_copy(t).start())
    y_mine = x * C + c

    ex_i1.recv()
    marks = flag(iota((Q, NO), 1) == z * Q + iota((Q, NO), 0))
    asked = i1r[...].reshape(Z * S8, NO).astype(BF16)
    if LW > Z * S8:
        asked = jnp.concatenate([asked] * (LW // (Z * S8)), axis=0)
    for_q = dot(marks, asked, 1, 1)
    for k in range(Q):
        i2s[k] = jnp.broadcast_to(for_q[k:k + 1, :], (8, LW))
    ex_i2 = along_q(lambda t: i2s.at[t], lambda f: i2r.at[f], blocks(i2r, Q), i2_ss, i2_rs)
    ex_i2.start()
    i2r[q] = i2s[q]

    for c0 in range(C):
        own = (y == y_mine) & (c == c0)

        @pl.when(own)
        def _():
            wr[c0] = ws[...]

        @pl.when(jnp.logical_not(own))
        def _():
            copy(ws, wr.at[c0], w1_ss.at[0], w1_rs.at[c0], z, y_mine * C + c0, x).wait_recv()
    for hcol in range(2):
        cols = slice(hcol * DH, (hcol + 1) * DH)
        w_all[z, x, c, :, cols] = jnp.concatenate(
            [wr[c0, hcol * 8:(hcol + 1) * 8, :].astype(F32) for c0 in range(C)], axis=0
        ).astype(BF16)
    ex_w2 = along_z(
        lambda t: w_all.at[z, x, c], lambda f: w_all.at[f, x, c], w_all.at[pl.ds(0, Z - 1), x, c], w2_ss, w2_rs
    )
    ex_w2.start()

    loads[2].wait()
    lane_q = iota((front, Q * 8), 1)

    ex_i2.recv()
    wanted = i2r[...].reshape(Q * 8, LW).astype(BF16)

    wx[x] = wanted
    ex_wx = along_x(lambda t: wx.at[x], lambda f: wx.at[f], blocks(wx, X), wx_ss, wx_rs)

    def picked(col_of, q_of):
        spread = dot(flag(iota((front, LW), 1) == col_of), wanted, 1, 1)
        ids = jnp.sum(jnp.where(lane_q == q_of * 8, spread, 0.0), axis=1, keepdims=True)
        return flag(ids == iota((front, rows), 1).astype(F32))

    chunks, wide = fa1s.shape[0], fa1s.shape[3]
    r = iota((front, 1), 0)
    pick_a = picked(quo(r, cap * Q) * S8 + quo(rem(r, cap * Q), Q), rem(r, Q))

    def column_blocks(first):
        return jnp.concatenate([feat[:, b * wide:(b + 1) * wide] for b in range(first, 2 * chunks, 2)], axis=1)

    rows_a = dot(pick_a, column_blocks(0)).astype(BF16)
    ex_fa1, ex_fb1, ex_fa2, ex_fb2 = [], [], [], []
    for k in range(chunks):
        at = slice(k * wide, (k + 1) * wide)
        fa1s[k] = rows_a[:, at].reshape(fa1s.shape[1:])
        ex_fa1.append(along_z(
            lambda t, k=k: fa1s.at[k, t], lambda f, k=k: fa1r.at[k, f], blocks(fa1r.at[k], Z), fa1_ss.at[k], fa1_rs.at[k]))
        ex_fb1.append(along_q(
            lambda t, k=k: fb1s.at[k, t], lambda f, k=k: fb1r.at[k, f], blocks(fb1r.at[k], Q), fb1_ss.at[k], fb1_rs.at[k]))
        ex_fa2.append(along_q(
            lambda t, k=k: fa2s.at[k, t], lambda f, k=k: fa2r.at[k, f], blocks(fa2r.at[k], Q), fa2_ss.at[k], fa2_rs.at[k]))
        ex_fb2.append(along_z(
            lambda t, k=k: fb2s.at[k, t], lambda f, k=k: fb2r.at[k, f], blocks(fb2r.at[k], Z), fb2_ss.at[k], fb2_rs.at[k]))
    ex_fa1[0].start()
    pick_b = picked(rem(r, Z) * S8 + quo(rem(r, cap * Z), Z), quo(r, cap * Z))
    rows_b = dot(pick_b, column_blocks(1)).astype(BF16)
    for k in range(chunks):
        at = slice(k * wide, (k + 1) * wide)
        fb1s[k] = rows_b[:, at].reshape(fb1s.shape[1:])
    ex_fb1[0].start()
    for k in range(1, chunks):
        ex_fa1[k].start()
        ex_fb1[k].start()
    for k in range(chunks):
        fa1r[k, z] = fa1s[k, z]
        fb1r[k, q] = fb1s[k, q]
    ex_wx.start()
    move_a[...] = regroup(Z * cap, Q, 1)
    move_b[...] = regroup(Q * cap, Z, 1)

    ex_w2.recv()
    ex_w3 = along_x(
        lambda t: w_all.at[:, x, c], lambda f: w_all.at[:, f, c], w_all.at[:, pl.ds(0, X - 1), c], w3_ss, w3_rs
    )
    ex_w3.start()

    for load in loads[3:]:
        load.wait()
    counts = counts_ref[...].astype(F32)
    counts8 = jnp.concatenate([counts, jnp.zeros((6, NO), F32)], axis=0).astype(BF16)

    def validity(slots):
        n = NO * slots
        at = iota((NO, n), 1)
        per = dot(counts8, flag(iota((NO, n), 0) == quo(at, slots)))
        j = rem(iota((1, n), 1), slots).astype(F32)
        first = flag(j < per[0:1, :], F32)
        second = flag(j - half < per[1:2, :], F32)
        return jnp.where(j < half, first, second)

    valid = validity(cap)
    outer_rows = []
    for b in range(row_blocks):
        tiles = []
        for cbk in range(col_blocks):
            m = jnp.zeros((tile, tile), jnp.int32)
            for k in range(K):
                m = m + omask[b, k] * (otile_ref[b, k] == cbk).astype(jnp.int32)
            tiles.append(m.astype(F32) * valid[:, cbk * tile:(cbk + 1) * tile])
        outer_rows.append(jnp.concatenate(tiles, axis=1))
    outer = jnp.concatenate(outer_rows, axis=0)
    outer_scale = 1.0 + jnp.sum(outer, axis=1, keepdims=True)
    oi, oc = iota((hop, front), 0), iota((hop, front), 1)
    self_col = quo(oi, half) * cap + rem(oi, half)
    outer_self = (outer + flag(oc == self_col, F32)).astype(BF16)
    outer_a = dot(outer_self, regroup(Z, Q, cap, transpose=True)).astype(BF16)

    hop_valid = validity(half)
    tiles = []
    for cbk in range(row_blocks):
        m = jnp.zeros((tile, tile), jnp.int32)
        for k in range(K):
            m = m + imask[0, k] * (itile_ref[0, k] == cbk).astype(jnp.int32)
        tiles.append(m.astype(F32) * hop_valid[:, cbk * tile:(cbk + 1) * tile])
    inner32 = jnp.concatenate(tiles, axis=1)
    inner_degree = jnp.maximum(jnp.sum(inner32, axis=1, keepdims=True), 1.0)
    inner = inner32.astype(BF16)
    inner_twice = jnp.concatenate([inner32.T, inner32.T], axis=1).astype(BF16)

    label_row = labels_ref[...]
    label_col = jnp.sum(
        jnp.where(iota((seeds, seeds), 0) == iota((seeds, seeds), 1), label_row, 0), axis=1, keepdims=True
    )
    one_hot = flag(label_col == iota((seeds, classes), 1), F32)

    for k in range(chunks):
        ex_fa1[k].recv()
        fa2s[k] = dot(move_a[...], fa1r[k].reshape(front, wide)).astype(BF16).reshape(fa2s.shape[1:])
        ex_fa2[k].start()
        fa2r[k, q] = fa2s[k, q]
        ex_fb1[k].recv()
        fb2s[k] = dot(move_b[...], fb1r[k].reshape(front, wide)).astype(BF16).reshape(fb2s.shape[1:])
        ex_fb2[k].start()
        fb2r[k, z] = fb2s[k, z]

    ex_w3.recv()
    w4 = to_sibling(w_all.at[:, :, c], w_all.at[:, :, c], w4_ss, w4_rs)
    w4_in = to_sibling(w_all.at[:, :, sib], w_all.at[:, :, sib], w4_ss, w4_rs)
    w4.start()

    swap_a[...] = regroup(Z, Q, half)
    swap_b[...] = regroup(Q, Z, half)
    ex_wx.recv()

    def places(x_of, j_of, z_of, q_of):
        n = X * hop
        pick = flag(iota((LW, n), 0) == z_of * S8 + j_of)
        ids = jnp.zeros((1, n), F32)
        for k in range(X):
            here = (iota((Q * 8, n), 0) == q_of * 8) & (x_of == k)
            ids = ids + jnp.sum(jnp.where(here, dot(wx[k], pick), 0.0), axis=0, keepdims=True)
        return flag(iota((rows, n), 0).astype(F32) == ids)

    s = iota((1, X * hop), 1)
    def plane(d):
        return lax.bitwise_and(x + X - d, jnp.full_like(d, X - 1))

    place_a[...] = places(
        plane(rem(quo(s, half * Z), X)), rem(s, half), rem(quo(s, half), Z), quo(s, half * Z * X)
    )
    place_b[...] = places(
        plane(quo(s, half * Q * Z)), rem(s, half), rem(quo(s, half * Q), Z), rem(quo(s, half), Q)
    )

    for k in range(chunks):
        ex_fa2[k].recv()
        part_a = (dot(outer_a, fa2r[k].reshape(front, wide)) / outer_scale).astype(BF16)
        ex_fb2[k].recv()
        part_b = (dot(outer_self, fb2r[k].reshape(front, wide)) / outer_scale).astype(BF16)
        for b, part in ((2 * k, part_a), (2 * k + 1, part_b)):
            agg[b // chunks, :, (b % chunks) * wide:(b % chunks + 1) * wide] = part
        if k == 0:
            w4_in.wait_recv()
        part = dot(
            jnp.concatenate([part_a, part_b], axis=1),
            w_all[:, :, :, :, 2 * k * wide:2 * (k + 1) * wide].reshape(HID, 2 * wide), 1, 1)
        pre[...] = part if k == 0 else pre[...] + part
    ga = to_sibling(agg.at[sib], agr, ga_ss, ga_rs)
    ga.start()

    hidden = jnp.maximum(pre[...], 0.0).astype(BF16)
    agg_two = (dot(inner, hidden) / inner_degree).astype(BF16)
    logits = dot(agg_two, cls[...], 1, 1)
    exponent = jnp.exp(logits - jnp.max(logits, axis=1, keepdims=True))
    softmax = exponent / jnp.sum(exponent, axis=1, keepdims=True)
    logit_grad = ((softmax - one_hot) / seeds).astype(BF16)
    widen = flag(iota((classes, CP), 0) == iota((classes, CP), 1))
    class_rows = dot(dot(logit_grad, widen).astype(BF16), agg_two, 0, 0).astype(BF16)
    for t in range(X):
        for cc in range(C):
            cs1[t * C + cc] = class_rows[:, cc * HH + t * cw:cc * HH + (t + 1) * cw]
    me_xc = x * C + c
    ex_c1 = along_xc(lambda t: cs1.at[t], lambda f: cr1.at[f], blocks(cr1, X * C), c1_ss, c1_rs)
    ex_c1.start()
    cr1[me_xc] = cs1[me_xc]

    agg_grad = dot(logit_grad, cls[...]) / inner_degree
    high = agg_grad.astype(BF16)
    low = (agg_grad - high.astype(F32)).astype(BF16)
    hidden_diff = dot(inner_twice, jnp.concatenate([high, low], axis=0))
    pgt[...] = jnp.where(pre[...] > 0.0, hidden_diff, 0.0).T.astype(BF16)
    g0 = to_sibling(pgt, pgtr, g0_ss, g0_rs)
    g0.start()
    diff[...] = hidden_diff.astype(BF16)

    def total(ref, n):
        acc = ref[0].astype(F32)
        for k in range(1, n):
            acc = acc + ref[k].astype(F32)
        return acc

    gmine = dot(pgt[...], agg[c])
    ga.wait_recv()
    g0.wait_recv()
    gmine = (gmine + dot(pgtr[...], agr[...])).astype(BF16).reshape(Z, X, YL * 16, DH)
    parts, span = gs1.shape[0], gs1.shape[4]
    for k in range(parts):
        for t in range(X):
            gs1[k, t] = gmine[:, t, :, k * span:(k + 1) * span]
    right, left, across = (lax.bitwise_and(x + d, X - 1) for d in (1, X - 1, 2))
    lower, upper = pl.ds(0, Z // 2), pl.ds(Z // 2, Z // 2)

    def g1(k, n, src, dst, to):
        return copy(src, dst, g1_ss.at[k, n], g1_rs.at[k, n], z, q, to)

    ring = [(
        g1(k, 0, gs1.at[k, across, lower], gra.at[k], right), g1(k, 1, gs1.at[k, across, upper], grb.at[k], left),
        g1(k, 2, gs1.at[k, right, upper], grl.at[k, upper], right), g1(k, 3, gs1.at[k, left, lower], grr.at[k, lower], left),
        g1(k, 4, gsa.at[k], grl.at[k, lower], right), g1(k, 5, gsb.at[k], grr.at[k, upper], left),
    ) for k in range(parts)]
    for k in range(parts):
        for one in ring[k][:4]:
            one.start()

    xw = HID // X
    xh = xw // 2

    def xz_leg(src, dst, ss, rs):
        def send(t):
            d, zz = t // Z, lax.bitwise_and(z + t, Z - 1)
            copy(src(d, zz), dst.at[d * Z + z], ss, rs, zz, q, lax.bitwise_and(x + d, X - 1)).start()
        each(X * Z, send)

    def wait_blocks(ref, n, ss, rs):
        some = ref.at[pl.ds(0, n)]
        return copy(some, some, ss, rs, z, q, lax.bitwise_and(x + 1, X - 1))

    for t in range(X):
        na1s[t * Z:(t + 1) * Z] = diff[:, t * xw:t * xw + xh].reshape(Z, Q * half, xh)
    xz_leg(lambda d, zz: na1s.at[lax.bitwise_and(x + d, X - 1) * Z + zz], na1r, na1_ss, na1_rs)
    second = jnp.concatenate([
        diff[:, pl.ds(pl.multiple_of(lax.bitwise_and(x + d, X - 1) * xw + xh, xh), xh)] for d in range(X)
    ], axis=1)
    nb1s[...] = dot(swap_a[...], second).astype(BF16).reshape(nb1s.shape)
    ex_nb1 = along_q(lambda t: nb1s.at[t], lambda f: nb1r.at[f], blocks(nb1r, Q), nb1_ss, nb1_rs)
    ex_nb1.start()
    ex_na2 = along_q(lambda t: na2s.at[t], lambda f: na2r.at[f], blocks(na2r, Q), na2_ss, na2_rs)
    na1r[z] = na1s[x * Z + z]
    nb1r[q] = nb1s[q]

    ex_c1.recv()
    cs2[...] = total(cr1, X * C).astype(BF16).reshape(cs2.shape)

    def to_blocks(act):
        def step(t, carry):
            @pl.when(t != y)
            def _():
                act(t)
            return carry
        lax.fori_loop(0, nb, step, 0)

    to_blocks(lambda t: copy(cs2.at[t], cr2.at[y], c2_ss, c2_rs, z, t * C + c, x).start())
    summing = y < nb
    ex_c2 = along_y(None, None, blocks(cr2, Y), c2_ss, c2_rs)
    ex_c3 = along_z(lambda t: cs3, lambda f: cr3.at[f], blocks(cr3, Z), c3_ss, c3_rs)
    ex_c4 = along_y(lambda t: cfin, lambda f: ca4.at[f], blocks(cr2, Y), c4_ss, c4_rs)

    for k in range(parts):
        r1, l1, r2, l2, r3, l3 = ring[k]
        r1.wait_recv()
        gsa[k] = (gs1[k, right, lower].astype(F32) + gra[k].astype(F32)).astype(BF16)
        r3.start()
        l1.wait_recv()
        gsb[k] = (gs1[k, left, upper].astype(F32) + grb[k].astype(F32)).astype(BF16)
        l3.start()

    @pl.when(summing)
    def _():
        cr2[y] = cs2[y]
        ex_c2.recv()
        cs3[...] = total(cr2, Y).astype(BF16)
        ex_c3.start()
        cr3[z] = cs3[...]

    ex_g2 = []
    for k in range(parts):
        for one in ring[k][2:]:
            one.wait_recv()
        gs2[k] = (gs1[k, x].astype(F32) + grl[k].astype(F32) + grr[k].astype(F32)).astype(BF16)
        ex_g2.append(along_z(
            lambda t, k=k: gs2.at[k, t], lambda f, k=k: gr2.at[k, f], blocks(gr2.at[k], Z), g2_ss.at[k], g2_rs.at[k]))
        ex_g2[k].start()
        gr2[k, z] = gs2[k, z]

    wait_blocks(na1r, X * Z - 1, na1_ss, na1_rs).wait_recv()
    came = jnp.concatenate([na1r[d * Z:(d + 1) * Z].reshape(hop, xh) for d in range(X)], axis=1)
    came = dot(swap_a[...], came).astype(BF16)
    for d in range(X):
        na2s[:, d] = came[:, d * xh:(d + 1) * xh].reshape(Q, Z * half, xh)
    ex_na2.start()
    na2r[q] = na2s[q]
    @pl.when(summing)
    def _():
        ex_c3.recv()
        cfin[...] = total(cr3, Z).astype(BF16)
        ex_c4.start()
        ca4[y] = cfin[...]

    ex_nb1.recv()
    came = dot(swap_b[...], nb1r[...].reshape(hop, X * xh)).astype(BF16)
    for d in range(X):
        nb2s[d * Z:(d + 1) * Z] = came[:, d * xh:(d + 1) * xh].reshape(Z, Q * half, xh)
    xz_leg(lambda d, zz: nb2s.at[d * Z + zz], nb2r, nb2_ss, nb2_rs)
    nb2r[z] = nb2s[z]

    @pl.when(summing)
    def _():
        some = ca4.at[pl.ds(0, nb - 1)]
        copy(some, some, c4_ss, c4_rs, z, q, x).wait_recv()

    @pl.when(jnp.logical_not(summing))
    def _():
        copy(ca4, ca4, c4_ss, c4_rs, z, q, x).wait_recv()

    ex_c5 = along_xc(lambda t: ca4, lambda f: ca5.at[f], blocks(ca5, X * C), c5_ss, c5_rs)
    ex_c5.start()
    ca5[me_xc] = ca4[...]

    for k in range(parts):
        ex_g2[k].recv()
        gs3[:, :, k * span:(k + 1) * span] = total(gr2.at[k], Z).astype(BF16).reshape(YL, 16, span)

    def g3_copy(yl):
        return copy(gs3.at[yl], gr3.at[y], g3_ss.at[yl], g3_rs, z, (x * YL + yl) * C + c, x)

    for yl in range(YL):
        @pl.when(x * YL + yl != y)
        def _():
            g3_copy(yl).start()
    owning = y // YL == x

    ex_na2.recv()
    node_out[:, :xh] = dot(place_a[...], na2r[...].reshape(X * hop, xh)).astype(BF16)

    def g4_copy(xx, cc):
        return copy(gs4.at[cc], gr4.at[c], g4_ss.at[xx * C + cc], g4_rs.at[c], z, y * C + cc, xx)

    def g4_each(act):
        for xx in range(X):
            for cc in range(C):
                @pl.when(owning & jnp.logical_not((x == xx) & (c == cc)))
                def _():
                    act(xx, cc)

    @pl.when(owning)
    def _():
        gr3[y] = gs3[y % YL]
        copy(blocks(gr3, Y), blocks(gr3, Y), g3_ss.at[0], g3_rs, z, q, x).wait_recv()
        gs4[...] = total(gr3, Y).reshape(gs4.shape)
        gr4[c] = gs4[c]

    g4_each(lambda xx, cc: g4_copy(xx, cc).start())

    wait_blocks(nb2r, X * Z - 1, nb2_ss, nb2_rs).wait_recv()
    node_out[:, xh:] = dot(place_b[...], nb2r[...].reshape(X * hop, xh)).astype(BF16)

    ex_c5.recv()
    for t in range(X):
        for cc in range(C):
            class_out[:, cc * HH + t * cw:cc * HH + (t + 1) * cw] = ca5[t * C + cc].reshape(CP, cw)

    for cc in range(C):
        @pl.when(jnp.logical_not(owning & (c == cc)))
        def _():
            copy(gs4.at[0], gr4.at[cc], g4_ss.at[0], g4_rs.at[cc], z, y * C + cc, y // YL).wait_recv()
        hidden_out[:, cc * DH:(cc + 1) * DH] = gr4[cc]

    for ex in (ex_i1, ex_i2, ex_wx, ex_w2, ex_w3, *ex_fa1, *ex_fb1, *ex_fa2, *ex_fb2, ex_nb1, ex_na2, *ex_g2, ex_c1, ex_c5):
        ex.sent()
    w1_each(lambda t: w1_copy(t).wait_send())
    for one in (w4, ga, g0, *[leg for legs in ring for leg in legs]):
        one.wait_send()
    wait_blocks(na1r, X * Z - 1, na1_ss, na1_rs).wait_send()
    wait_blocks(nb2r, X * Z - 1, nb2_ss, nb2_rs).wait_send()

    @pl.when(summing)
    def _():
        some = cs2.at[pl.ds(0, nb - 1)]
        copy(some, some, c2_ss, c2_rs, z, q, x).wait_send()
        ex_c3.sent()
        ex_c4.sent()

    @pl.when(jnp.logical_not(summing))
    def _():
        copy(cs2, cs2, c2_ss, c2_rs, z, q, x).wait_send()

    for yl in range(YL):
        @pl.when(x * YL + yl != y)
        def _():
            g3_copy(yl).wait_send()
    g4_each(lambda xx, cc: g4_copy(xx, cc).wait_send())


def on_device(
    grid, features, hidden_weight, class_weight, request_ids, request_counts,
    outer_tiles, outer_masks, inner_tiles, inner_masks, labels,
):
    Z, Y, C, X = grid
    Q = Y * C
    NO = Z * Q
    cap = request_ids.shape[1]
    half = cap // 2
    rows, D = features.shape
    classes, HID = class_weight.shape
    tile = outer_masks.shape[2]
    hop = NO * half
    DH, HH, YL = D // 2, HID // 2, Y // X
    cb = 32 if classes > 32 else 8
    nb = -(-classes // cb)
    CP, cw = nb * cb, HID // (C * X)
    LW = max(Z * 8, 128)
    dims = (Z, Y, C, X, cap, tile, rows, classes)
    vm, dma = pltpu.VMEM, pltpu.SemaphoreType.DMA
    xh, nk, gk = HID // X // 2, DH // 128, 1
    scratch = [
        vm(features.shape, BF16), vm(outer_masks.shape, jnp.int32), vm(inner_masks.shape, jnp.int32),
        vm(class_weight.shape, BF16), vm(hidden_weight.shape, BF16),
        vm((cap, NO), jnp.int32), vm((2, NO), jnp.int32), vm((1, labels.shape[0]), jnp.int32),
        vm((8, NO), F32), vm((Z, 8, NO), F32), vm((Q, 8, LW), F32), vm((Q, 8, LW), F32),
        vm((X, Q * 8, LW), BF16), vm((rows, X * hop), BF16), vm((rows, X * hop), BF16),
        vm((16, DH), BF16), vm((C, 16, DH), BF16), vm((Z, X, C, 16, D), BF16),
        *[vm((nk, Z, cap * Q, DH // nk), BF16)] * 2, *[vm((nk, Q, cap * Z, DH // nk), BF16)] * 2,
        *[vm((nk, Q, cap * Z, DH // nk), BF16)] * 2, *[vm((nk, Z, cap * Q, DH // nk), BF16)] * 2,
        vm((cap * NO, cap * NO), BF16), vm((cap * NO, cap * NO), BF16), vm((hop, hop), BF16), vm((hop, hop), BF16),
        vm((2, hop, DH), BF16), vm((hop, DH), BF16), vm((hop, HID), F32), vm((HID, hop), BF16), vm((HID, hop), BF16),
        vm((hop, HID), BF16),
        vm((X * Z, Q * half, xh), BF16), vm((X * Z, Q * half, xh), BF16),
        *[vm((Q, X, Z * half, xh), BF16)] * 2, *[vm((Q, Z * half, HH), BF16)] * 2,
        vm((X * Z, Q * half, xh), BF16), vm((X * Z, Q * half, xh), BF16),
        vm((gk, X, Z, YL * 16, DH // gk), BF16), *[vm((gk, Z // 2, YL * 16, DH // gk), BF16)] * 4,
        *[vm((gk, Z, YL * 16, DH // gk), BF16)] * 4,
        vm((YL, 16, DH), BF16), vm((Y, 16, DH), BF16), vm((C, 8, DH), F32), vm((C, 8, DH), F32),
        vm((X * C, CP, cw), BF16), vm((X * C, CP, cw), BF16), vm((nb, cb, cw), BF16), vm((Y, cb, cw), BF16),
        vm((cb, cw), BF16), vm((Z, cb, cw), BF16), vm((cb, cw), BF16), vm((nb, cb, cw), BF16),
        vm((X * C, nb, cb, cw), BF16),
        dma((8,)),
        *[dma] * 6,
        dma((Y,)), dma((C,)), *[dma] * 6,
        *[dma((nk,))] * 8, *[dma] * 8,
        *[dma] * 4, dma((gk, 6)), dma((gk, 6)), dma((gk,)), dma((gk,)), dma((YL,)), dma, dma((X * C,)), dma((C,)),
        *[dma] * 10,
    ]
    hbm = pl.BlockSpec(memory_space=pl.ANY)
    vmem = pl.BlockSpec(memory_space=pltpu.VMEM)
    smem = pl.BlockSpec(memory_space=pltpu.SMEM)
    hidden_grad, class_grad, node_grad = pl.pallas_call(
        functools.partial(kernel, dims),
        out_shape=(
            jax.ShapeDtypeStruct(hidden_weight.shape, F32),
            jax.ShapeDtypeStruct((CP, HID), BF16),
            jax.ShapeDtypeStruct((rows, HID // X), BF16),
        ),
        in_specs=[hbm, hbm, hbm, hbm, hbm, smem, hbm, smem, hbm, hbm],
        out_specs=(vmem, vmem, vmem),
        scratch_shapes=scratch,
        compiler_params=pltpu.CompilerParams(
            collective_id=0, has_side_effects=True, vmem_limit_bytes=56 * 1024 * 1024
        ),
        cost_estimate=pl.CostEstimate(flops=2_000_000_000, bytes_accessed=3_000_000, transcendentals=20_000),
    )(
        features, hidden_weight, class_weight, request_ids.T, request_counts.T,
        outer_tiles, outer_masks, inner_tiles, inner_masks, labels.reshape(1, -1),
    )
    return hidden_grad, class_grad[:classes].astype(F32), node_grad


def solution(mesh):
    grid = GRIDS[(mesh.shape["owner"], mesh.shape["rep"])]
    placed = (
        P("owner", None),
        P("owner", None),
        P(),
        P(("owner", "rep"), None),
        P(("owner", "rep"), None),
        P(("owner", "rep"), None),
        P(("owner", "rep"), None, None, None),
        P(("owner", "rep"), None),
        P(("owner", "rep"), None, None, None),
        P(("owner", "rep")),
    )
    return jax.shard_map(
        functools.partial(on_device, grid),
        mesh=mesh,
        in_specs=placed,
        out_specs=(P("owner", None), P(), P("owner", "rep")),
        check_vma=False,
    )
```

```python
import functools

import jax
import jax.numpy as jnp
from jax import lax
from jax.experimental import pallas as pl
from jax.experimental.pallas import tpu as pltpu
from jax.sharding import PartitionSpec as P

MESH = pl.DeviceIdType.MESH
F32 = jnp.float32
BF16 = jnp.bfloat16

GRIDS = {(128, 4): (8, 8, 2, 4), (32, 4): (2, 8, 2, 4)}


def iota(shape, dim):
    return lax.broadcasted_iota(jnp.int32, shape, dim)


def quo(a, n):
    return lax.shift_right_logical(a, jnp.full_like(a, n.bit_length() - 1))


def rem(a, n):
    return lax.bitwise_and(a, jnp.full_like(a, n - 1))


def flag(cond, dtype=BF16):
    return jnp.where(cond, 1.0, 0.0).astype(F32).astype(dtype)


def dot(a, b, ca=1, cb=0):
    return lax.dot_general(a, b, (((ca,), (cb,)), ((), ())), preferred_element_type=F32)


def regroup(outer, middle, inner, transpose=False):
    n = outer * middle * inner
    o, i = iota((n, n), 0), iota((n, n), 1)
    if transpose:
        o, i = i, o
    m, rest = quo(o, outer * inner), rem(o, outer * inner)
    a, b = quo(rest, inner), rem(rest, inner)
    return flag(i == a * (middle * inner) + m * inner + b)


def kernel(
    dims,
    feat_hbm, weight_hbm, cls_hbm, ids_hbm, counts_hbm, otile_ref, omask_hbm, itile_ref, imask_hbm, labels_hbm,
    hidden_out, class_out, node_out,
    feat, omask, imask, cls, weight_ref, ids_ref, counts_ref, labels_ref,
    i1s, i1r, i2s, i2r, wx, place_a, place_b,
    ws, wr, w_all,
    fa1s_0, fa1s_1, fa1r_0, fa1r_1, fb1s_0, fb1s_1, fb1r_0, fb1r_1,
    fa2s_0, fa2s_1, fa2r_0, fa2r_1, fb2s_0, fb2s_1, fb2r_0, fb2r_1, move_a, move_b, swap_a, swap_b,
    agg, agr, pre, pgt, pgtr, diff,
    na1s, na1r, na2s, na2r, nb1s, nb1r, nb2s, nb2r,
    gs1, gra, grb, gsa, gsb, grl, grr, gs2, gr2, gs3, gr3, gs4, gr4,
    cs1, cr1, cs2, cr2, cs3, cr3, cfin, ca4, ca5,
    local_sem,
    i1_ss, i1_rs, i2_ss, i2_rs, wx_ss, wx_rs,
    w1_ss, w1_rs, w2_ss, w2_rs, w3_ss, w3_rs, w4_ss, w4_rs,
    fa1_ss, fa1_rs, fa2_ss, fa2_rs, fb1_ss, fb1_rs, fb2_ss, fb2_rs,
    na1_ss, na1_rs, na2_ss, na2_rs, nb1_ss, nb1_rs, nb2_ss, nb2_rs,
    ga_ss, ga_rs, g0_ss, g0_rs, g1_ss, g1_rs, g2_ss, g2_rs, g3_ss, g3_rs, g4_ss, g4_rs,
    c1_ss, c1_rs, c2_ss, c2_rs, c3_ss, c3_rs, c4_ss, c4_rs, c5_ss, c5_rs,
):
    Z, Y, C, X, cap, tile, rows, classes = dims
    Q = Y * C
    NO = Z * Q
    half = cap // 2
    hop, front = NO * half, NO * cap
    D, HID = feat.shape[1], pre.shape[1]
    DH, HH = D // 2, HID // 2
    YL = Y // X
    nb, cb, cw = cs2.shape
    CP = nb * cb
    seeds = labels_ref.shape[1]
    row_blocks, col_blocks, K = hop // tile, front // tile, otile_ref.shape[1]
    LW = i2s.shape[2]
    S8 = 8

    me_o = lax.axis_index("owner")
    x = lax.axis_index("rep")
    z = me_o // Q
    q = me_o % Q
    y = q // C
    c = q % C
    sib = C - 1 - c

    def copy(src, dst, ss, rs, zz, qq, xx):
        return pltpu.make_async_remote_copy(
            src_ref=src, dst_ref=dst, send_sem=ss, recv_sem=rs,
            device_id=(zz * Q + qq, xx), device_id_type=MESH,
        )

    def each(n, body):
        def step(i, carry):
            body(i)
            return carry
        lax.fori_loop(1, n, step, 0)

    class Exchange:
        def __init__(self, n, me, at, src, dst, bulk, ss, rs):
            self.n, self.me, self.at, self.src, self.dst, self.bulk, self.ss, self.rs = n, me, at, src, dst, bulk, ss, rs

        def start(self):
            def send(d):
                to = lax.bitwise_and(self.me + d, self.n - 1)
                copy(self.src(to), self.dst(self.me), self.ss, self.rs, *self.at(to)).start()
            each(self.n, send)

        def all(self):
            return copy(self.bulk, self.bulk, self.ss, self.rs, *self.at(lax.bitwise_and(self.me + 1, self.n - 1)))

        def recv(self):
            self.all().wait_recv()

        def sent(self):
            self.all().wait_send()

    def along_z(*rest):
        return Exchange(Z, z, lambda t: (t, q, x), *rest)

    def along_q(*rest):
        return Exchange(Q, q, lambda t: (z, t, x), *rest)

    def along_y(*rest):
        return Exchange(Y, y, lambda t: (z, t * C + c, x), *rest)

    def along_x(*rest):
        return Exchange(X, x, lambda t: (z, q, t), *rest)

    def along_xz(*rest):
        return Exchange(X * Z, x * Z + z, lambda t: (lax.bitwise_and(t, Z - 1), q, t // Z), *rest)

    def along_xc(*rest):
        return Exchange(X * C, x * C + c, lambda t: (z, y * C + lax.bitwise_and(t, C - 1), t // C), *rest)

    def blocks(ref, n):
        return ref.at[pl.ds(0, n - 1)]

    def to_sibling(src, dst, ss, rs):
        return copy(src, dst, ss, rs, z, y * C + sib, x)

    staged = (
        (ids_hbm, ids_ref), (weight_hbm, weight_ref), (feat_hbm, feat), (counts_hbm, counts_ref),
        (omask_hbm, omask), (imask_hbm, imask), (labels_hbm, labels_ref), (cls_hbm, cls),
    )
    loads = [pltpu.make_async_copy(src, dst, local_sem.at[k]) for k, (src, dst) in enumerate(staged)]
    for load in loads:
        load.start()

    barrier = pltpu.get_barrier_semaphore()

    def greet(zz, qq, xx):
        pl.semaphore_signal(barrier, inc=1, device_id=(zz * Q + qq, xx), device_id_type=MESH)

    each(Z, lambda d: greet(lax.bitwise_and(z + d, Z - 1), q, x))
    each(Q, lambda d: greet(z, lax.bitwise_and(q + d, Q - 1), x))
    each(X, lambda d: greet(z, q, lax.bitwise_and(x + d, X - 1)))

    i1s[...] = jnp.zeros_like(i1s)
    for load in loads[:2]:
        load.wait()
    i1s[0:cap, :] = ids_ref[...].astype(F32)
    w32 = weight_ref[...].astype(F32)
    ws[...] = jnp.concatenate([w32[:, :DH], w32[:, DH:]], axis=0).astype(BF16)

    pl.semaphore_wait(barrier, (Z - 1) + (Q - 1) + (X - 1))

    ex_i1 = along_z(lambda t: i1s, lambda f: i1r.at[f], blocks(i1r, Z), i1_ss, i1_rs)
    ex_i1.start()
    i1r[z] = i1s[...]

    w_core = y % C

    def w1_copy(t):
        return copy(ws, wr.at[c], w1_ss.at[t], w1_rs.at[c], z, t * C + w_core, x)

    def w1_each(act):
        def step(t, carry):
            @pl.when((y // C == x) & jnp.logical_not((t == y) & (w_core == c)))
            def _():
                act(t)
            return carry
        lax.fori_loop(0, Y, step, 0)

    w1_each(lambda t: w1_copy(t).start())
    y_mine = x * C + c

    ex_i1.recv()
    marks = flag(iota((Q, NO), 1) == z * Q + iota((Q, NO), 0))
    asked = i1r[...].reshape(Z * S8, NO).astype(BF16)
    if LW > Z * S8:
        asked = jnp.concatenate([asked] * (LW // (Z * S8)), axis=0)
    for_q = dot(marks, asked, 1, 1)
    for k in range(Q):
        i2s[k] = jnp.broadcast_to(for_q[k:k + 1, :], (8, LW))
    ex_i2 = along_q(lambda t: i2s.at[t], lambda f: i2r.at[f], blocks(i2r, Q), i2_ss, i2_rs)
    ex_i2.start()
    i2r[q] = i2s[q]

    for c0 in range(C):
        own = (y == y_mine) & (c == c0)

        @pl.when(own)
        def _():
            wr[c0] = ws[...]

        @pl.when(jnp.logical_not(own))
        def _():
            copy(ws, wr.at[c0], w1_ss.at[0], w1_rs.at[c0], z, y_mine * C + c0, x).wait_recv()
    for hcol in range(2):
        cols = slice(hcol * DH, (hcol + 1) * DH)
        w_all[z, x, c, :, cols] = jnp.concatenate(
            [wr[c0, hcol * 8:(hcol + 1) * 8, :].astype(F32) for c0 in range(C)], axis=0
        ).astype(BF16)
    ex_w2 = along_z(
        lambda t: w_all.at[z, x, c], lambda f: w_all.at[f, x, c], w_all.at[pl.ds(0, Z - 1), x, c], w2_ss, w2_rs
    )
    ex_w2.start()

    loads[2].wait()
    lane_q = iota((front, Q * 8), 1)

    ex_i2.recv()
    wanted = i2r[...].reshape(Q * 8, LW).astype(BF16)

    wx[x] = wanted
    ex_wx = along_x(lambda t: wx.at[x], lambda f: wx.at[f], blocks(wx, X), wx_ss, wx_rs)

    def picked(col_of, q_of):
        spread = dot(flag(iota((front, LW), 1) == col_of), wanted, 1, 1)
        ids = jnp.sum(jnp.where(lane_q == q_of * 8, spread, 0.0), axis=1, keepdims=True)
        return flag(ids == iota((front, rows), 1).astype(F32))

    wide, nk = 128, DH // 128
    spans = ((0, nk - 1), (nk - 1, nk))
    fa1s, fa1r, fb1s, fb1r = (fa1s_0, fa1s_1), (fa1r_0, fa1r_1), (fb1s_0, fb1s_1), (fb1r_0, fb1r_1)
    fa2s, fa2r, fb2s, fb2r = (fa2s_0, fa2s_1), (fa2r_0, fa2r_1), (fb2s_0, fb2s_1), (fb2r_0, fb2r_1)
    chunks = len(spans)
    r = iota((front, 1), 0)
    pick_a = picked(quo(r, cap * Q) * S8 + quo(rem(r, cap * Q), Q), rem(r, Q))

    def column_blocks(first):
        return jnp.concatenate([feat[:, b * wide:(b + 1) * wide] for b in range(first, 2 * nk, 2)], axis=1)

    rows_a = dot(pick_a, column_blocks(0)).astype(BF16)
    ex_fa1, ex_fb1, ex_fa2, ex_fb2 = [], [], [], []
    for k in range(chunks):
        at = slice(spans[k][0] * wide, spans[k][1] * wide)
        fa1s[k][...] = rows_a[:, at].reshape(fa1s[k].shape)
        ex_fa1.append(along_z(
            lambda t, k=k: fa1s[k].at[t], lambda f, k=k: fa1r[k].at[f], blocks(fa1r[k], Z), fa1_ss.at[k], fa1_rs.at[k]))
        ex_fb1.append(along_q(
            lambda t, k=k: fb1s[k].at[t], lambda f, k=k: fb1r[k].at[f], blocks(fb1r[k], Q), fb1_ss.at[k], fb1_rs.at[k]))
        ex_fa2.append(along_q(
            lambda t, k=k: fa2s[k].at[t], lambda f, k=k: fa2r[k].at[f], blocks(fa2r[k], Q), fa2_ss.at[k], fa2_rs.at[k]))
        ex_fb2.append(along_z(
            lambda t, k=k: fb2s[k].at[t], lambda f, k=k: fb2r[k].at[f], blocks(fb2r[k], Z), fb2_ss.at[k], fb2_rs.at[k]))
    ex_fa1[0].start()
    pick_b = picked(rem(r, Z) * S8 + quo(rem(r, cap * Z), Z), quo(r, cap * Z))
    rows_b = dot(pick_b, column_blocks(1)).astype(BF16)
    for k in range(chunks):
        at = slice(spans[k][0] * wide, spans[k][1] * wide)
        fb1s[k][...] = rows_b[:, at].reshape(fb1s[k].shape)
    ex_fb1[0].start()
    for k in range(1, chunks):
        ex_fa1[k].start()
        ex_fb1[k].start()
    for k in range(chunks):
        fa1r[k][z] = fa1s[k][z]
        fb1r[k][q] = fb1s[k][q]
    ex_wx.start()
    move_a[...] = regroup(Z * cap, Q, 1)
    move_b[...] = regroup(Q * cap, Z, 1)

    ex_w2.recv()
    ex_w3 = along_x(
        lambda t: w_all.at[:, x, c], lambda f: w_all.at[:, f, c], w_all.at[:, pl.ds(0, X - 1), c], w3_ss, w3_rs
    )
    ex_w3.start()

    for load in loads[3:]:
        load.wait()
    counts = counts_ref[...].astype(F32)
    counts8 = jnp.concatenate([counts, jnp.zeros((6, NO), F32)], axis=0).astype(BF16)

    def validity(slots):
        n = NO * slots
        at = iota((NO, n), 1)
        per = dot(counts8, flag(iota((NO, n), 0) == quo(at, slots)))
        j = rem(iota((1, n), 1), slots).astype(F32)
        first = flag(j < per[0:1, :], F32)
        second = flag(j - half < per[1:2, :], F32)
        return jnp.where(j < half, first, second)

    valid = validity(cap)
    outer_rows = []
    for b in range(row_blocks):
        tiles = []
        for cbk in range(col_blocks):
            m = jnp.zeros((tile, tile), jnp.int32)
            for k in range(K):
                m = m + omask[b, k] * (otile_ref[b, k] == cbk).astype(jnp.int32)
            tiles.append(m.astype(F32) * valid[:, cbk * tile:(cbk + 1) * tile])
        outer_rows.append(jnp.concatenate(tiles, axis=1))
    outer = jnp.concatenate(outer_rows, axis=0)
    outer_scale = 1.0 + jnp.sum(outer, axis=1, keepdims=True)
    oi, oc = iota((hop, front), 0), iota((hop, front), 1)
    self_col = quo(oi, half) * cap + rem(oi, half)
    outer_self = (outer + flag(oc == self_col, F32)).astype(BF16)
    outer_a = dot(outer_self, regroup(Z, Q, cap, transpose=True)).astype(BF16)

    hop_valid = validity(half)
    tiles = []
    for cbk in range(row_blocks):
        m = jnp.zeros((tile, tile), jnp.int32)
        for k in range(K):
            m = m + imask[0, k] * (itile_ref[0, k] == cbk).astype(jnp.int32)
        tiles.append(m.astype(F32) * hop_valid[:, cbk * tile:(cbk + 1) * tile])
    inner32 = jnp.concatenate(tiles, axis=1)
    inner_degree = jnp.maximum(jnp.sum(inner32, axis=1, keepdims=True), 1.0)
    inner = inner32.astype(BF16)
    inner_twice = jnp.concatenate([inner32.T, inner32.T], axis=1).astype(BF16)

    label_row = labels_ref[...]
    label_col = jnp.sum(
        jnp.where(iota((seeds, seeds), 0) == iota((seeds, seeds), 1), label_row, 0), axis=1, keepdims=True
    )
    one_hot = flag(label_col == iota((seeds, classes), 1), F32)

    for k in range(chunks):
        ex_fa1[k].recv()
        fa2s[k][...] = dot(move_a[...], fa1r[k][...].reshape(front, -1)).astype(BF16).reshape(fa2s[k].shape)
        ex_fa2[k].start()
        fa2r[k][q] = fa2s[k][q]
        ex_fb1[k].recv()
        fb2s[k][...] = dot(move_b[...], fb1r[k][...].reshape(front, -1)).astype(BF16).reshape(fb2s[k].shape)
        ex_fb2[k].start()
        fb2r[k][z] = fb2s[k][z]

    ex_w3.recv()
    w4 = to_sibling(w_all.at[:, :, c], w_all.at[:, :, c], w4_ss, w4_rs)
    w4_in = to_sibling(w_all.at[:, :, sib], w_all.at[:, :, sib], w4_ss, w4_rs)
    w4.start()

    swap_a[...] = regroup(Z, Q, half)
    swap_b[...] = regroup(Q, Z, half)
    ex_wx.recv()

    def places(x_of, j_of, z_of, q_of):
        n = X * hop
        pick = flag(iota((LW, n), 0) == z_of * S8 + j_of)
        ids = jnp.zeros((1, n), F32)
        for k in range(X):
            here = (iota((Q * 8, n), 0) == q_of * 8) & (x_of == k)
            ids = ids + jnp.sum(jnp.where(here, dot(wx[k], pick), 0.0), axis=0, keepdims=True)
        return flag(iota((rows, n), 0).astype(F32) == ids)

    s = iota((1, X * hop), 1)
    def plane(d):
        return lax.bitwise_and(x + X - d, jnp.full_like(d, X - 1))

    place_a[...] = places(
        plane(rem(quo(s, half * Z), X)), rem(s, half), rem(quo(s, half), Z), quo(s, half * Z * X)
    )
    place_b[...] = places(
        plane(quo(s, half * Q * Z)), rem(s, half), rem(quo(s, half * Q), Z), rem(quo(s, half), Q)
    )

    for k in range(chunks):
        ex_fa2[k].recv()
        part_a = (dot(outer_a, fa2r[k][...].reshape(front, -1)) / outer_scale).astype(BF16)
        ex_fb2[k].recv()
        part_b = (dot(outer_self, fb2r[k][...].reshape(front, -1)) / outer_scale).astype(BF16)
        first, last = spans[k]
        columns = []
        for i in range(last - first):
            for b, part in ((2 * (first + i), part_a), (2 * (first + i) + 1, part_b)):
                columns.append(part[:, i * wide:(i + 1) * wide])
                agg[b // nk, :, (b % nk) * wide:(b % nk + 1) * wide] = columns[-1]
        if k == 0:
            w4_in.wait_recv()
        part = dot(
            jnp.concatenate(columns, axis=1),
            w_all[:, :, :, :, 2 * first * wide:2 * last * wide].reshape(HID, -1), 1, 1)
        pre[...] = part if k == 0 else pre[...] + part
    ga = to_sibling(agg.at[sib], agr, ga_ss, ga_rs)
    ga.start()

    hidden = jnp.maximum(pre[...], 0.0).astype(BF16)
    agg_two = (dot(inner, hidden) / inner_degree).astype(BF16)
    logits = dot(agg_two, cls[...], 1, 1)
    exponent = jnp.exp(logits - jnp.max(logits, axis=1, keepdims=True))
    softmax = exponent / jnp.sum(exponent, axis=1, keepdims=True)
    logit_grad = ((softmax - one_hot) / seeds).astype(BF16)
    agg_grad = dot(logit_grad, cls[...]) / inner_degree
    high = agg_grad.astype(BF16)
    low = (agg_grad - high.astype(F32)).astype(BF16)
    hidden_diff = dot(inner_twice, jnp.concatenate([high, low], axis=0))
    pgt[...] = jnp.where(pre[...] > 0.0, hidden_diff, 0.0).T.astype(BF16)
    g0 = to_sibling(pgt, pgtr, g0_ss, g0_rs)
    g0.start()
    diff[...] = hidden_diff.astype(BF16)

    def total(ref, n):
        acc = ref[0].astype(F32)
        for k in range(1, n):
            acc = acc + ref[k].astype(F32)
        return acc

    widen = flag(iota((classes, CP), 0) == iota((classes, CP), 1))
    class_rows = dot(dot(logit_grad, widen).astype(BF16), agg_two, 0, 0).astype(BF16)
    for t in range(X):
        for cc in range(C):
            cs1[t * C + cc] = class_rows[:, cc * HH + t * cw:cc * HH + (t + 1) * cw]
    me_xc = x * C + c
    ex_c1 = along_xc(lambda t: cs1.at[t], lambda f: cr1.at[f], blocks(cr1, X * C), c1_ss, c1_rs)
    ex_c1.start()
    cr1[me_xc] = cs1[me_xc]

    gmine = dot(pgt[...], agg[c])
    ga.wait_recv()
    g0.wait_recv()
    gmine = (gmine + dot(pgtr[...], agr[...])).astype(BF16).reshape(Z, X, YL * 16, DH)
    parts, span = gs1.shape[0], gs1.shape[4]
    for k in range(parts):
        for t in range(X):
            gs1[k, t] = gmine[:, t, :, k * span:(k + 1) * span]
    right, left, across = (lax.bitwise_and(x + d, X - 1) for d in (1, X - 1, 2))
    lower, upper = pl.ds(0, Z // 2), pl.ds(Z // 2, Z // 2)

    def g1(k, n, src, dst, to):
        return copy(src, dst, g1_ss.at[k, n], g1_rs.at[k, n], z, q, to)

    ring = [(
        g1(k, 0, gs1.at[k, across, lower], gra.at[k], right), g1(k, 1, gs1.at[k, across, upper], grb.at[k], left),
        g1(k, 2, gs1.at[k, right, upper], grl.at[k, upper], right), g1(k, 3, gs1.at[k, left, lower], grr.at[k, lower], left),
        g1(k, 4, gsa.at[k], grl.at[k, lower], right), g1(k, 5, gsb.at[k], grr.at[k, upper], left),
    ) for k in range(parts)]
    for k in range(parts):
        for one in ring[k][:4]:
            one.start()

    xw = HID // X
    xh = xw // 2

    def xz_leg(src, dst, ss, rs):
        def send(t):
            d, zz = t // Z, lax.bitwise_and(z + t, Z - 1)
            copy(src(d, zz), dst.at[d * Z + z], ss, rs, zz, q, lax.bitwise_and(x + d, X - 1)).start()
        each(X * Z, send)

    def wait_blocks(ref, n, ss, rs):
        some = ref.at[pl.ds(0, n)]
        return copy(some, some, ss, rs, z, q, lax.bitwise_and(x + 1, X - 1))

    for t in range(X):
        na1s[t * Z:(t + 1) * Z] = diff[:, t * xw:t * xw + xh].reshape(Z, Q * half, xh)
    xz_leg(lambda d, zz: na1s.at[lax.bitwise_and(x + d, X - 1) * Z + zz], na1r, na1_ss, na1_rs)
    second = jnp.concatenate([
        diff[:, pl.ds(pl.multiple_of(lax.bitwise_and(x + d, X - 1) * xw + xh, xh), xh)] for d in range(X)
    ], axis=1)
    nb1s[...] = dot(swap_a[...], second).astype(BF16).reshape(nb1s.shape)
    ex_nb1 = along_q(lambda t: nb1s.at[t], lambda f: nb1r.at[f], blocks(nb1r, Q), nb1_ss, nb1_rs)
    ex_nb1.start()
    ex_na2 = along_q(lambda t: na2s.at[t], lambda f: na2r.at[f], blocks(na2r, Q), na2_ss, na2_rs)
    na1r[z] = na1s[x * Z + z]
    nb1r[q] = nb1s[q]

    ex_c1.recv()
    cs2[...] = total(cr1, X * C).astype(BF16).reshape(cs2.shape)

    def to_blocks(act):
        def step(t, carry):
            @pl.when(t != y)
            def _():
                act(t)
            return carry
        lax.fori_loop(0, nb, step, 0)

    to_blocks(lambda t: copy(cs2.at[t], cr2.at[y], c2_ss, c2_rs, z, t * C + c, x).start())
    summing = y < nb
    ex_c2 = along_y(None, None, blocks(cr2, Y), c2_ss, c2_rs)
    ex_c3 = along_z(lambda t: cs3, lambda f: cr3.at[f], blocks(cr3, Z), c3_ss, c3_rs)
    ex_c4 = along_y(lambda t: cfin, lambda f: ca4.at[f], blocks(cr2, Y), c4_ss, c4_rs)

    for k in range(parts):
        r1, l1, r2, l2, r3, l3 = ring[k]
        r1.wait_recv()
        gsa[k] = (gs1[k, right, lower].astype(F32) + gra[k].astype(F32)).astype(BF16)
        r3.start()
        l1.wait_recv()
        gsb[k] = (gs1[k, left, upper].astype(F32) + grb[k].astype(F32)).astype(BF16)
        l3.start()

    @pl.when(summing)
    def _():
        cr2[y] = cs2[y]
        ex_c2.recv()
        cs3[...] = total(cr2, Y).astype(BF16)
        ex_c3.start()
        cr3[z] = cs3[...]

    ex_g2 = []
    for k in range(parts):
        for one in ring[k][2:]:
            one.wait_recv()
        gs2[k] = (gs1[k, x].astype(F32) + grl[k].astype(F32) + grr[k].astype(F32)).astype(BF16)
        ex_g2.append(along_z(
            lambda t, k=k: gs2.at[k, t], lambda f, k=k: gr2.at[k, f], blocks(gr2.at[k], Z), g2_ss.at[k], g2_rs.at[k]))
        ex_g2[k].start()
        gr2[k, z] = gs2[k, z]

    wait_blocks(na1r, X * Z - 1, na1_ss, na1_rs).wait_recv()
    came = jnp.concatenate([na1r[d * Z:(d + 1) * Z].reshape(hop, xh) for d in range(X)], axis=1)
    came = dot(swap_a[...], came).astype(BF16)
    for d in range(X):
        na2s[:, d] = came[:, d * xh:(d + 1) * xh].reshape(Q, Z * half, xh)
    ex_na2.start()
    na2r[q] = na2s[q]
    @pl.when(summing)
    def _():
        ex_c3.recv()
        cfin[...] = total(cr3, Z).astype(BF16)
        ex_c4.start()
        ca4[y] = cfin[...]

    ex_nb1.recv()
    came = dot(swap_b[...], nb1r[...].reshape(hop, X * xh)).astype(BF16)
    for d in range(X):
        nb2s[d * Z:(d + 1) * Z] = came[:, d * xh:(d + 1) * xh].reshape(Z, Q * half, xh)
    xz_leg(lambda d, zz: nb2s.at[d * Z + zz], nb2r, nb2_ss, nb2_rs)
    nb2r[z] = nb2s[z]

    @pl.when(summing)
    def _():
        some = ca4.at[pl.ds(0, nb - 1)]
        copy(some, some, c4_ss, c4_rs, z, q, x).wait_recv()

    @pl.when(jnp.logical_not(summing))
    def _():
        copy(ca4, ca4, c4_ss, c4_rs, z, q, x).wait_recv()

    ex_c5 = along_xc(lambda t: ca4, lambda f: ca5.at[f], blocks(ca5, X * C), c5_ss, c5_rs)
    ex_c5.start()
    ca5[me_xc] = ca4[...]

    for k in range(parts):
        ex_g2[k].recv()
        gs3[:, :, k * span:(k + 1) * span] = total(gr2.at[k], Z).astype(BF16).reshape(YL, 16, span)

    def g3_copy(yl):
        return copy(gs3.at[yl], gr3.at[y], g3_ss.at[yl], g3_rs, z, (x * YL + yl) * C + c, x)

    for yl in range(YL):
        @pl.when(x * YL + yl != y)
        def _():
            g3_copy(yl).start()
    owning = y // YL == x

    ex_na2.recv()
    node_out[:, :xh] = dot(place_a[...], na2r[...].reshape(X * hop, xh)).astype(BF16)

    def g4_copy(xx, cc):
        return copy(gs4.at[cc], gr4.at[c], g4_ss.at[xx * C + cc], g4_rs.at[c], z, y * C + cc, xx)

    def g4_each(act):
        for xx in range(X):
            for cc in range(C):
                @pl.when(owning & jnp.logical_not((x == xx) & (c == cc)))
                def _():
                    act(xx, cc)

    @pl.when(owning)
    def _():
        gr3[y] = gs3[y % YL]
        copy(blocks(gr3, Y), blocks(gr3, Y), g3_ss.at[0], g3_rs, z, q, x).wait_recv()
        gs4[...] = total(gr3, Y).reshape(gs4.shape)
        gr4[c] = gs4[c]

    g4_each(lambda xx, cc: g4_copy(xx, cc).start())

    wait_blocks(nb2r, X * Z - 1, nb2_ss, nb2_rs).wait_recv()
    node_out[:, xh:] = dot(place_b[...], nb2r[...].reshape(X * hop, xh)).astype(BF16)

    ex_c5.recv()
    for t in range(X):
        for cc in range(C):
            class_out[:, cc * HH + t * cw:cc * HH + (t + 1) * cw] = ca5[t * C + cc].reshape(CP, cw)

    for cc in range(C):
        @pl.when(jnp.logical_not(owning & (c == cc)))
        def _():
            copy(gs4.at[0], gr4.at[cc], g4_ss.at[0], g4_rs.at[cc], z, y * C + cc, y // YL).wait_recv()
        hidden_out[:, cc * DH:(cc + 1) * DH] = gr4[cc]

    for ex in (ex_i1, ex_i2, ex_wx, ex_w2, ex_w3, *ex_fa1, *ex_fb1, *ex_fa2, *ex_fb2, ex_nb1, ex_na2, *ex_g2, ex_c1, ex_c5):
        ex.sent()
    w1_each(lambda t: w1_copy(t).wait_send())
    for one in (w4, ga, g0, *[leg for legs in ring for leg in legs]):
        one.wait_send()
    wait_blocks(na1r, X * Z - 1, na1_ss, na1_rs).wait_send()
    wait_blocks(nb2r, X * Z - 1, nb2_ss, nb2_rs).wait_send()

    @pl.when(summing)
    def _():
        some = cs2.at[pl.ds(0, nb - 1)]
        copy(some, some, c2_ss, c2_rs, z, q, x).wait_send()
        ex_c3.sent()
        ex_c4.sent()

    @pl.when(jnp.logical_not(summing))
    def _():
        copy(cs2, cs2, c2_ss, c2_rs, z, q, x).wait_send()

    for yl in range(YL):
        @pl.when(x * YL + yl != y)
        def _():
            g3_copy(yl).wait_send()
    g4_each(lambda xx, cc: g4_copy(xx, cc).wait_send())


def on_device(
    grid, features, hidden_weight, class_weight, request_ids, request_counts,
    outer_tiles, outer_masks, inner_tiles, inner_masks, labels,
):
    Z, Y, C, X = grid
    Q = Y * C
    NO = Z * Q
    cap = request_ids.shape[1]
    half = cap // 2
    rows, D = features.shape
    classes, HID = class_weight.shape
    tile = outer_masks.shape[2]
    hop = NO * half
    DH, HH, YL = D // 2, HID // 2, Y // X
    cb = 32 if classes > 32 else 8
    nb = -(-classes // cb)
    CP, cw = nb * cb, HID // (C * X)
    LW = max(Z * 8, 128)
    dims = (Z, Y, C, X, cap, tile, rows, classes)
    vm, dma = pltpu.VMEM, pltpu.SemaphoreType.DMA
    xh, nk, gk = HID // X // 2, DH // 128, 1
    by_z = [vm((Z, cap * Q, n * 128), BF16) for n in (nk - 1, 1)]
    by_q = [vm((Q, cap * Z, n * 128), BF16) for n in (nk - 1, 1)]
    scratch = [
        vm(features.shape, BF16), vm(outer_masks.shape, jnp.int32), vm(inner_masks.shape, jnp.int32),
        vm(class_weight.shape, BF16), vm(hidden_weight.shape, BF16),
        vm((cap, NO), jnp.int32), vm((2, NO), jnp.int32), vm((1, labels.shape[0]), jnp.int32),
        vm((8, NO), F32), vm((Z, 8, NO), F32), vm((Q, 8, LW), F32), vm((Q, 8, LW), F32),
        vm((X, Q * 8, LW), BF16), vm((rows, X * hop), BF16), vm((rows, X * hop), BF16),
        vm((16, DH), BF16), vm((C, 16, DH), BF16), vm((Z, X, C, 16, D), BF16),
        *by_z, *by_z, *by_q, *by_q, *by_q, *by_q, *by_z, *by_z,
        vm((cap * NO, cap * NO), BF16), vm((cap * NO, cap * NO), BF16), vm((hop, hop), BF16), vm((hop, hop), BF16),
        vm((2, hop, DH), BF16), vm((hop, DH), BF16), vm((hop, HID), F32), vm((HID, hop), BF16), vm((HID, hop), BF16),
        vm((hop, HID), BF16),
        vm((X * Z, Q * half, xh), BF16), vm((X * Z, Q * half, xh), BF16),
        *[vm((Q, X, Z * half, xh), BF16)] * 2, *[vm((Q, Z * half, HH), BF16)] * 2,
        vm((X * Z, Q * half, xh), BF16), vm((X * Z, Q * half, xh), BF16),
        vm((gk, X, Z, YL * 16, DH // gk), BF16), *[vm((gk, Z // 2, YL * 16, DH // gk), BF16)] * 4,
        *[vm((gk, Z, YL * 16, DH // gk), BF16)] * 4,
        vm((YL, 16, DH), BF16), vm((Y, 16, DH), BF16), vm((C, 8, DH), F32), vm((C, 8, DH), F32),
        vm((X * C, CP, cw), BF16), vm((X * C, CP, cw), BF16), vm((nb, cb, cw), BF16), vm((Y, cb, cw), BF16),
        vm((cb, cw), BF16), vm((Z, cb, cw), BF16), vm((cb, cw), BF16), vm((nb, cb, cw), BF16),
        vm((X * C, nb, cb, cw), BF16),
        dma((8,)),
        *[dma] * 6,
        dma((Y,)), dma((C,)), *[dma] * 6,
        *[dma((2,))] * 8, *[dma] * 8,
        *[dma] * 4, dma((gk, 6)), dma((gk, 6)), dma((gk,)), dma((gk,)), dma((YL,)), dma, dma((X * C,)), dma((C,)),
        *[dma] * 10,
    ]
    hbm = pl.BlockSpec(memory_space=pl.ANY)
    vmem = pl.BlockSpec(memory_space=pltpu.VMEM)
    smem = pl.BlockSpec(memory_space=pltpu.SMEM)
    hidden_grad, class_grad, node_grad = pl.pallas_call(
        functools.partial(kernel, dims),
        out_shape=(
            jax.ShapeDtypeStruct(hidden_weight.shape, F32),
            jax.ShapeDtypeStruct((CP, HID), BF16),
            jax.ShapeDtypeStruct((rows, HID // X), BF16),
        ),
        in_specs=[hbm, hbm, hbm, hbm, hbm, smem, hbm, smem, hbm, hbm],
        out_specs=(vmem, vmem, vmem),
        scratch_shapes=scratch,
        compiler_params=pltpu.CompilerParams(
            collective_id=0, has_side_effects=True, vmem_limit_bytes=56 * 1024 * 1024
        ),
        cost_estimate=pl.CostEstimate(flops=2_000_000_000, bytes_accessed=3_000_000, transcendentals=20_000),
    )(
        features, hidden_weight, class_weight, request_ids.T, request_counts.T,
        outer_tiles, outer_masks, inner_tiles, inner_masks, labels.reshape(1, -1),
    )
    return hidden_grad, class_grad[:classes].astype(F32), node_grad


def solution(mesh):
    grid = GRIDS[(mesh.shape["owner"], mesh.shape["rep"])]
    placed = (
        P("owner", None),
        P("owner", None),
        P(),
        P(("owner", "rep"), None),
        P(("owner", "rep"), None),
        P(("owner", "rep"), None),
        P(("owner", "rep"), None, None, None),
        P(("owner", "rep"), None),
        P(("owner", "rep"), None, None, None),
        P(("owner", "rep")),
    )
    return jax.shard_map(
        functools.partial(on_device, grid),
        mesh=mesh,
        in_specs=placed,
        out_specs=(P("owner", None), P(), P("owner", "rep")),
        check_vma=False,
    )
```

```python
import functools

import jax
import jax.numpy as jnp
from jax import lax
from jax.experimental import pallas as pl
from jax.experimental.pallas import tpu as pltpu
from jax.sharding import PartitionSpec as P

MESH = pl.DeviceIdType.MESH
F32 = jnp.float32
BF16 = jnp.bfloat16

GRIDS = {(128, 4): (8, 8, 2, 4), (32, 4): (2, 8, 2, 4)}


def iota(shape, dim):
    return lax.broadcasted_iota(jnp.int32, shape, dim)


def quo(a, n):
    return lax.shift_right_logical(a, jnp.full_like(a, n.bit_length() - 1))


def rem(a, n):
    return lax.bitwise_and(a, jnp.full_like(a, n - 1))


def flag(cond, dtype=BF16):
    return jnp.where(cond, 1.0, 0.0).astype(F32).astype(dtype)


def dot(a, b, ca=1, cb=0):
    return lax.dot_general(a, b, (((ca,), (cb,)), ((), ())), preferred_element_type=F32)


def regroup(outer, middle, inner, transpose=False):
    n = outer * middle * inner
    o, i = iota((n, n), 0), iota((n, n), 1)
    if transpose:
        o, i = i, o
    m, rest = quo(o, outer * inner), rem(o, outer * inner)
    a, b = quo(rest, inner), rem(rest, inner)
    return flag(i == a * (middle * inner) + m * inner + b)


def kernel(
    dims,
    feat_hbm, weight_hbm, cls_hbm, ids_hbm, counts_hbm, otile_ref, omask_hbm, itile_ref, imask_hbm, labels_hbm,
    hidden_out, class_out, node_out,
    feat, omask, imask, cls, weight_ref, ids_ref, counts_ref, labels_ref,
    i1s, i1r, i2s, i2r, wx, place_a, place_b,
    ws, wr, w_all,
    fa1s_0, fa1s_1, fa1r_0, fa1r_1, fb1s_0, fb1s_1, fb1r_0, fb1r_1,
    fa2s_0, fa2s_1, fa2r_0, fa2r_1, fb2s_0, fb2s_1, fb2r_0, fb2r_1, move_a, move_b, swap_a, swap_b,
    agg, agr, pre, pgt, pgtr, diff,
    na1s, na1r, na2s, na2r, nb1s, nb1r, nb2s, nb2r,
    gs1, gra, grb, gsa, gsb, grl, grr, gs2, gr2, gs3, gr3, gs4, gr4,
    cmine, cs0, cr0, cs1, cr1, cs2, cr2, cs3, cr3, cfin, ca4, ca5, ca6,
    local_sem,
    i1_ss, i1_rs, i2_ss, i2_rs, wx_ss, wx_rs,
    w1_ss, w1_rs, w2_ss, w2_rs, w3_ss, w3_rs, w4_ss, w4_rs,
    fa1_ss, fa1_rs, fa2_ss, fa2_rs, fb1_ss, fb1_rs, fb2_ss, fb2_rs,
    na1_ss, na1_rs, na2_ss, na2_rs, nb1_ss, nb1_rs, nb2_ss, nb2_rs,
    ga_ss, ga_rs, g0_ss, g0_rs, g1_ss, g1_rs, g2_ss, g2_rs, g3_ss, g3_rs, g4_ss, g4_rs,
    c0_ss, c0_rs, c1_ss, c1_rs, c2_ss, c2_rs, c3_ss, c3_rs, c4_ss, c4_rs, c5_ss, c5_rs, c6_ss, c6_rs,
):
    Z, Y, C, X, cap, tile, rows, classes = dims
    Q = Y * C
    NO = Z * Q
    half = cap // 2
    hop, front = NO * half, NO * cap
    D, HID = feat.shape[1], pre.shape[1]
    DH, HH = D // 2, HID // 2
    YL = Y // X
    nb, cb, cw = cs2.shape
    CP = nb * cb
    seeds = labels_ref.shape[1]
    row_blocks, col_blocks, K = hop // tile, front // tile, otile_ref.shape[1]
    LW = i2s.shape[2]
    S8 = 8

    me_o = lax.axis_index("owner")
    x = lax.axis_index("rep")
    z = me_o // Q
    q = me_o % Q
    y = q // C
    c = q % C
    sib = C - 1 - c

    def copy(src, dst, ss, rs, zz, qq, xx):
        return pltpu.make_async_remote_copy(
            src_ref=src, dst_ref=dst, send_sem=ss, recv_sem=rs,
            device_id=(zz * Q + qq, xx), device_id_type=MESH,
        )

    def each(n, body):
        def step(i, carry):
            body(i)
            return carry
        lax.fori_loop(1, n, step, 0)

    class Exchange:
        def __init__(self, n, me, at, src, dst, bulk, ss, rs):
            self.n, self.me, self.at, self.src, self.dst, self.bulk, self.ss, self.rs = n, me, at, src, dst, bulk, ss, rs

        def start(self):
            def send(d):
                to = lax.bitwise_and(self.me + d, self.n - 1)
                copy(self.src(to), self.dst(self.me), self.ss, self.rs, *self.at(to)).start()
            each(self.n, send)

        def all(self):
            return copy(self.bulk, self.bulk, self.ss, self.rs, *self.at(lax.bitwise_and(self.me + 1, self.n - 1)))

        def recv(self):
            self.all().wait_recv()

        def sent(self):
            self.all().wait_send()

    def along_z(*rest):
        return Exchange(Z, z, lambda t: (t, q, x), *rest)

    def along_q(*rest):
        return Exchange(Q, q, lambda t: (z, t, x), *rest)

    def along_y(*rest):
        return Exchange(Y, y, lambda t: (z, t * C + c, x), *rest)

    def along_x(*rest):
        return Exchange(X, x, lambda t: (z, q, t), *rest)

    def along_xz(*rest):
        return Exchange(X * Z, x * Z + z, lambda t: (lax.bitwise_and(t, Z - 1), q, t // Z), *rest)

    def along_xc(*rest):
        return Exchange(X * C, x * C + c, lambda t: (z, y * C + lax.bitwise_and(t, C - 1), t // C), *rest)

    def blocks(ref, n):
        return ref.at[pl.ds(0, n - 1)]

    def to_sibling(src, dst, ss, rs):
        return copy(src, dst, ss, rs, z, y * C + sib, x)

    staged = (
        (ids_hbm, ids_ref), (weight_hbm, weight_ref), (feat_hbm, feat), (counts_hbm, counts_ref),
        (omask_hbm, omask), (imask_hbm, imask), (labels_hbm, labels_ref), (cls_hbm, cls),
    )
    loads = [pltpu.make_async_copy(src, dst, local_sem.at[k]) for k, (src, dst) in enumerate(staged)]
    for load in loads:
        load.start()

    barrier = pltpu.get_barrier_semaphore()

    def greet(zz, qq, xx):
        pl.semaphore_signal(barrier, inc=1, device_id=(zz * Q + qq, xx), device_id_type=MESH)

    each(Z, lambda d: greet(lax.bitwise_and(z + d, Z - 1), q, x))
    each(Q, lambda d: greet(z, lax.bitwise_and(q + d, Q - 1), x))
    each(X, lambda d: greet(z, q, lax.bitwise_and(x + d, X - 1)))

    i1s[...] = jnp.zeros_like(i1s)
    for load in loads[:2]:
        load.wait()
    i1s[0:cap, :] = ids_ref[...].astype(F32)
    w32 = weight_ref[...].astype(F32)
    ws[...] = jnp.concatenate([w32[:, :DH], w32[:, DH:]], axis=0).astype(BF16)

    pl.semaphore_wait(barrier, (Z - 1) + (Q - 1) + (X - 1))

    ex_i1 = along_z(lambda t: i1s, lambda f: i1r.at[f], blocks(i1r, Z), i1_ss, i1_rs)
    ex_i1.start()
    i1r[z] = i1s[...]

    w_core = y % C

    def w1_copy(t):
        return copy(ws, wr.at[c], w1_ss.at[t], w1_rs.at[c], z, t * C + w_core, x)

    def w1_each(act):
        def step(t, carry):
            @pl.when((y // C == x) & jnp.logical_not((t == y) & (w_core == c)))
            def _():
                act(t)
            return carry
        lax.fori_loop(0, Y, step, 0)

    w1_each(lambda t: w1_copy(t).start())
    y_mine = x * C + c

    ex_i1.recv()
    marks = flag(iota((Q, NO), 1) == z * Q + iota((Q, NO), 0))
    asked = i1r[...].reshape(Z * S8, NO).astype(BF16)
    if LW > Z * S8:
        asked = jnp.concatenate([asked] * (LW // (Z * S8)), axis=0)
    for_q = dot(marks, asked, 1, 1)
    for k in range(Q):
        i2s[k] = jnp.broadcast_to(for_q[k:k + 1, :], (8, LW))
    ex_i2 = along_q(lambda t: i2s.at[t], lambda f: i2r.at[f], blocks(i2r, Q), i2_ss, i2_rs)
    ex_i2.start()
    i2r[q] = i2s[q]

    for c0 in range(C):
        own = (y == y_mine) & (c == c0)

        @pl.when(own)
        def _():
            wr[c0] = ws[...]

        @pl.when(jnp.logical_not(own))
        def _():
            copy(ws, wr.at[c0], w1_ss.at[0], w1_rs.at[c0], z, y_mine * C + c0, x).wait_recv()
    for hcol in range(2):
        cols = slice(hcol * DH, (hcol + 1) * DH)
        w_all[z, x, c, :, cols] = jnp.concatenate(
            [wr[c0, hcol * 8:(hcol + 1) * 8, :].astype(F32) for c0 in range(C)], axis=0
        ).astype(BF16)
    def w2(k, way):
        block = w_all.at[lax.bitwise_and(z + (Z - k if way == 0 else k), Z - 1), x, c]
        to = lax.bitwise_and(z + (1 if way == 0 else Z - 1), Z - 1)
        return copy(block, block, w2_ss.at[k, way], w2_rs.at[k, way], to, q, x)

    def w2_steps(k):
        return [w2(k, way) for way, steps in ((0, Z // 2), (1, Z // 2 - 1)) if 0 <= k < steps]

    def w2_go(k):
        for one in w2_steps(k - 1):
            one.wait_recv()
        for one in w2_steps(k):
            one.start()

    w2_go(0)

    loads[2].wait()
    lane_q = iota((front, Q * 8), 1)

    ex_i2.recv()
    wanted = i2r[...].reshape(Q * 8, LW).astype(BF16)

    wx[x] = wanted
    ex_wx = along_x(lambda t: wx.at[x], lambda f: wx.at[f], blocks(wx, X), wx_ss, wx_rs)

    def picked(col_of, q_of):
        spread = dot(flag(iota((front, LW), 1) == col_of), wanted, 1, 1)
        ids = jnp.sum(jnp.where(lane_q == q_of * 8, spread, 0.0), axis=1, keepdims=True)
        return flag(ids == iota((front, rows), 1).astype(F32))

    wide, nk = 128, DH // 128
    spans = ((0, nk - 1), (nk - 1, nk))
    fa1s, fa1r, fb1s, fb1r = (fa1s_0, fa1s_1), (fa1r_0, fa1r_1), (fb1s_0, fb1s_1), (fb1r_0, fb1r_1)
    fa2s, fa2r, fb2s, fb2r = (fa2s_0, fa2s_1), (fa2r_0, fa2r_1), (fb2s_0, fb2s_1), (fb2r_0, fb2r_1)
    chunks = len(spans)
    r = iota((front, 1), 0)
    pick_a = picked(quo(r, cap * Q) * S8 + quo(rem(r, cap * Q), Q), rem(r, Q))

    def column_blocks(first):
        return jnp.concatenate([feat[:, b * wide:(b + 1) * wide] for b in range(first, 2 * nk, 2)], axis=1)

    rows_a = dot(pick_a, column_blocks(0)).astype(BF16)
    ex_fa1, ex_fb1, ex_fa2, ex_fb2 = [], [], [], []
    for k in range(chunks):
        at = slice(spans[k][0] * wide, spans[k][1] * wide)
        fa1s[k][...] = rows_a[:, at].reshape(fa1s[k].shape)
        ex_fa1.append(along_z(
            lambda t, k=k: fa1s[k].at[t], lambda f, k=k: fa1r[k].at[f], blocks(fa1r[k], Z), fa1_ss.at[k], fa1_rs.at[k]))
        ex_fb1.append(along_q(
            lambda t, k=k: fb1s[k].at[t], lambda f, k=k: fb1r[k].at[f], blocks(fb1r[k], Q), fb1_ss.at[k], fb1_rs.at[k]))
        ex_fa2.append(along_q(
            lambda t, k=k: fa2s[k].at[t], lambda f, k=k: fa2r[k].at[f], blocks(fa2r[k], Q), fa2_ss.at[k], fa2_rs.at[k]))
        ex_fb2.append(along_z(
            lambda t, k=k: fb2s[k].at[t], lambda f, k=k: fb2r[k].at[f], blocks(fb2r[k], Z), fb2_ss.at[k], fb2_rs.at[k]))
    ex_fa1[0].start()
    w2_go(1)
    pick_b = picked(rem(r, Z) * S8 + quo(rem(r, cap * Z), Z), quo(r, cap * Z))
    rows_b = dot(pick_b, column_blocks(1)).astype(BF16)
    for k in range(chunks):
        at = slice(spans[k][0] * wide, spans[k][1] * wide)
        fb1s[k][...] = rows_b[:, at].reshape(fb1s[k].shape)
    ex_fb1[0].start()
    for k in range(1, chunks):
        ex_fa1[k].start()
        ex_fb1[k].start()
    for k in range(chunks):
        fa1r[k][z] = fa1s[k][z]
        fb1r[k][q] = fb1s[k][q]
    ex_wx.start()
    move_a[...] = regroup(Z * cap, Q, 1)
    move_b[...] = regroup(Q * cap, Z, 1)

    w2_go(2)

    for load in loads[3:]:
        load.wait()
    counts = counts_ref[...].astype(F32)
    counts8 = jnp.concatenate([counts, jnp.zeros((6, NO), F32)], axis=0).astype(BF16)

    def validity(slots):
        n = NO * slots
        at = iota((NO, n), 1)
        per = dot(counts8, flag(iota((NO, n), 0) == quo(at, slots)))
        j = rem(iota((1, n), 1), slots).astype(F32)
        first = flag(j < per[0:1, :], F32)
        second = flag(j - half < per[1:2, :], F32)
        return jnp.where(j < half, first, second)

    valid = validity(cap)
    outer_rows = []
    for b in range(row_blocks):
        tiles = []
        for cbk in range(col_blocks):
            m = jnp.zeros((tile, tile), jnp.int32)
            for k in range(K):
                m = m + omask[b, k] * (otile_ref[b, k] == cbk).astype(jnp.int32)
            tiles.append(m.astype(F32) * valid[:, cbk * tile:(cbk + 1) * tile])
        outer_rows.append(jnp.concatenate(tiles, axis=1))
    outer = jnp.concatenate(outer_rows, axis=0)
    outer_scale = 1.0 + jnp.sum(outer, axis=1, keepdims=True)
    oi, oc = iota((hop, front), 0), iota((hop, front), 1)
    self_col = quo(oi, half) * cap + rem(oi, half)
    outer_self = (outer + flag(oc == self_col, F32)).astype(BF16)
    outer_a = dot(outer_self, regroup(Z, Q, cap, transpose=True)).astype(BF16)

    hop_valid = validity(half)
    tiles = []
    for cbk in range(row_blocks):
        m = jnp.zeros((tile, tile), jnp.int32)
        for k in range(K):
            m = m + imask[0, k] * (itile_ref[0, k] == cbk).astype(jnp.int32)
        tiles.append(m.astype(F32) * hop_valid[:, cbk * tile:(cbk + 1) * tile])
    inner32 = jnp.concatenate(tiles, axis=1)
    inner_degree = jnp.maximum(jnp.sum(inner32, axis=1, keepdims=True), 1.0)
    inner = inner32.astype(BF16)
    inner_twice = jnp.concatenate([inner32.T, inner32.T], axis=1).astype(BF16)

    label_row = labels_ref[...]
    label_col = jnp.sum(
        jnp.where(iota((seeds, seeds), 0) == iota((seeds, seeds), 1), label_row, 0), axis=1, keepdims=True
    )
    one_hot = flag(label_col == iota((seeds, classes), 1), F32)

    w2_go(3)
    ex_w3 = along_x(
        lambda t: w_all.at[:, x, c], lambda f: w_all.at[:, f, c], w_all.at[:, pl.ds(0, X - 1), c], w3_ss, w3_rs
    )
    for k in range(chunks):
        ex_fa1[k].recv()
        fa2s[k][...] = dot(move_a[...], fa1r[k][...].reshape(front, -1)).astype(BF16).reshape(fa2s[k].shape)
        ex_fa2[k].start()
        fa2r[k][q] = fa2s[k][q]
        ex_fb1[k].recv()
        fb2s[k][...] = dot(move_b[...], fb1r[k][...].reshape(front, -1)).astype(BF16).reshape(fb2s[k].shape)
        ex_fb2[k].start()
        fb2r[k][z] = fb2s[k][z]
        if k == 0:
            w2_go(Z // 2)
            ex_w3.start()

    swap_a[...] = regroup(Z, Q, half)
    swap_b[...] = regroup(Q, Z, half)
    ex_wx.recv()

    def places(x_of, j_of, z_of, q_of):
        n = X * hop
        pick = flag(iota((LW, n), 0) == z_of * S8 + j_of)
        ids = jnp.zeros((1, n), F32)
        for k in range(X):
            here = (iota((Q * 8, n), 0) == q_of * 8) & (x_of == k)
            ids = ids + jnp.sum(jnp.where(here, dot(wx[k], pick), 0.0), axis=0, keepdims=True)
        return flag(iota((rows, n), 0).astype(F32) == ids)

    s = iota((1, X * hop), 1)
    def plane(d):
        return lax.bitwise_and(x + X - d, jnp.full_like(d, X - 1))

    place_a[...] = places(
        plane(rem(quo(s, half * Z), X)), rem(s, half), rem(quo(s, half), Z), quo(s, half * Z * X)
    )
    place_b[...] = places(
        plane(quo(s, half * Q * Z)), rem(s, half), rem(quo(s, half * Q), Z), rem(quo(s, half), Q)
    )

    ex_w3.recv()
    w4 = to_sibling(w_all.at[:, :, c], w_all.at[:, :, c], w4_ss, w4_rs)
    w4_in = to_sibling(w_all.at[:, :, sib], w_all.at[:, :, sib], w4_ss, w4_rs)
    w4.start()

    for k in range(chunks):
        ex_fa2[k].recv()
        part_a = (dot(outer_a, fa2r[k][...].reshape(front, -1)) / outer_scale).astype(BF16)
        ex_fb2[k].recv()
        part_b = (dot(outer_self, fb2r[k][...].reshape(front, -1)) / outer_scale).astype(BF16)
        first, last = spans[k]
        columns = []
        for i in range(last - first):
            for b, part in ((2 * (first + i), part_a), (2 * (first + i) + 1, part_b)):
                columns.append(part[:, i * wide:(i + 1) * wide])
                agg[b // nk, :, (b % nk) * wide:(b % nk + 1) * wide] = columns[-1]
        if k == 0:
            w4_in.wait_recv()
        part = dot(
            jnp.concatenate(columns, axis=1),
            w_all[:, :, :, :, 2 * first * wide:2 * last * wide].reshape(HID, -1), 1, 1)
        pre[...] = part if k == 0 else pre[...] + part
    ga = to_sibling(agg.at[sib], agr, ga_ss, ga_rs)
    ga.start()

    hidden = jnp.maximum(pre[...], 0.0).astype(BF16)
    agg_two = (dot(inner, hidden) / inner_degree).astype(BF16)
    logits = dot(agg_two, cls[...], 1, 1)
    exponent = jnp.exp(logits - jnp.max(logits, axis=1, keepdims=True))
    softmax = exponent / jnp.sum(exponent, axis=1, keepdims=True)
    logit_grad = ((softmax - one_hot) / seeds).astype(BF16)
    agg_grad = dot(logit_grad, cls[...]) / inner_degree
    high = agg_grad.astype(BF16)
    low = (agg_grad - high.astype(F32)).astype(BF16)
    hidden_diff = dot(inner_twice, jnp.concatenate([high, low], axis=0))
    pgt[...] = jnp.where(pre[...] > 0.0, hidden_diff, 0.0).T.astype(BF16)
    g0 = to_sibling(pgt, pgtr, g0_ss, g0_rs)
    g0.start()
    diff[...] = hidden_diff.astype(BF16)

    def total(ref, n):
        acc = ref[0].astype(F32)
        for k in range(1, n):
            acc = acc + ref[k].astype(F32)
        return acc

    widen = flag(iota((classes, CP), 0) == iota((classes, CP), 1))
    class_rows = dot(dot(logit_grad, widen).astype(BF16), agg_two, 0, 0)
    cs0[...] = jnp.where(c == 0, class_rows[:, HH:], class_rows[:, :HH]).astype(BF16)
    c0 = to_sibling(cs0, cr0, c0_ss, c0_rs)
    c0.start()
    cmine[...] = jnp.where(c == 0, class_rows[:, :HH], class_rows[:, HH:])

    gmine = dot(pgt[...], agg[c])
    ga.wait_recv()
    g0.wait_recv()
    gmine = (gmine + dot(pgtr[...], agr[...])).astype(BF16).reshape(Z, X, YL * 16, DH)
    parts, span = gs1.shape[0], gs1.shape[4]
    for k in range(parts):
        for t in range(X):
            gs1[k, t] = gmine[:, t, :, k * span:(k + 1) * span]
    right, left, across = (lax.bitwise_and(x + d, X - 1) for d in (1, X - 1, 2))
    lower, upper = pl.ds(0, Z // 2), pl.ds(Z // 2, Z // 2)

    def g1(k, n, src, dst, to):
        return copy(src, dst, g1_ss.at[k, n], g1_rs.at[k, n], z, q, to)

    ring = [(
        g1(k, 0, gs1.at[k, across, lower], gra.at[k], right), g1(k, 1, gs1.at[k, across, upper], grb.at[k], left),
        g1(k, 2, gs1.at[k, right, upper], grl.at[k, upper], right), g1(k, 3, gs1.at[k, left, lower], grr.at[k, lower], left),
        g1(k, 4, gsa.at[k], grl.at[k, lower], right), g1(k, 5, gsb.at[k], grr.at[k, upper], left),
    ) for k in range(parts)]
    for k in range(parts):
        for one in ring[k][:4]:
            one.start()

    c0.wait_recv()
    cmine[...] = cmine[...] + cr0[...].astype(F32)
    for t in range(X):
        cs1[t] = cmine[:, t * cw:(t + 1) * cw].astype(BF16)
    ex_c1 = along_x(lambda t: cs1.at[t], lambda f: cr1.at[f], blocks(cr1, X), c1_ss, c1_rs)
    ex_c1.start()
    cr1[x] = cs1[x]

    xw = HID // X
    xh = xw // 2

    def xz_leg(src, dst, ss, rs):
        def send(t):
            d, zz = t // Z, lax.bitwise_and(z + t, Z - 1)
            copy(src(d, zz), dst.at[d * Z + z], ss, rs, zz, q, lax.bitwise_and(x + d, X - 1)).start()
        each(X * Z, send)

    def wait_blocks(ref, n, ss, rs):
        some = ref.at[pl.ds(0, n)]
        return copy(some, some, ss, rs, z, q, lax.bitwise_and(x + 1, X - 1))

    for t in range(X):
        na1s[t * Z:(t + 1) * Z] = diff[:, t * xw:t * xw + xh].reshape(Z, Q * half, xh)
    xz_leg(lambda d, zz: na1s.at[lax.bitwise_and(x + d, X - 1) * Z + zz], na1r, na1_ss, na1_rs)
    second = jnp.concatenate([
        diff[:, pl.ds(pl.multiple_of(lax.bitwise_and(x + d, X - 1) * xw + xh, xh), xh)] for d in range(X)
    ], axis=1)
    nb1s[...] = dot(swap_a[...], second).astype(BF16).reshape(nb1s.shape)
    ex_nb1 = along_q(lambda t: nb1s.at[t], lambda f: nb1r.at[f], blocks(nb1r, Q), nb1_ss, nb1_rs)
    ex_nb1.start()
    ex_na2 = along_q(lambda t: na2s.at[t], lambda f: na2r.at[f], blocks(na2r, Q), na2_ss, na2_rs)
    na1r[z] = na1s[x * Z + z]
    nb1r[q] = nb1s[q]

    ex_c1.recv()
    cs2[...] = total(cr1, X).astype(BF16).reshape(cs2.shape)

    def to_blocks(act):
        def step(t, carry):
            @pl.when(t != y)
            def _():
                act(t)
            return carry
        lax.fori_loop(0, nb, step, 0)

    to_blocks(lambda t: copy(cs2.at[t], cr2.at[y], c2_ss, c2_rs, z, t * C + c, x).start())
    summing = y < nb
    ex_c2 = along_y(None, None, blocks(cr2, Y), c2_ss, c2_rs)
    ex_c3 = along_z(lambda t: cs3, lambda f: cr3.at[f], blocks(cr3, Z), c3_ss, c3_rs)
    ex_c4 = along_y(lambda t: cfin, lambda f: ca4.at[f], blocks(cr2, Y), c4_ss, c4_rs)

    for k in range(parts):
        r1, l1, r2, l2, r3, l3 = ring[k]
        r1.wait_recv()
        gsa[k] = (gs1[k, right, lower].astype(F32) + gra[k].astype(F32)).astype(BF16)
        r3.start()
        l1.wait_recv()
        gsb[k] = (gs1[k, left, upper].astype(F32) + grb[k].astype(F32)).astype(BF16)
        l3.start()

    @pl.when(summing)
    def _():
        cr2[y] = cs2[y]
        ex_c2.recv()
        cs3[...] = total(cr2, Y).astype(BF16)
        ex_c3.start()
        cr3[z] = cs3[...]

    ex_g2 = []
    for k in range(parts):
        for one in ring[k][2:]:
            one.wait_recv()
        gs2[k] = (gs1[k, x].astype(F32) + grl[k].astype(F32) + grr[k].astype(F32)).astype(BF16)
        ex_g2.append(along_z(
            lambda t, k=k: gs2.at[k, t], lambda f, k=k: gr2.at[k, f], blocks(gr2.at[k], Z), g2_ss.at[k], g2_rs.at[k]))
        ex_g2[k].start()
        gr2[k, z] = gs2[k, z]

    wait_blocks(na1r, X * Z - 1, na1_ss, na1_rs).wait_recv()
    came = jnp.concatenate([na1r[d * Z:(d + 1) * Z].reshape(hop, xh) for d in range(X)], axis=1)
    came = dot(swap_a[...], came).astype(BF16)
    for d in range(X):
        na2s[:, d] = came[:, d * xh:(d + 1) * xh].reshape(Q, Z * half, xh)
    ex_na2.start()
    na2r[q] = na2s[q]
    @pl.when(summing)
    def _():
        ex_c3.recv()
        cfin[...] = total(cr3, Z).astype(BF16)
        ex_c4.start()
        ca4[y] = cfin[...]

    ex_nb1.recv()
    came = dot(swap_b[...], nb1r[...].reshape(hop, X * xh)).astype(BF16)
    for d in range(X):
        nb2s[d * Z:(d + 1) * Z] = came[:, d * xh:(d + 1) * xh].reshape(Z, Q * half, xh)
    xz_leg(lambda d, zz: nb2s.at[d * Z + zz], nb2r, nb2_ss, nb2_rs)
    nb2r[z] = nb2s[z]

    @pl.when(summing)
    def _():
        some = ca4.at[pl.ds(0, nb - 1)]
        copy(some, some, c4_ss, c4_rs, z, q, x).wait_recv()

    @pl.when(jnp.logical_not(summing))
    def _():
        copy(ca4, ca4, c4_ss, c4_rs, z, q, x).wait_recv()

    ex_c5 = along_x(lambda t: ca4, lambda f: ca5.at[f], blocks(ca5, X), c5_ss, c5_rs)
    ex_c5.start()
    ca5[x] = ca4[...]

    for k in range(parts):
        ex_g2[k].recv()
        gs3[:, :, k * span:(k + 1) * span] = total(gr2.at[k], Z).astype(BF16).reshape(YL, 16, span)

    def g3_copy(yl):
        return copy(gs3.at[yl], gr3.at[y], g3_ss.at[yl], g3_rs, z, (x * YL + yl) * C + c, x)

    for yl in range(YL):
        @pl.when(x * YL + yl != y)
        def _():
            g3_copy(yl).start()
    owning = y // YL == x

    ex_na2.recv()
    node_out[:, :xh] = dot(place_a[...], na2r[...].reshape(X * hop, xh)).astype(BF16)

    def g4_copy(xx, cc):
        return copy(gs4.at[cc], gr4.at[c], g4_ss.at[xx * C + cc], g4_rs.at[c], z, y * C + cc, xx)

    def g4_each(act):
        for xx in range(X):
            for cc in range(C):
                @pl.when(owning & jnp.logical_not((x == xx) & (c == cc)))
                def _():
                    act(xx, cc)

    @pl.when(owning)
    def _():
        gr3[y] = gs3[y % YL]
        copy(blocks(gr3, Y), blocks(gr3, Y), g3_ss.at[0], g3_rs, z, q, x).wait_recv()
        gs4[...] = total(gr3, Y).reshape(gs4.shape)
        gr4[c] = gs4[c]

    g4_each(lambda xx, cc: g4_copy(xx, cc).start())

    ex_c5.recv()
    c6 = to_sibling(ca5, ca6, c6_ss, c6_rs)
    c6.start()

    wait_blocks(nb2r, X * Z - 1, nb2_ss, nb2_rs).wait_recv()
    node_out[:, xh:] = dot(place_b[...], nb2r[...].reshape(X * hop, xh)).astype(BF16)

    for cc in range(C):
        @pl.when(jnp.logical_not(owning & (c == cc)))
        def _():
            copy(gs4.at[0], gr4.at[cc], g4_ss.at[0], g4_rs.at[cc], z, y * C + cc, y // YL).wait_recv()
        hidden_out[:, cc * DH:(cc + 1) * DH] = gr4[cc]

    c6.wait_recv()
    for t in range(X):
        ours, theirs = ca5[t].reshape(CP, cw), ca6[t].reshape(CP, cw)
        for cc in range(C):
            class_out[:, cc * HH + t * cw:cc * HH + (t + 1) * cw] = jnp.where(c == cc, ours, theirs)

    for ex in (ex_i1, ex_i2, ex_wx, ex_w3, *ex_fa1, *ex_fb1, *ex_fa2, *ex_fb2, ex_nb1, ex_na2, *ex_g2, ex_c1, ex_c5):
        ex.sent()
    w1_each(lambda t: w1_copy(t).wait_send())
    for one in (w4, ga, g0, c0, c6, *[step for k in range(Z // 2) for step in w2_steps(k)], *[leg for legs in ring for leg in legs]):
        one.wait_send()
    wait_blocks(na1r, X * Z - 1, na1_ss, na1_rs).wait_send()
    wait_blocks(nb2r, X * Z - 1, nb2_ss, nb2_rs).wait_send()

    @pl.when(summing)
    def _():
        some = cs2.at[pl.ds(0, nb - 1)]
        copy(some, some, c2_ss, c2_rs, z, q, x).wait_send()
        ex_c3.sent()
        ex_c4.sent()

    @pl.when(jnp.logical_not(summing))
    def _():
        copy(cs2, cs2, c2_ss, c2_rs, z, q, x).wait_send()

    for yl in range(YL):
        @pl.when(x * YL + yl != y)
        def _():
            g3_copy(yl).wait_send()
    g4_each(lambda xx, cc: g4_copy(xx, cc).wait_send())


def on_device(
    grid, features, hidden_weight, class_weight, request_ids, request_counts,
    outer_tiles, outer_masks, inner_tiles, inner_masks, labels,
):
    Z, Y, C, X = grid
    Q = Y * C
    NO = Z * Q
    cap = request_ids.shape[1]
    half = cap // 2
    rows, D = features.shape
    classes, HID = class_weight.shape
    tile = outer_masks.shape[2]
    hop = NO * half
    DH, HH, YL = D // 2, HID // 2, Y // X
    cb = 32 if classes > 32 else 8
    nb = -(-classes // cb)
    CP, cw = nb * cb, HID // (C * X)
    LW = max(Z * 8, 128)
    dims = (Z, Y, C, X, cap, tile, rows, classes)
    vm, dma = pltpu.VMEM, pltpu.SemaphoreType.DMA
    xh, nk, gk = HID // X // 2, DH // 128, 1
    by_z = [vm((Z, cap * Q, n * 128), BF16) for n in (nk - 1, 1)]
    by_q = [vm((Q, cap * Z, n * 128), BF16) for n in (nk - 1, 1)]
    scratch = [
        vm(features.shape, BF16), vm(outer_masks.shape, jnp.int32), vm(inner_masks.shape, jnp.int32),
        vm(class_weight.shape, BF16), vm(hidden_weight.shape, BF16),
        vm((cap, NO), jnp.int32), vm((2, NO), jnp.int32), vm((1, labels.shape[0]), jnp.int32),
        vm((8, NO), F32), vm((Z, 8, NO), F32), vm((Q, 8, LW), F32), vm((Q, 8, LW), F32),
        vm((X, Q * 8, LW), BF16), vm((rows, X * hop), BF16), vm((rows, X * hop), BF16),
        vm((16, DH), BF16), vm((C, 16, DH), BF16), vm((Z, X, C, 16, D), BF16),
        *by_z, *by_z, *by_q, *by_q, *by_q, *by_q, *by_z, *by_z,
        vm((cap * NO, cap * NO), BF16), vm((cap * NO, cap * NO), BF16), vm((hop, hop), BF16), vm((hop, hop), BF16),
        vm((2, hop, DH), BF16), vm((hop, DH), BF16), vm((hop, HID), F32), vm((HID, hop), BF16), vm((HID, hop), BF16),
        vm((hop, HID), BF16),
        vm((X * Z, Q * half, xh), BF16), vm((X * Z, Q * half, xh), BF16),
        *[vm((Q, X, Z * half, xh), BF16)] * 2, *[vm((Q, Z * half, HH), BF16)] * 2,
        vm((X * Z, Q * half, xh), BF16), vm((X * Z, Q * half, xh), BF16),
        vm((gk, X, Z, YL * 16, DH // gk), BF16), *[vm((gk, Z // 2, YL * 16, DH // gk), BF16)] * 4,
        *[vm((gk, Z, YL * 16, DH // gk), BF16)] * 4,
        vm((YL, 16, DH), BF16), vm((Y, 16, DH), BF16), vm((C, 8, DH), F32), vm((C, 8, DH), F32),
        vm((CP, HH), F32), vm((CP, HH), BF16), vm((CP, HH), BF16),
        vm((X, CP, cw), BF16), vm((X, CP, cw), BF16), vm((nb, cb, cw), BF16), vm((Y, cb, cw), BF16),
        vm((cb, cw), BF16), vm((Z, cb, cw), BF16), vm((cb, cw), BF16), vm((nb, cb, cw), BF16),
        vm((X, nb, cb, cw), BF16), vm((X, nb, cb, cw), BF16),
        dma((8,)),
        *[dma] * 6,
        dma((Y,)), dma((C,)), dma((Z // 2, 2)), dma((Z // 2, 2)), *[dma] * 4,
        *[dma((2,))] * 8, *[dma] * 8,
        *[dma] * 4, dma((gk, 6)), dma((gk, 6)), dma((gk,)), dma((gk,)), dma((YL,)), dma, dma((X * C,)), dma((C,)),
        *[dma] * 14,
    ]
    hbm = pl.BlockSpec(memory_space=pl.ANY)
    vmem = pl.BlockSpec(memory_space=pltpu.VMEM)
    smem = pl.BlockSpec(memory_space=pltpu.SMEM)
    hidden_grad, class_grad, node_grad = pl.pallas_call(
        functools.partial(kernel, dims),
        out_shape=(
            jax.ShapeDtypeStruct(hidden_weight.shape, F32),
            jax.ShapeDtypeStruct((CP, HID), BF16),
            jax.ShapeDtypeStruct((rows, HID // X), BF16),
        ),
        in_specs=[hbm, hbm, hbm, hbm, hbm, smem, hbm, smem, hbm, hbm],
        out_specs=(vmem, vmem, vmem),
        scratch_shapes=scratch,
        compiler_params=pltpu.CompilerParams(
            collective_id=0, has_side_effects=True, vmem_limit_bytes=56 * 1024 * 1024
        ),
        cost_estimate=pl.CostEstimate(flops=2_000_000_000, bytes_accessed=3_000_000, transcendentals=20_000),
    )(
        features, hidden_weight, class_weight, request_ids.T, request_counts.T,
        outer_tiles, outer_masks, inner_tiles, inner_masks, labels.reshape(1, -1),
    )
    return hidden_grad, class_grad[:classes].astype(F32), node_grad


def solution(mesh):
    grid = GRIDS[(mesh.shape["owner"], mesh.shape["rep"])]
    placed = (
        P("owner", None),
        P("owner", None),
        P(),
        P(("owner", "rep"), None),
        P(("owner", "rep"), None),
        P(("owner", "rep"), None),
        P(("owner", "rep"), None, None, None),
        P(("owner", "rep"), None),
        P(("owner", "rep"), None, None, None),
        P(("owner", "rep")),
    )
    return jax.shard_map(
        functools.partial(on_device, grid),
        mesh=mesh,
        in_specs=placed,
        out_specs=(P("owner", None), P(), P("owner", "rep")),
        check_vma=False,
    )
```
